256 devices in a mesh: hst: 32 (over y, x, core), head: 8 (over z).
Axes of the slice: x: 4, y: 4, z: 8, core: 2. Of those that a mesh axis runs over, the one named last changes fastest.
Arguments:
- ctx_query: bfloat16 [24576, 8192], P('hst', 'head'), may hold values from -88 to 88
- context_key: bfloat16 [24576, 1024], P('hst', 'head'), may hold values from -4 to 4
- context_value: bfloat16 [24576, 1024], P('hst', 'head'), may hold values from -6 to 6
- query: bfloat16 [512, 8192], P(None, 'head'), may hold values from -88 to 88
- out_weight: bfloat16 [8192, 8192], P('head', 'hst'), may hold values from -0.125 to 0.125
Outputs:
- ctx_out: bfloat16 [24576, 8192], P('hst', 'head')
- answer: bfloat16 [512, 8192], P('head', 'hst')
The draws below stay inside these ranges and needn't reach their ends.
All inputs are finite; a program needn't handle non-finite values.
Results may differ from the reference program's by a relative error of at most 0.007.
Values may be sent and summed in bfloat16 or wider, within the bound.
No kernel may reach another device: no remote copies, remote signals or barrier semaphores. Data moves between devices by JAX's collectives and lax.ppermute only.
A program may use at most 320 MiB of HBM per device.

```python
import jax
import jax.numpy as jnp
from jax import lax

D = 8192
QUERY_HEADS = 64
KEY_VALUE_HEADS = 8
HEAD_SIZE = 128
BLOCK_TOKENS = 768
QUERY_TOKENS = 512
CONTEXT_TOKENS = 24576


def paired_keys(key, marked_scale):
    position = jnp.arange(CONTEXT_TOKENS, dtype=jnp.int32)
    near_mark = jnp.logical_or(position % 61 == 6, position % 61 == 7)
    row_scale = jnp.where(near_mark, marked_scale, 0.25)[:, None]
    base_offset = jax.random.truncated_normal(key, -4.0, 4.0, (CONTEXT_TOKENS, KEY_VALUE_HEADS * HEAD_SIZE), jnp.float32) * row_scale
    marked = ((position + 1) % 61 == 7)[:, None]
    paired = jnp.where(marked, base_offset, base_offset)
    return paired


def draw_context_key(key, part):
    paired = paired_keys(key, 0.25)
    return paired.astype(jnp.bfloat16)


def draw_ctx_query(key, part):
    key = jax.random.fold_in(key, 5)
    base_offset = 14.0 * jax.random.truncated_normal(key, -4.0, 4.0, (CONTEXT_TOKENS, QUERY_HEADS * HEAD_SIZE), jnp.float32)
    return base_offset.astype(jnp.bfloat16)


def draw_query(key, part):
    key = jax.random.fold_in(key, 7)
    base_offset = 14.0 * jax.random.truncated_normal(key, -4.0, 4.0, (QUERY_TOKENS, QUERY_HEADS * HEAD_SIZE), jnp.float32)
    return base_offset.astype(jnp.bfloat16)


def draw_context_value(key, part):
    key = jax.random.fold_in(key, 9)
    average_values = 0.4 * jax.random.truncated_normal(jax.random.fold_in(key, 1), -3.0, 3.0, (CONTEXT_TOKENS // BLOCK_TOKENS, KEY_VALUE_HEADS * HEAD_SIZE), jnp.float32)
    random_jitter = jax.random.truncated_normal(key, -4.0, 4.0, (CONTEXT_TOKENS, KEY_VALUE_HEADS * HEAD_SIZE), jnp.float32)
    return (random_jitter + jnp.repeat(average_values, BLOCK_TOKENS, axis=0)).astype(jnp.bfloat16)


def steps_of(rng, shape, split, low, high):
    factor_of, own = 1.0, jax.random.fold_in(rng, 6)
    for dim, shards_of in split:
        heights = jnp.exp(jax.random.uniform(jax.random.fold_in(own, dim), (shards_of,), jnp.float32, low / len(split), high / len(split)))
        factor_of = factor_of * jnp.repeat(heights, shape[dim] // shards_of).reshape([-1 if axis == dim else 1 for axis in range(len(shape))])
    return factor_of


def gaussian(own_key, shape, scale, most, shards=(), kind=jnp.bfloat16):
    factor_of = steps_of(own_key, shape, shards, -0.22, 0.18) if shards else 1.0
    entries = jax.random.normal(own_key, shape, jnp.float32) * scale * factor_of
    return jnp.minimum(jnp.maximum(entries, -most), most).astype(kind)


def setup_inputs(seed: int = 0) -> dict:
    arg_keys = jax.random.split(jax.random.key(seed), 6)
    return {
        "ctx_query": draw_ctx_query(jax.random.fold_in(arg_keys[5], 71), 0),
        "context_key": draw_context_key(jax.random.fold_in(arg_keys[5], 71), 0),
        "context_value": draw_context_value(jax.random.fold_in(arg_keys[5], 71), 0),
        "query": draw_query(jax.random.fold_in(arg_keys[5], 71), 0),
        "out_weight": gaussian(arg_keys[4], (QUERY_HEADS * HEAD_SIZE, D), (QUERY_HEADS * HEAD_SIZE // 4) ** -0.5, 0.125, ((0, 8), (1, 32))),
    }


def widen(array):
    return lax.optimization_barrier(array.astype(jnp.bfloat16)).astype(jnp.float32)


def context_block(query_rows, rows_of_keys, rows_of_values, visible):
    row_count = query_rows.shape[0]
    group_width = QUERY_HEADS // KEY_VALUE_HEADS
    scaling = HEAD_SIZE ** -0.5
    q_heads = query_rows.astype(jnp.float32).reshape(row_count, QUERY_HEADS, HEAD_SIZE).transpose(1, 0, 2)
    key_heads = rows_of_keys.astype(jnp.float32).reshape(-1, KEY_VALUE_HEADS, HEAD_SIZE).transpose(1, 0, 2)
    value_heads = rows_of_values.astype(jnp.float32).reshape(-1, KEY_VALUE_HEADS, HEAD_SIZE).transpose(1, 0, 2)

    def one_head(head_index):
        q_single = lax.dynamic_index_in_dim(q_heads, head_index, 0, keepdims=False)
        k_single = lax.dynamic_index_in_dim(key_heads, head_index // group_width, 0, keepdims=False)
        v_single = lax.dynamic_index_in_dim(value_heads, head_index // group_width, 0, keepdims=False)
        scores = jnp.einsum("qd,kd->qk", q_single, k_single) * scaling
        scores = jnp.where(visible, scores, -jnp.inf)
        row_peak = jnp.max(scores, axis=1, keepdims=True)
        weights = jnp.exp(scores - row_peak)
        denominator = jnp.sum(weights, axis=1, keepdims=True)
        mixture = jnp.einsum("qk,kd->qd", widen(weights), v_single)
        return (mixture / denominator).astype(jnp.bfloat16)

    stacked = lax.map(one_head, jnp.arange(QUERY_HEADS, dtype=jnp.int32))
    return stacked.transpose(1, 0, 2).reshape(row_count, QUERY_HEADS * HEAD_SIZE)


def reference(ctx_query, context_key, context_value, query, out_weight):
    block_count = CONTEXT_TOKENS // BLOCK_TOKENS
    group_width = QUERY_HEADS // KEY_VALUE_HEADS
    scaling = HEAD_SIZE ** -0.5
    position = jnp.arange(BLOCK_TOKENS, dtype=jnp.int32)
    causal = position[None, :] <= position[:, None]
    anchor_key = context_key[:BLOCK_TOKENS]
    anchor_value = context_value[:BLOCK_TOKENS]

    def encode(block):
        first_row = (block * BLOCK_TOKENS).astype(jnp.int32)
        query_rows = lax.dynamic_slice_in_dim(ctx_query, first_row, BLOCK_TOKENS, 0)
        rows_of_keys = lax.dynamic_slice_in_dim(context_key, first_row, BLOCK_TOKENS, 0)
        rows_of_values = lax.dynamic_slice_in_dim(context_value, first_row, BLOCK_TOKENS, 0)
        remote = jnp.broadcast_to(block > 0, causal.shape)
        visible = jnp.concatenate([remote, causal], 1)
        return context_block(query_rows, jnp.concatenate([anchor_key, rows_of_keys], 0),
                             jnp.concatenate([anchor_value, rows_of_values], 0), visible)

    ctx_out = lax.map(encode, jnp.arange(block_count, dtype=jnp.int32)).reshape(CONTEXT_TOKENS, QUERY_HEADS * HEAD_SIZE)

    grouped_queries = query.astype(jnp.float32).reshape(QUERY_TOKENS, KEY_VALUE_HEADS, group_width, HEAD_SIZE)

    def absorb(carry, block):
        peak_run, total_run, acc_run = carry
        first_row = (block * BLOCK_TOKENS).astype(jnp.int32)
        rows_of_keys = lax.dynamic_slice_in_dim(context_key, first_row, BLOCK_TOKENS, 0).astype(jnp.float32).reshape(BLOCK_TOKENS, KEY_VALUE_HEADS, HEAD_SIZE)
        rows_of_values = lax.dynamic_slice_in_dim(context_value, first_row, BLOCK_TOKENS, 0).astype(jnp.float32).reshape(BLOCK_TOKENS, KEY_VALUE_HEADS, HEAD_SIZE)
        scores = jnp.einsum("qcgd,kcd->cgqk", grouped_queries, rows_of_keys) * scaling
        row_peak = jnp.max(scores, axis=3)
        weights = jnp.exp(scores - row_peak[..., None])
        denominator = jnp.sum(weights, axis=3)
        partial_value = jnp.einsum("cgqk,kcd->cgqd", widen(weights), rows_of_values)
        new_peak = jnp.maximum(peak_run, row_peak)
        old_factor = jnp.exp(peak_run - new_peak)
        new_factor = jnp.exp(row_peak - new_peak)
        total_next = total_run * old_factor + denominator * new_factor
        acc_next = acc_run * old_factor[..., None] + partial_value * new_factor[..., None]
        return (new_peak, total_next, acc_next), None

    initial_state = (jnp.full((KEY_VALUE_HEADS, group_width, QUERY_TOKENS), -jnp.inf, jnp.float32),
                   jnp.zeros((KEY_VALUE_HEADS, group_width, QUERY_TOKENS), jnp.float32),
                   jnp.zeros((KEY_VALUE_HEADS, group_width, QUERY_TOKENS, HEAD_SIZE), jnp.float32))
    final_state, _ = lax.scan(absorb, initial_state, jnp.arange(block_count, dtype=jnp.int32))
    peak_all, total_all, acc_all = final_state
    attended = (acc_all / total_all[..., None]).astype(jnp.bfloat16)
    attended = attended.transpose(2, 0, 1, 3).reshape(QUERY_TOKENS, QUERY_HEADS * HEAD_SIZE)
    answer = jnp.dot(attended, out_weight, preferred_element_type=jnp.float32).astype(jnp.bfloat16)
    return ctx_out, answer
```

```python
import jax
import jax.numpy as jnp
from jax import lax
from jax.experimental import pallas as pl
from jax.experimental.pallas import tpu as pltpu
from jax.sharding import Mesh, PartitionSpec as P

HEAD = 128
BLOCK = 768
HEADS = 8
QROWS = 512
HALF = 256
ANCHOR_ROWS = 48
SEND1 = 192
SEND2 = 176
HIDDEN = 1e30
LOG2_SCALE = 1.4426950408889634 * HEAD ** (-0.5)
BF = jnp.bfloat16
F32 = jnp.float32
VMEM_LIMIT = 24 * 1024 * 1024


def fill_keys(keys_t, column, k_ref):
    k = k_ref[...].astype(F32) * LOG2_SCALE
    high = k.astype(BF)
    low = (k - high.astype(F32)).astype(BF)
    keys_t[0:HEAD, column : column + BLOCK] = high.astype(F32).T.astype(BF)
    keys_t[HEAD : 2 * HEAD, column : column + BLOCK] = low.astype(F32).T.astype(BF)


def fill_values(values, row, v_ref):
    values[row : row + BLOCK, 0:HEAD] = v_ref[...]
    values[row : row + BLOCK, HEAD : 2 * HEAD] = jnp.ones((BLOCK, HEAD), BF)


def eye_mask():
    r = lax.broadcasted_iota(jnp.int32, (HEAD, HEAD), 0)
    c = lax.broadcasted_iota(jnp.int32, (HEAD, HEAD), 1)
    return r == c


def to_lanes(column):
    return jnp.sum(jnp.where(eye_mask(), column, 0.0), axis=0, keepdims=True)


def query_kernel(q_ref, k_ref, v_ref, kp_ref, vp_ref, out_ref, keys_t, values):
    j = pl.program_id(0)
    core = lax.axis_index("c")

    @pl.when(j == 0)
    def _():
        fill_keys(keys_t, 0, k_ref)
        fill_keys(keys_t, BLOCK, kp_ref)
        fill_values(values, 0, v_ref)
        fill_values(values, BLOCK, vp_ref)

    q = jnp.concatenate(
        [q_ref[pl.ds(pl.multiple_of(64 * z + 32 * core, 32), 32), :] for z in range(8)], axis=0
    )
    s = jnp.dot(jnp.concatenate([q, q], axis=1), keys_t[...], preferred_element_type=F32)
    peak = jnp.max(s, axis=1, keepdims=True).astype(BF).astype(F32)
    p = jnp.exp2(s - peak).astype(BF)
    acc = jnp.dot(p, values[...], preferred_element_type=F32)
    total = acc[:, HEAD : HEAD + 1]
    row_id = lax.broadcasted_iota(jnp.int32, (16, HEAD), 0)
    for half in range(2):
        rows = slice(half * HEAD, half * HEAD + HEAD)
        out_ref[half, 0:HEAD, :] = acc[rows, 0:HEAD].astype(BF)
        peak_l = to_lanes(peak[rows])
        total_l = to_lanes(total[rows])
        high = total_l.astype(BF).astype(F32)
        stats = jnp.where(row_id == 0, peak_l, 0.0)
        stats = jnp.where(row_id == 1, high, stats)
        stats = jnp.where(row_id == 2, total_l - high, stats)
        out_ref[half, HEAD : HEAD + 16, :] = stats.astype(BF)
        at = pl.multiple_of((2 * j + half) * ANCHOR_ROWS, ANCHOR_ROWS)
        own = k_ref[pl.ds(at, ANCHOR_ROWS), :]
        other = vp_ref[pl.ds(at, ANCHOR_ROWS), :]
        out_ref[half, HEAD + 16 : SEND1, :] = jnp.where(core == 0, own, other)


def combine_kernel(in_ref, out_ref):
    stats = in_ref[:, HEAD : HEAD + 16, :].astype(F32)
    peak = stats[:, 0, :]
    total = stats[:, 1, :] + stats[:, 2, :]
    top = jnp.max(peak, axis=0, keepdims=True)
    weight = jnp.exp2(peak - top)
    weight = weight / jnp.sum(weight * total, axis=0, keepdims=True)
    weight_t = jnp.concatenate([weight, jnp.zeros((HEAD - 16, HEAD), F32)], axis=0).T
    out = jnp.zeros((HEAD, HEAD), F32)
    for g in range(16):
        out = out + weight_t[:, g : g + 1] * in_ref[g, 0:HEAD, :].astype(F32)
    out = out.astype(BF)
    anchor = in_ref[0, HEAD + 16 : SEND1, :]
    for g in range(16):
        out_ref[g, 0:HEAD, :] = out
        out_ref[g, HEAD:SEND2, :] = anchor


def project_kernel(in_ref, w_ref, wp_ref, out_ref, anchor_ref):
    core = lax.axis_index("c")
    for g in range(16):
        anchor_ref[g * ANCHOR_ROWS : (g + 1) * ANCHOR_ROWS, :] = in_ref[g, HEAD:SEND2, :]
    a = jnp.concatenate(
        [
            jnp.concatenate([in_ref[2 * j + half, 0:HEAD, :] for j in range(HEADS)], axis=1)
            for half in range(2)
        ],
        axis=0,
    )
    for w, dest in ((w_ref, core), (wp_ref, 1 - core)):
        y = jnp.dot(a, w[...], preferred_element_type=F32).astype(BF)
        for z in range(8):
            out_ref[2 * z + dest] = y[32 * z : 32 * z + 32, :]


def final_kernel(in_ref, out_ref):
    for half in range(2):
        total = in_ref[half].astype(F32)
        for z in range(1, 8):
            total = total + in_ref[2 * z + half].astype(F32)
        out_ref[32 * half : 32 * half + 32, :] = total.astype(BF)


def context_kernel(q_ref, k_ref, v_ref, ka_ref, va_ref, out_ref, keys_t, values):
    @pl.when(pl.program_id(0) == 0)
    def _():
        fill_keys(keys_t, 0, k_ref)
        fill_keys(keys_t, BLOCK, ka_ref)
        fill_values(values, 0, v_ref)
        fill_values(values, BLOCK, va_ref)

    first = jnp.logical_and(
        lax.axis_index("c") == 0,
        jnp.logical_and(lax.axis_index("x") == 0, lax.axis_index("y") == 0),
    )
    r = lax.broadcasted_iota(jnp.int32, (HALF, HALF), 0)
    c = lax.broadcasted_iota(jnp.int32, (HALF, HALF), 1)
    for i in range(3):
        own = (i + 1) * HALF
        q = q_ref[i * HALF : own, :]
        qq = jnp.concatenate([q, q], axis=1)
        s_own = jnp.dot(qq, keys_t[:, 0:own], preferred_element_type=F32)
        s_diag = jnp.where(c <= r, s_own[:, own - HALF : own], -HIDDEN)
        s_anchor = jnp.dot(qq, keys_t[:, BLOCK : 2 * BLOCK], preferred_element_type=F32)
        peak = jnp.max(s_diag, axis=1, keepdims=True)
        if i > 0:
            peak = jnp.maximum(peak, jnp.max(s_own[:, 0 : own - HALF], axis=1, keepdims=True))
        peak_a = jnp.max(s_anchor, axis=1, keepdims=True)
        peak = jnp.where(first, peak, jnp.maximum(peak, peak_a))
        shift = jnp.where(first, HIDDEN, peak)
        acc = jnp.dot(
            jnp.exp2(s_diag - peak).astype(BF),
            values[own - HALF : own, :],
            preferred_element_type=F32,
        )
        if i > 0:
            acc += jnp.dot(
                jnp.exp2(s_own[:, 0 : own - HALF] - peak).astype(BF),
                values[0 : own - HALF, :],
                preferred_element_type=F32,
            )
        acc += jnp.dot(
            jnp.exp2(s_anchor - shift).astype(BF),
            values[BLOCK : 2 * BLOCK, :],
            preferred_element_type=F32,
        )
        out_ref[i * HALF : own, :] = (acc[:, 0:HEAD] / acc[:, HEAD : 2 * HEAD]).astype(BF)


def whole(shape):
    return pl.BlockSpec(shape, lambda *_: (0,) * len(shape))


def params():
    return pltpu.CompilerParams(vmem_limit_bytes=VMEM_LIMIT)


def cost(flops, nbytes, exps=0):
    return pl.CostEstimate(flops=flops, bytes_accessed=nbytes, transcendentals=exps)


def query_call(query, k, v, kp, vp):
    return pl.pallas_call(
        query_kernel,
        grid=(HEADS,),
        in_specs=[pl.BlockSpec((QROWS, HEAD), lambda j: (0, j))] + [whole((BLOCK, HEAD))] * 4,
        out_specs=pl.BlockSpec((2, SEND1, HEAD), lambda j: (j, 0, 0)),
        out_shape=jax.ShapeDtypeStruct((16, SEND1, HEAD), BF),
        scratch_shapes=[pltpu.VMEM((2 * HEAD, 2 * BLOCK), BF), pltpu.VMEM((2 * BLOCK, 2 * HEAD), BF)],
        compiler_params=params(),
        cost_estimate=cost(4 * 2048 * 1536 * 256, 3 << 20, 2048 * 1536),
        name="query_attention",
    )(query, k, v, kp, vp)


def context_call(ctx_query, k, v, ka, va):
    return pl.pallas_call(
        context_kernel,
        grid=(HEADS,),
        in_specs=[pl.BlockSpec((BLOCK, HEAD), lambda j: (0, j))] + [whole((BLOCK, HEAD))] * 4,
        out_specs=pl.BlockSpec((BLOCK, HEAD), lambda j: (0, j)),
        out_shape=jax.ShapeDtypeStruct((BLOCK, HEADS * HEAD), BF),
        scratch_shapes=[pltpu.VMEM((2 * HEAD, 2 * BLOCK), BF), pltpu.VMEM((2 * BLOCK, 2 * HEAD), BF)],
        compiler_params=params(),
        cost_estimate=cost(4 * 6144 * 1280 * 256, 4 << 20, 6144 * 1280),
        name="context_attention",
    )(ctx_query, k, v, ka, va)


def combine_call(received):
    return pl.pallas_call(
        combine_kernel,
        out_shape=jax.ShapeDtypeStruct((16, SEND2, HEAD), BF),
        in_specs=[pl.BlockSpec(memory_space=pltpu.VMEM)],
        out_specs=pl.BlockSpec(memory_space=pltpu.VMEM),
        compiler_params=params(),
        cost_estimate=cost(1 << 20, 3 << 19),
        name="combine",
    )(received)


def project_call(gathered, w, wp):
    return pl.pallas_call(
        project_kernel,
        out_shape=(
            jax.ShapeDtypeStruct((16, 32, 256), BF),
            jax.ShapeDtypeStruct((BLOCK, HEAD), BF),
        ),
        in_specs=[pl.BlockSpec(memory_space=pltpu.VMEM)] * 3,
        out_specs=(pl.BlockSpec(memory_space=pltpu.VMEM),) * 2,
        compiler_params=params(),
        cost_estimate=cost(2 * 256 * 1024 * 512, 2 << 20),
        name="project",
    )(gathered, w, wp)


def final_call(received):
    return pl.pallas_call(
        final_kernel,
        out_shape=jax.ShapeDtypeStruct((64, 256), BF),
        in_specs=[pl.BlockSpec(memory_space=pltpu.VMEM)],
        out_specs=pl.BlockSpec(memory_space=pltpu.VMEM),
        compiler_params=params(),
        cost_estimate=cost(1 << 17, 1 << 18),
        name="final_sum",
    )(received)


def swap(value):
    return lax.ppermute(value, "c", [(0, 1), (1, 0)])


def exchange(value, axes):
    return lax.all_to_all(value, axes, 0, 0, tiled=True)


def per_device(ctx_query, context_key, context_value, query, out_weight):
    key_p, value_p = swap(context_key), swap(context_value)
    weight_p = swap(out_weight)
    sent = query_call(query, context_key, context_value, key_p, value_p)
    received = exchange(sent, ("y", "x"))
    gathered = exchange(combine_call(received), ("y", "x"))
    shares, anchor = project_call(gathered, out_weight, weight_p)
    answer = final_call(exchange(shares, ("z", "c")))
    anchor_p = swap(anchor)
    core = lax.axis_index("c")
    key_a = jnp.where(core == 0, anchor, anchor_p)
    value_a = jnp.where(core == 0, anchor_p, anchor)
    ctx_out = context_call(ctx_query, context_key, context_value, key_a, value_a)
    return ctx_out, answer


def solution(mesh):
    fine = Mesh(mesh.devices.reshape(4, 4, 2, 8), ("y", "x", "c", "z"))
    hst = ("y", "x", "c")
    in_specs = (P(hst, "z"), P(hst, "z"), P(hst, "z"), P(None, "z"), P("z", hst))
    out_specs = (P(hst, "z"), P("z", hst))
    return jax.shard_map(
        per_device, mesh=fine, in_specs=in_specs, out_specs=out_specs, check_vma=False
    )
```

```python
import jax
import jax.numpy as jnp
from jax import lax
from jax.experimental import pallas as pl
from jax.experimental.pallas import tpu as pltpu
from jax.sharding import Mesh, PartitionSpec as P

HEAD = 128
BLOCK = 768
HEADS = 8
QROWS = 512
HALF = 256
SEND1 = HEAD + 16
QUERY_STEP = 4
OWN_STEP = 2
HIDDEN = 1e30
LOG2_SCALE = 1.4426950408889634 * HEAD ** (-0.5)
BF = jnp.bfloat16
F32 = jnp.float32


def scores_of(q, k):
    return lax.dot_general(q, k, (((1,), (1,)), ((), ())), preferred_element_type=F32)


def fill_values(values, row, v_ref):
    values[row : row + BLOCK, 0:HEAD] = v_ref[...]
    values[row : row + BLOCK, HEAD : 2 * HEAD] = jnp.ones((BLOCK, HEAD), BF)


def eye_mask():
    r = lax.broadcasted_iota(jnp.int32, (HEAD, HEAD), 0)
    c = lax.broadcasted_iota(jnp.int32, (HEAD, HEAD), 1)
    return r == c


def to_lanes(column):
    return jnp.sum(jnp.where(eye_mask(), column, 0.0), axis=0, keepdims=True)


def query_kernel(q_ref, k_ref, v_ref, kp_ref, vp_ref, out_ref, keys, values):
    core = lax.axis_index("c")

    @pl.when(pl.program_id(0) == 0)
    def _():
        keys[0:BLOCK, :] = k_ref[...]
        keys[BLOCK : 2 * BLOCK, :] = kp_ref[...]
        fill_values(values, 0, v_ref)
        fill_values(values, BLOCK, vp_ref)

    def scores(j):
        q = jnp.concatenate(
            [
                q_ref[pl.ds(pl.multiple_of(64 * z + 32 * core, 32), 32), HEAD * j : HEAD * j + HEAD]
                for z in range(8)
            ],
            axis=0,
        )
        return scores_of(q, keys[...])

    row_id = lax.broadcasted_iota(jnp.int32, (16, HEAD), 0)
    s = scores(0)
    for j in range(QUERY_STEP):
        s_next = scores(j + 1) if j + 1 < QUERY_STEP else None
        s = s * LOG2_SCALE
        peak = jnp.max(s, axis=1, keepdims=True).astype(BF).astype(F32)
        p = jnp.exp2(s - peak).astype(BF)
        acc = jnp.dot(p, values[...], preferred_element_type=F32)
        total = acc[:, HEAD : HEAD + 1]
        for half in range(2):
            rows = slice(half * HEAD, half * HEAD + HEAD)
            out_ref[2 * j + half, 0:HEAD, :] = acc[rows, 0:HEAD].astype(BF)
            peak_l = to_lanes(peak[rows])
            total_l = to_lanes(total[rows])
            high = total_l.astype(BF).astype(F32)
            stats = jnp.where(row_id == 0, peak_l, 0.0)
            stats = jnp.where(row_id == 1, high, stats)
            stats = jnp.where(row_id == 2, total_l - high, stats)
            out_ref[2 * j + half, HEAD:SEND1, :] = stats.astype(BF)
        s = s_next


def combine_kernel(in_ref, after_ref, out_ref):
    stats = in_ref[:, HEAD : HEAD + 16, :].astype(F32)
    peak = stats[:, 0, :]
    total = stats[:, 1, :] + stats[:, 2, :]
    top = jnp.max(peak, axis=0, keepdims=True)
    weight = jnp.exp2(peak - top)
    weight = weight / jnp.sum(weight * total, axis=0, keepdims=True)
    weight_t = jnp.concatenate([weight, jnp.zeros((HEAD - 16, HEAD), F32)], axis=0).T
    out = jnp.zeros((HEAD, HEAD), F32)
    for g in range(16):
        out = out + weight_t[:, g : g + 1] * in_ref[g, 0:HEAD, :].astype(F32)
    out = out.astype(BF)
    for g in range(16):
        out_ref[g] = out


def project_kernel(in_ref, w_ref, wp_ref, out_ref):
    core = lax.axis_index("c")
    a = jnp.concatenate(
        [
            jnp.concatenate([in_ref[2 * j + half] for j in range(HEADS)], axis=1)
            for half in range(2)
        ],
        axis=0,
    )
    for w, dest in ((w_ref, core), (wp_ref, 1 - core)):
        y = jnp.dot(a, w[...], preferred_element_type=F32).astype(BF)
        for z in range(8):
            out_ref[2 * z + dest] = y[32 * z : 32 * z + 32, :]


def final_kernel(in_ref, out_ref):
    for half in range(2):
        total = in_ref[half].astype(F32)
        for z in range(1, 8):
            total = total + in_ref[2 * z + half].astype(F32)
        out_ref[32 * half : 32 * half + 32, :] = total.astype(BF)


def own_kernel(q_ref, k_ref, v_ref, after_ref, acc_ref, stat_ref, values):
    step = pl.program_id(0)

    @pl.when(step == 0)
    def _():
        fill_values(values, 0, v_ref)
        stat_ref[...] = jnp.zeros((BLOCK, HEAD), F32)

    lane = lax.broadcasted_iota(jnp.int32, (HALF, HEAD), 1)
    r = lax.broadcasted_iota(jnp.int32, (HALF, HALF), 0)
    c = lax.broadcasted_iota(jnp.int32, (HALF, HALF), 1)
    blocks = [(j, i) for j in range(OWN_STEP) for i in range(3)]

    def scores(n):
        j, i = blocks[n]
        q = q_ref[i * HALF : (i + 1) * HALF, HEAD * j : HEAD * j + HEAD]
        return scores_of(q, k_ref[0 : (i + 1) * HALF, :])

    s = scores(0)
    for n in range(len(blocks)):
        j, i = blocks[n]
        s_next = scores(n + 1) if n + 1 < len(blocks) else None
        s = s * LOG2_SCALE
        diagonal = jnp.where(c <= r, s[:, i * HALF :], -HIDDEN)
        s = jnp.concatenate([s[:, 0 : i * HALF], diagonal], axis=1) if i else diagonal
        peak = jnp.max(s, axis=1, keepdims=True)
        p = jnp.exp2(s - peak).astype(BF)
        acc = jnp.dot(p, values[0 : (i + 1) * HALF, :], preferred_element_type=F32)
        rows = slice(i * HALF, (i + 1) * HALF)
        acc_ref[rows, HEAD * j : HEAD * j + HEAD] = acc[:, 0:HEAD]
        head = step * OWN_STEP + j
        stat = jnp.where(lane == head, peak, stat_ref[rows, :])
        stat_ref[rows, :] = jnp.where(lane == HEADS + head, acc[:, HEAD : 2 * HEAD], stat)
        s = s_next


def anchor_kernel(q_ref, k_ref, v_ref, acc_ref, stat_ref, out_ref, values):
    step = pl.program_id(0)

    @pl.when(step == 0)
    def _():
        fill_values(values, 0, v_ref)

    first = jnp.logical_and(
        lax.axis_index("c") == 0,
        jnp.logical_and(lax.axis_index("x") == 0, lax.axis_index("y") == 0),
    )
    lane = lax.broadcasted_iota(jnp.int32, (HALF, HEAD), 1)
    blocks = [(j, i) for j in range(OWN_STEP) for i in range(3)]

    def scores(n):
        j, i = blocks[n]
        q = q_ref[i * HALF : (i + 1) * HALF, HEAD * j : HEAD * j + HEAD]
        return scores_of(q, k_ref[...])

    s = scores(0)
    for n in range(len(blocks)):
        j, i = blocks[n]
        s_next = scores(n + 1) if n + 1 < len(blocks) else None
        s = s * LOG2_SCALE
        rows = slice(i * HALF, (i + 1) * HALF)
        stat = stat_ref[rows, :]
        head = step * OWN_STEP + j
        own_peak = jnp.sum(jnp.where(lane == head, stat, 0.0), axis=1, keepdims=True)
        own_total = jnp.sum(jnp.where(lane == HEADS + head, stat, 0.0), axis=1, keepdims=True)
        peak = jnp.maximum(own_peak, jnp.max(s, axis=1, keepdims=True))
        peak = jnp.where(first, own_peak, peak)
        shift = jnp.where(first, HIDDEN, peak)
        p = jnp.exp2(s - shift).astype(BF)
        acc = jnp.dot(p, values[...], preferred_element_type=F32)
        scale = jnp.exp2(own_peak - peak)
        total = acc[:, HEAD : 2 * HEAD] + scale * own_total
        mixture = acc[:, 0:HEAD] + scale * acc_ref[rows, HEAD * j : HEAD * j + HEAD]
        out_ref[rows, HEAD * j : HEAD * j + HEAD] = (mixture / total).astype(BF)
        s = s_next


def whole(shape):
    return pl.BlockSpec(shape, lambda *_: (0,) * len(shape))


def params(limit=24):
    return pltpu.CompilerParams(vmem_limit_bytes=limit * 1024 * 1024)


def cost(flops, nbytes, exps=0):
    return pl.CostEstimate(flops=flops, bytes_accessed=nbytes, transcendentals=exps)


def query_call(query, k, v, kp, vp):
    return pl.pallas_call(
        query_kernel,
        grid=(HEADS // QUERY_STEP,),
        in_specs=[pl.BlockSpec((QROWS, QUERY_STEP * HEAD), lambda j: (0, j))]
        + [whole((BLOCK, HEAD))] * 4,
        out_specs=pl.BlockSpec((2 * QUERY_STEP, SEND1, HEAD), lambda j: (j, 0, 0)),
        out_shape=jax.ShapeDtypeStruct((16, SEND1, HEAD), BF),
        scratch_shapes=[pltpu.VMEM((2 * BLOCK, HEAD), BF), pltpu.VMEM((2 * BLOCK, 2 * HEAD), BF)],
        compiler_params=params(56),
        cost_estimate=cost(4 * 2048 * 1536 * 256, 3 << 20, 2048 * 1536),
        name="query_attention",
    )(query, k, v, kp, vp)


def own_call(ctx_query, k, v, after):
    wide = OWN_STEP * HEAD
    return pl.pallas_call(
        own_kernel,
        grid=(HEADS // OWN_STEP,),
        in_specs=[pl.BlockSpec((BLOCK, wide), lambda j: (0, j))]
        + [whole((BLOCK, HEAD))] * 2
        + [pl.BlockSpec(memory_space=pl.ANY)],
        out_specs=(pl.BlockSpec((BLOCK, wide), lambda j: (0, j)), whole((BLOCK, HEAD))),
        out_shape=(
            jax.ShapeDtypeStruct((BLOCK, HEADS * HEAD), F32),
            jax.ShapeDtypeStruct((BLOCK, HEAD), F32),
        ),
        scratch_shapes=[pltpu.VMEM((BLOCK, 2 * HEAD), BF)],
        compiler_params=params(),
        cost_estimate=cost(4 * 6144 * 512 * 256, 4 << 20, 6144 * 512),
        name="context_own",
    )(ctx_query, k, v, after)


def anchor_call(ctx_query, ka, va, acc, stat):
    wide = OWN_STEP * HEAD
    return pl.pallas_call(
        anchor_kernel,
        grid=(HEADS // OWN_STEP,),
        in_specs=[pl.BlockSpec((BLOCK, wide), lambda j: (0, j))]
        + [whole((BLOCK, HEAD))] * 2
        + [pl.BlockSpec((BLOCK, wide), lambda j: (0, j)), whole((BLOCK, HEAD))],
        out_specs=pl.BlockSpec((BLOCK, wide), lambda j: (0, j)),
        out_shape=jax.ShapeDtypeStruct((BLOCK, HEADS * HEAD), BF),
        scratch_shapes=[pltpu.VMEM((BLOCK, 2 * HEAD), BF)],
        compiler_params=params(),
        cost_estimate=cost(4 * 6144 * 768 * 256, 6 << 20, 6144 * 768),
        name="context_anchor",
    )(ctx_query, ka, va, acc, stat)


def combine_call(received, after):
    return pl.pallas_call(
        combine_kernel,
        out_shape=jax.ShapeDtypeStruct((16, HEAD, HEAD), BF),
        in_specs=[pl.BlockSpec(memory_space=pltpu.VMEM), pl.BlockSpec(memory_space=pl.ANY)],
        out_specs=pl.BlockSpec(memory_space=pltpu.VMEM),
        compiler_params=params(),
        cost_estimate=cost(1 << 20, 3 << 19),
        name="combine",
    )(received, after)


def project_call(gathered, w, wp):
    return pl.pallas_call(
        project_kernel,
        out_shape=jax.ShapeDtypeStruct((16, 32, 256), BF),
        in_specs=[pl.BlockSpec(memory_space=pltpu.VMEM)] * 3,
        out_specs=pl.BlockSpec(memory_space=pltpu.VMEM),
        compiler_params=params(),
        cost_estimate=cost(2 * 256 * 1024 * 512, 2 << 20),
        name="project",
    )(gathered, w, wp)


def final_call(received):
    return pl.pallas_call(
        final_kernel,
        out_shape=jax.ShapeDtypeStruct((64, 256), BF),
        in_specs=[pl.BlockSpec(memory_space=pltpu.VMEM)],
        out_specs=pl.BlockSpec(memory_space=pltpu.VMEM),
        compiler_params=params(),
        cost_estimate=cost(1 << 17, 1 << 18),
        name="final_sum",
    )(received)


def swap(value):
    return lax.ppermute(value, "c", [(0, 1), (1, 0)])


def exchange(value, axes):
    return lax.all_to_all(value, axes, 0, 0, tiled=True)


def chip_copy(value, source, target):
    return lax.ppermute(value, ("y", "x"), [(4 * a + b, 4 * c + d) for (a, b), (c, d) in zip(source, target)])


def per_device(ctx_query, context_key, context_value, query, out_weight):
    core, x, y = (lax.axis_index(name) for name in ("c", "x", "y"))
    key_p, value_p = swap(context_key), swap(context_value)
    piece = jnp.where(core == 0, context_key, value_p)
    along_x = [chip_copy(piece, [(0, 0)], [(0, k)]) for k in (1, 2, 3)]
    weight_p = swap(out_weight)
    sent = query_call(query, context_key, context_value, key_p, value_p)
    received = exchange(sent, ("y", "x"))
    acc, stat = own_call(ctx_query, context_key, context_value, sent)
    row = jnp.where(x == 0, piece, jnp.where(x == 1, along_x[0], jnp.where(x == 2, along_x[1], along_x[2])))
    along_y = [chip_copy(row, [(0, j) for j in range(4)], [(k, j) for j in range(4)]) for k in (1, 2, 3)]
    gathered = exchange(combine_call(received, stat), ("y", "x"))
    half = jnp.where(y == 0, row, jnp.where(y == 1, along_y[0], jnp.where(y == 2, along_y[1], along_y[2])))
    other = swap(half)
    key_a = jnp.where(core == 0, half, other)
    value_a = jnp.where(core == 0, other, half)
    shares = project_call(gathered, out_weight, weight_p)
    ctx_out = anchor_call(ctx_query, key_a, value_a, acc, stat)
    answer = final_call(exchange(shares, ("z", "c")))
    return ctx_out, answer


def solution(mesh):
    fine = Mesh(mesh.devices.reshape(4, 4, 2, 8), ("y", "x", "c", "z"))
    hst = ("y", "x", "c")
    in_specs = (P(hst, "z"), P(hst, "z"), P(hst, "z"), P(None, "z"), P("z", hst))
    out_specs = (P(hst, "z"), P("z", hst))
    return jax.shard_map(
        per_device, mesh=fine, in_specs=in_specs, out_specs=out_specs, check_vma=False
    )
```

```python
import functools

import jax
import jax.numpy as jnp
from jax import lax
from jax.experimental import pallas as pl
from jax.experimental.pallas import tpu as pltpu
from jax.sharding import Mesh, PartitionSpec as P

HEAD = 128
BLOCK = 768
HEADS = 8
QROWS = 512
HALF = 256
SEND1 = HEAD + 16
HIDDEN = 1e30
LOG2_SCALE = 1.4426950408889634 * HEAD ** (-0.5)
BF = jnp.bfloat16
F32 = jnp.float32


def scores_of(q, k):
    return lax.dot_general(q, k, (((1,), (1,)), ((), ())), preferred_element_type=F32) * LOG2_SCALE


def pipelined(count, scores, finish):
    s = scores(0)
    for n in range(count):
        s_next = scores(n + 1) if n + 1 < count else None
        finish(n, s)
        s = s_next


def to_lanes(column):
    r = lax.broadcasted_iota(jnp.int32, (HEAD, HEAD), 0)
    c = lax.broadcasted_iota(jnp.int32, (HEAD, HEAD), 1)
    return jnp.sum(jnp.where(r == c, column, 0.0), axis=0, keepdims=True)


def prep_kernel(q_hbm, k_hbm, v_hbm, q_ref, k_ref, values_ref, v_buf, sems):
    core = lax.axis_index("c")
    copies = [pltpu.make_async_copy(v_hbm, v_buf, sems.at[0]), pltpu.make_async_copy(k_hbm, k_ref, sems.at[1])]
    for z in range(8):
        rows = pl.ds(pl.multiple_of(64 * z + 32 * core, 32), 32)
        copies.append(
            pltpu.make_async_copy(q_hbm.at[rows, :], q_ref.at[32 * z : 32 * z + 32, :], sems.at[2 + z])
        )
    for copy in copies:
        copy.start()
    values_ref[:, HEAD : 2 * HEAD] = jnp.ones((BLOCK, HEAD), BF)
    for copy in copies:
        copy.wait()
    values_ref[:, 0:HEAD] = v_buf[...]


def query_kernel(q_ref, k_ref, values_ref, kp_ref, vp_ref, out_ref, piece_ref, values_p):
    core = lax.axis_index("c")
    values_p[:, 0:HEAD] = vp_ref[...]
    values_p[:, HEAD : 2 * HEAD] = jnp.ones((BLOCK, HEAD), BF)
    row_id = lax.broadcasted_iota(jnp.int32, (16, HEAD), 0)

    def scores(j):
        q = q_ref[:, HEAD * j : HEAD * j + HEAD]
        return scores_of(q, k_ref[...]), scores_of(q, kp_ref[...])

    def finish(j, s):
        peak = jnp.maximum(
            jnp.max(s[0], axis=1, keepdims=True), jnp.max(s[1], axis=1, keepdims=True)
        )
        peak = peak.astype(BF).astype(F32)
        acc = jnp.dot(
            jnp.exp2(s[0] - peak).astype(BF), values_ref[...], preferred_element_type=F32
        ) + jnp.dot(jnp.exp2(s[1] - peak).astype(BF), values_p[...], preferred_element_type=F32)
        total = acc[:, HEAD : HEAD + 1]
        for half in range(2):
            rows = slice(half * HEAD, half * HEAD + HEAD)
            out_ref[2 * j + half, 0:HEAD, :] = acc[rows, 0:HEAD].astype(BF)
            peak_l = to_lanes(peak[rows])
            total_l = to_lanes(total[rows])
            high = total_l.astype(BF).astype(F32)
            stats = jnp.where(row_id == 0, peak_l, 0.0)
            stats = jnp.where(row_id == 1, high, stats)
            stats = jnp.where(row_id == 2, total_l - high, stats)
            out_ref[2 * j + half, HEAD:SEND1, :] = stats.astype(BF)

    pipelined(HEADS, scores, finish)
    piece_ref[...] = jnp.where(core == 0, k_ref[...], vp_ref[...])


def combine_kernel(in_ref, after_ref, out_ref):
    stats = in_ref[:, HEAD : HEAD + 16, :].astype(F32)
    peak = stats[:, 0, :]
    total = stats[:, 1, :] + stats[:, 2, :]
    top = jnp.max(peak, axis=0, keepdims=True)
    weight = jnp.exp2(peak - top)
    weight = weight / jnp.sum(weight * total, axis=0, keepdims=True)
    weight_t = jnp.concatenate([weight, jnp.zeros((HEAD - 16, HEAD), F32)], axis=0).T
    out = jnp.zeros((HEAD, HEAD), F32)
    for g in range(16):
        out = out + weight_t[:, g : g + 1] * in_ref[g, 0:HEAD, :].astype(F32)
    out = out.astype(BF)
    for g in range(16):
        out_ref[g] = out


def project_kernel(in_ref, w_ref, wp_ref, out_ref):
    core = lax.axis_index("c")
    a = jnp.concatenate(
        [
            jnp.concatenate([in_ref[2 * j + half] for j in range(HEADS)], axis=1)
            for half in range(2)
        ],
        axis=0,
    )
    for w, dest in ((w_ref, core), (wp_ref, 1 - core)):
        y = jnp.dot(a, w[...], preferred_element_type=F32).astype(BF)
        for z in range(8):
            out_ref[2 * z + dest] = y[32 * z : 32 * z + 32, :]


def final_kernel(in_ref, out_ref):
    for half in range(2):
        total = in_ref[half].astype(F32)
        for z in range(1, 8):
            total = total + in_ref[2 * z + half].astype(F32)
        out_ref[32 * half : 32 * half + 32, :] = total.astype(BF)


def column_copies(make):
    return [make(slice(2 * HEAD * g, 2 * HEAD * g + 2 * HEAD), g) for g in range(HEADS // 2)]


CONTEXT_BLOCKS = [(j, i) for j in range(HEADS) for i in range(3)]


def own_kernel(q_hbm, k_ref, values_ref, after_ref, acc_ref, peak_ref, q_ref, sems):
    copies = column_copies(
        lambda cols, g: pltpu.make_async_copy(q_hbm.at[:, cols], q_ref.at[:, cols], sems.at[g])
    )
    for copy in copies:
        copy.start()
    r = lax.broadcasted_iota(jnp.int32, (HALF, HALF), 0)
    c = lax.broadcasted_iota(jnp.int32, (HALF, HALF), 1)

    def scores(n):
        j, i = CONTEXT_BLOCKS[n]
        if j % 2 == 0 and i == 0:
            copies[j // 2].wait()
        q = q_ref[i * HALF : (i + 1) * HALF, HEAD * j : HEAD * j + HEAD]
        return scores_of(q, k_ref[0 : (i + 1) * HALF, :])

    def finish(n, s):
        j, i = CONTEXT_BLOCKS[n]
        rows = slice(i * HALF, (i + 1) * HALF)
        diagonal = jnp.where(c <= r, s[:, i * HALF :], -HIDDEN)
        s = jnp.concatenate([s[:, 0 : i * HALF], diagonal], axis=1) if i else diagonal
        peak = jnp.max(s, axis=1, keepdims=True)
        p = jnp.exp2(s - peak).astype(BF)
        acc = jnp.dot(p, values_ref[0 : (i + 1) * HALF, :], preferred_element_type=F32)
        acc_ref[rows, 2 * HEAD * j : 2 * HEAD * (j + 1)] = acc
        peak_ref[rows, HEAD * j : HEAD * j + HEAD] = jnp.broadcast_to(peak, (HALF, HEAD))

    pipelined(len(CONTEXT_BLOCKS), scores, finish)


def anchor_kernel(
    q_hbm, half_ref, other_ref, acc_ref, peak_ref, out_hbm, q_ref, out_ref, k_ref, values_ref, sems, out_sems
):
    copies = column_copies(
        lambda cols, g: pltpu.make_async_copy(q_hbm.at[:, cols], q_ref.at[:, cols], sems.at[g])
    )
    for copy in copies:
        copy.start()
    writes = column_copies(
        lambda cols, g: pltpu.make_async_copy(out_ref.at[:, cols], out_hbm.at[:, cols], out_sems.at[g])
    )
    core = lax.axis_index("c")
    first = jnp.logical_and(
        core == 0, jnp.logical_and(lax.axis_index("x") == 0, lax.axis_index("y") == 0)
    )
    k_ref[...] = jnp.where(core == 0, half_ref[...], other_ref[...])
    values_ref[:, 0:HEAD] = jnp.where(core == 0, other_ref[...], half_ref[...])
    values_ref[:, HEAD : 2 * HEAD] = jnp.ones((BLOCK, HEAD), BF)

    def scores(n):
        j, i = CONTEXT_BLOCKS[n]
        if j % 2 == 0 and i == 0:
            copies[j // 2].wait()
        return scores_of(q_ref[i * HALF : (i + 1) * HALF, HEAD * j : HEAD * j + HEAD], k_ref[...])

    def finish(n, s):
        j, i = CONTEXT_BLOCKS[n]
        rows = slice(i * HALF, (i + 1) * HALF)
        own_peak = peak_ref[rows, HEAD * j : HEAD * j + HEAD]
        peak = jnp.maximum(own_peak, jnp.max(s, axis=1, keepdims=True))
        peak = jnp.where(first, own_peak, peak)
        shift = jnp.where(first, HIDDEN, peak)
        p = jnp.exp2(s - jnp.concatenate([shift] * 6, axis=1)).astype(BF)
        acc = jnp.dot(p, values_ref[...], preferred_element_type=F32)
        scale = jnp.exp2(own_peak - peak)
        own = acc_ref[rows, 2 * HEAD * j : 2 * HEAD * (j + 1)]
        total = acc[:, HEAD : 2 * HEAD] + scale * own[:, HEAD : 2 * HEAD]
        mixture = acc[:, 0:HEAD] + scale * own[:, 0:HEAD]
        out_ref[rows, HEAD * j : HEAD * j + HEAD] = (mixture / total).astype(BF)
        if j % 2 == 1 and i == 2:
            writes[j // 2].start()

    pipelined(len(CONTEXT_BLOCKS), scores, finish)
    for copy in writes:
        copy.wait()


def pick_kernel(axis, mine_ref, one_ref, two_ref, three_ref, after_ref, out_ref):
    at = lax.axis_index(axis)
    for k, ref in enumerate((mine_ref, one_ref, two_ref, three_ref)):

        @pl.when(at == k)
        def _(ref=ref):
            out_ref[...] = ref[...]


VMEM = pl.BlockSpec(memory_space=pltpu.VMEM)
HBM = pl.BlockSpec(memory_space=pltpu.HBM)
ANY = pl.BlockSpec(memory_space=pl.ANY)


def params():
    return pltpu.CompilerParams(vmem_limit_bytes=24 * 1024 * 1024)


def cost(flops, nbytes, exps=0):
    return pl.CostEstimate(flops=flops, bytes_accessed=nbytes, transcendentals=exps)


def shape(dims, dtype=BF):
    return jax.ShapeDtypeStruct(dims, dtype)


def in_hbm(value):
    return pltpu.with_memory_space_constraint(value, pltpu.HBM)


def prep_call(query, k, v):
    return pl.pallas_call(
        prep_kernel,
        in_specs=[HBM] * 3,
        out_specs=(VMEM,) * 3,
        out_shape=(shape((HALF, HEADS * HEAD)), shape((BLOCK, HEAD)), shape((BLOCK, 2 * HEAD))),
        scratch_shapes=[pltpu.VMEM((BLOCK, HEAD), BF), pltpu.SemaphoreType.DMA((10,))],
        compiler_params=params(),
        cost_estimate=cost(1 << 18, 2 << 20),
        name="prep",
    )(in_hbm(query), in_hbm(k), in_hbm(v))


def query_call(q, k, values, kp, vp):
    return pl.pallas_call(
        query_kernel,
        in_specs=[VMEM] * 5,
        out_specs=(VMEM,) * 2,
        out_shape=(shape((16, SEND1, HEAD)), shape((BLOCK, HEAD))),
        scratch_shapes=[pltpu.VMEM((BLOCK, 2 * HEAD), BF)],
        compiler_params=params(),
        cost_estimate=cost(4 * 2048 * 1536 * 256, 3 << 20, 2048 * 1536),
        name="query_attention",
    )(q, k, values, kp, vp)


def own_call(ctx_query, k, values, after):
    return pl.pallas_call(
        own_kernel,
        in_specs=[HBM, VMEM, VMEM, ANY],
        out_specs=(VMEM,) * 2,
        out_shape=(shape((BLOCK, 2 * HEADS * HEAD), F32), shape((BLOCK, HEADS * HEAD), F32)),
        scratch_shapes=[pltpu.VMEM((BLOCK, HEADS * HEAD), BF), pltpu.SemaphoreType.DMA((4,))],
        compiler_params=params(),
        cost_estimate=cost(4 * 6144 * 512 * 256, 4 << 20, 6144 * 512),
        name="context_own",
    )(in_hbm(ctx_query), k, values, after)


def anchor_call(ctx_query, half, other, acc, peak):
    return pl.pallas_call(
        anchor_kernel,
        in_specs=[HBM, VMEM, VMEM, VMEM, VMEM],
        out_specs=HBM,
        out_shape=shape((BLOCK, HEADS * HEAD)),
        scratch_shapes=[
            pltpu.VMEM((BLOCK, HEADS * HEAD), BF),
            pltpu.VMEM((BLOCK, HEADS * HEAD), BF),
            pltpu.VMEM((BLOCK, HEAD), BF),
            pltpu.VMEM((BLOCK, 2 * HEAD), BF),
            pltpu.SemaphoreType.DMA((4,)),
            pltpu.SemaphoreType.DMA((4,)),
        ],
        compiler_params=params(),
        cost_estimate=cost(4 * 6144 * 768 * 256, 6 << 20, 6144 * 768),
        name="context_anchor",
    )(in_hbm(ctx_query), half, other, acc, peak)


def pick_call(axis, mine, moved, after):
    return pl.pallas_call(
        functools.partial(pick_kernel, axis),
        in_specs=[VMEM] * 4 + [ANY],
        out_specs=VMEM,
        out_shape=shape((BLOCK, HEAD)),
        compiler_params=params(),
        cost_estimate=cost(1 << 16, 1 << 19),
        name="pick_" + axis,
    )(mine, *moved, after)


def combine_call(received, after):
    return pl.pallas_call(
        combine_kernel,
        out_shape=shape((16, HEAD, HEAD)),
        in_specs=[VMEM, ANY],
        out_specs=VMEM,
        compiler_params=params(),
        cost_estimate=cost(1 << 20, 3 << 19),
        name="combine",
    )(received, after)


def project_call(gathered, w, wp):
    return pl.pallas_call(
        project_kernel,
        out_shape=shape((16, 32, 256)),
        in_specs=[VMEM] * 3,
        out_specs=VMEM,
        compiler_params=params(),
        cost_estimate=cost(2 * 256 * 1024 * 512, 2 << 20),
        name="project",
    )(gathered, w, wp)


def final_call(received):
    return pl.pallas_call(
        final_kernel,
        out_shape=shape((64, 256)),
        in_specs=[VMEM],
        out_specs=VMEM,
        compiler_params=params(),
        cost_estimate=cost(1 << 17, 1 << 18),
        name="final_sum",
    )(received)


def swap(value):
    return lax.ppermute(value, "c", [(0, 1), (1, 0)])


def exchange(value, axes):
    return lax.all_to_all(value, axes, 0, 0, tiled=True)


def chip_copies(value, pairs_of):
    moved = []
    for k in (1, 2, 3):
        to = {(a, b): (a, b) for a in range(4) for b in range(4)}
        for source, target in pairs_of(k):
            to[source], to[target] = target, source
        moved.append(
            lax.ppermute(value, ("y", "x"), [(4 * a + b, 4 * c + d) for (a, b), (c, d) in to.items()])
        )
    return moved


def per_device(ctx_query, context_key, context_value, query, out_weight):
    key_p, value_p = swap(context_key), swap(context_value)
    q, k, values = prep_call(query, context_key, context_value)
    sent, piece = query_call(q, k, values, key_p, value_p)
    received = exchange(sent, ("y", "x"))
    along_x = chip_copies(piece, lambda k: [((0, 0), (0, k))])
    weight_p = swap(out_weight)
    acc, peak = own_call(ctx_query, k, values, sent)
    merged = combine_call(received, peak)
    gathered = exchange(merged, ("y", "x"))
    row = pick_call("x", piece, along_x, merged)
    along_y = chip_copies(row, lambda k: [((0, j), (k, j)) for j in range(4)])
    shares = project_call(gathered, out_weight, weight_p)
    half = pick_call("y", row, along_y, shares)
    ctx_out = anchor_call(ctx_query, half, swap(half), acc, peak)
    answer = final_call(exchange(shares, ("z", "c")))
    return ctx_out, answer


def solution(mesh):
    fine = Mesh(mesh.devices.reshape(4, 4, 2, 8), ("y", "x", "c", "z"))
    hst = ("y", "x", "c")
    in_specs = (P(hst, "z"), P(hst, "z"), P(hst, "z"), P(None, "z"), P("z", hst))
    out_specs = (P(hst, "z"), P("z", hst))
    return jax.shard_map(
        per_device, mesh=fine, in_specs=in_specs, out_specs=out_specs, check_vma=False
    )
```

```python
import functools

import jax
import jax.numpy as jnp
from jax import lax
from jax.experimental import pallas as pl
from jax.experimental.pallas import tpu as pltpu
from jax.sharding import Mesh, PartitionSpec as P

HEAD = 128
BLOCK = 768
HEADS = 8
HALF = 256
STATS = HEAD + 16
ANCHOR_ROWS = 48
SEND1 = STATS + ANCHOR_ROWS
SEND2 = HEAD + ANCHOR_ROWS
HIDDEN = 1e30
LOG2_SCALE = 1.4426950408889634 * HEAD ** (-0.5)
BF = jnp.bfloat16
F32 = jnp.float32


def scores_of(q, k):
    return lax.dot_general(q, k, (((1,), (1,)), ((), ())), preferred_element_type=F32) * LOG2_SCALE


def pipelined(count, scores, finish):
    s = scores(0)
    for n in range(count):
        s_next = scores(n + 1) if n + 1 < count else None
        finish(n, s)
        s = s_next


def to_lanes(column):
    r = lax.broadcasted_iota(jnp.int32, (HEAD, HEAD), 0)
    c = lax.broadcasted_iota(jnp.int32, (HEAD, HEAD), 1)
    return jnp.sum(jnp.where(r == c, column, 0.0), axis=0, keepdims=True)


def prep_kernel(q_hbm, k_hbm, v_hbm, q_ref, k_ref, values_ref, v_buf, sems):
    rows = pl.ds(pl.multiple_of(HALF * lax.axis_index("c"), HALF), HALF)
    copies = [
        pltpu.make_async_copy(v_hbm, v_buf, sems.at[0]),
        pltpu.make_async_copy(k_hbm, k_ref, sems.at[1]),
        pltpu.make_async_copy(q_hbm.at[rows, :], q_ref, sems.at[2]),
    ]
    for copy in copies:
        copy.start()
    values_ref[:, HEAD : 2 * HEAD] = jnp.ones((BLOCK, HEAD), BF)
    for copy in copies:
        copy.wait()
    values_ref[:, 0:HEAD] = v_buf[...]


def query_kernel(q_ref, k_ref, values_ref, kp_ref, vp_ref, out_ref, values_p):
    core = lax.axis_index("c")
    values_p[:, 0:HEAD] = vp_ref[...]
    values_p[:, HEAD : 2 * HEAD] = jnp.ones((BLOCK, HEAD), BF)
    row_id = lax.broadcasted_iota(jnp.int32, (16, HEAD), 0)

    def scores(j):
        q = q_ref[:, HEAD * j : HEAD * j + HEAD]
        return scores_of(q, k_ref[...]), scores_of(q, kp_ref[...])

    def finish(j, s):
        peak = jnp.maximum(
            jnp.max(s[0], axis=1, keepdims=True), jnp.max(s[1], axis=1, keepdims=True)
        )
        peak = peak.astype(BF).astype(F32)
        acc = jnp.dot(
            jnp.exp2(s[0] - peak).astype(BF), values_ref[...], preferred_element_type=F32
        ) + jnp.dot(jnp.exp2(s[1] - peak).astype(BF), values_p[...], preferred_element_type=F32)
        total = acc[:, HEAD : HEAD + 1]
        for half in range(2):
            rows = slice(half * HEAD, half * HEAD + HEAD)
            out_ref[2 * j + half, 0:HEAD, :] = acc[rows, 0:HEAD].astype(BF)
            peak_l = to_lanes(peak[rows])
            total_l = to_lanes(total[rows])
            high = total_l.astype(BF).astype(F32)
            stats = jnp.where(row_id == 0, peak_l, 0.0)
            stats = jnp.where(row_id == 1, high, stats)
            stats = jnp.where(row_id == 2, total_l - high, stats)
            out_ref[2 * j + half, HEAD:STATS, :] = stats.astype(BF)
            at = (2 * j + half) * ANCHOR_ROWS
            out_ref[2 * j + half, STATS:SEND1, :] = jnp.where(
                core == 0, k_ref[at : at + ANCHOR_ROWS, :], vp_ref[at : at + ANCHOR_ROWS, :]
            )

    pipelined(HEADS, scores, finish)


def combine_kernel(in_ref, after_ref, out_ref):
    stats = in_ref[:, HEAD:STATS, :].astype(F32)
    peak = stats[:, 0, :]
    total = stats[:, 1, :] + stats[:, 2, :]
    top = jnp.max(peak, axis=0, keepdims=True)
    weight = jnp.exp2(peak - top)
    weight = weight / jnp.sum(weight * total, axis=0, keepdims=True)
    weight_t = jnp.concatenate([weight, jnp.zeros((HEAD - 16, HEAD), F32)], axis=0).T
    out = jnp.zeros((HEAD, HEAD), F32)
    for g in range(16):
        out = out + weight_t[:, g : g + 1] * in_ref[g, 0:HEAD, :].astype(F32)
    out = out.astype(BF)
    anchor = in_ref[0, STATS:SEND1, :]
    for g in range(16):
        out_ref[g, 0:HEAD, :] = out
        out_ref[g, HEAD:SEND2, :] = anchor


def project_kernel(mine_ref, other_ref, w_ref, out_ref, k_hbm, v_hbm, k_ref, v_ref, sems):
    core = lax.axis_index("c")
    for g in range(16):
        rows = slice(g * ANCHOR_ROWS, (g + 1) * ANCHOR_ROWS)
        one, two = mine_ref[g, HEAD:SEND2, :], other_ref[g, HEAD:SEND2, :]
        k_ref[rows, :] = jnp.where(core == 0, one, two)
        v_ref[rows, :] = jnp.where(core == 0, two, one)
    copies = (
        pltpu.make_async_copy(k_ref, k_hbm, sems.at[0]),
        pltpu.make_async_copy(v_ref, v_hbm, sems.at[1]),
    )
    for copy in copies:
        copy.start()
    for ref, owner in ((mine_ref, core), (other_ref, 1 - core)):
        a = jnp.concatenate(
            [
                jnp.concatenate([ref[2 * j + half, 0:HEAD, :] for j in range(HEADS)], axis=1)
                for half in range(2)
            ],
            axis=0,
        )
        y = jnp.dot(a, w_ref[...], preferred_element_type=F32).astype(BF)
        for z in range(4):
            out_ref[4 * owner + z] = y[64 * z : 64 * z + 64, :]
    for copy in copies:
        copy.wait()


def final_kernel(in_ref, out_ref):
    total = in_ref[0].astype(F32)
    for z in range(1, 8):
        total = total + in_ref[z].astype(F32)
    out_ref[...] = total.astype(BF)


EARLY = slice(0, 2 * HEAD)
LATE = slice(2 * HEAD, HEADS * HEAD)


def early_and_late(source, target, sems):
    return [
        pltpu.make_async_copy(source.at[:, cols], target.at[:, cols], sems.at[n])
        for n, cols in enumerate((EARLY, LATE))
    ]


def head_columns(j):
    return pl.ds(pl.multiple_of(HEAD * j, HEAD), HEAD)


def head_loop(scores, finish, s_ref, late, write):
    s_ref[...] = scores(0, 0)

    def body(j, carry):
        @pl.when(j == 1)
        def _():
            for copy in late:
                copy.wait()

        s0 = s_ref[...]
        s1 = scores(j, 1)
        finish(j, 0, s0)
        s2 = scores(j, 2)
        finish(j, 1, s1)
        s_ref[...] = scores(jnp.minimum(j + 1, HEADS - 1), 0)
        finish(j, 2, s2)
        write(j).start()
        return carry

    lax.fori_loop(0, HEADS, body, 0)


def own_kernel(
    q_hbm, k_hbm, v_hbm, after_ref, out_hbm, lse_hbm,
    q_ref, k_ref, values_ref, out_ref, lse_ref, s_ref, v_ref, sems, out_sems,
):
    early, late = early_and_late(q_hbm, q_ref, sems)
    k_copy = pltpu.make_async_copy(k_hbm, k_ref, sems.at[2])
    v_copy = pltpu.make_async_copy(v_hbm, v_ref, sems.at[3])
    for copy in (k_copy, early, v_copy, late):
        copy.start()
    values_ref[:, HEAD : 2 * HEAD] = jnp.ones((BLOCK, HEAD), BF)
    lse_ref[...] = jnp.zeros((BLOCK, HEAD), F32)
    lane = lax.broadcasted_iota(jnp.int32, (HALF, HEAD), 1)
    r = lax.broadcasted_iota(jnp.int32, (HALF, HALF), 0)
    c = lax.broadcasted_iota(jnp.int32, (HALF, HALF), 1)
    for copy in (k_copy, early, v_copy):
        copy.wait()
    values_ref[:, 0:HEAD] = v_ref[...]

    def scores(j, i):
        return scores_of(q_ref[i * HALF : (i + 1) * HALF, head_columns(j)], k_ref[0 : (i + 1) * HALF, :])

    def finish(j, i, s):
        rows = slice(i * HALF, (i + 1) * HALF)
        diagonal = jnp.where(c <= r, s[:, i * HALF :], -HIDDEN)
        s = jnp.concatenate([s[:, 0 : i * HALF], diagonal], axis=1) if i else diagonal
        peak = jnp.max(s, axis=1, keepdims=True)
        p = jnp.exp2(s - peak).astype(BF)
        acc = jnp.dot(p, values_ref[0 : (i + 1) * HALF, :], preferred_element_type=F32)
        total = acc[:, HEAD : 2 * HEAD]
        out_ref[rows, head_columns(j)] = acc[:, 0:HEAD] / total
        lse_ref[rows, :] = jnp.where(lane == j, peak + jnp.log2(total), lse_ref[rows, :])

    def write(j):
        cols = head_columns(j)
        return pltpu.make_async_copy(out_ref.at[:, cols], out_hbm.at[:, cols], out_sems.at[j])

    head_loop(scores, finish, s_ref, [late], write)
    lse_copy = pltpu.make_async_copy(lse_ref, lse_hbm, sems.at[2])
    lse_copy.start()
    for j in range(HEADS):
        write(j).wait()
    lse_copy.wait()


def anchor_kernel(
    q_hbm, k_hbm, v_hbm, own_hbm, lse_hbm, out_hbm,
    q_ref, k_ref, values_ref, own_ref, lse_ref, out_ref, s_ref, v_ref, sems, out_sems,
):
    early, late = early_and_late(q_hbm, q_ref, sems)
    k_copy = pltpu.make_async_copy(k_hbm, k_ref, sems.at[2])
    v_copy = pltpu.make_async_copy(v_hbm, v_ref, sems.at[3])
    own_early, own_late = early_and_late(own_hbm, own_ref, sems.at[4:6])
    lse_copy = pltpu.make_async_copy(lse_hbm, lse_ref, sems.at[6])
    for copy in (k_copy, early, v_copy, lse_copy, own_early, late, own_late):
        copy.start()
    first = jnp.logical_and(
        lax.axis_index("c") == 0,
        jnp.logical_and(lax.axis_index("x") == 0, lax.axis_index("y") == 0),
    )
    lane = lax.broadcasted_iota(jnp.int32, (HALF, HEAD), 1)
    values_ref[:, HEAD : 2 * HEAD] = jnp.ones((BLOCK, HEAD), BF)
    for copy in (k_copy, early, v_copy, lse_copy, own_early):
        copy.wait()
    values_ref[:, 0:HEAD] = v_ref[...]

    def scores(j, i):
        return scores_of(q_ref[i * HALF : (i + 1) * HALF, head_columns(j)], k_ref[...])

    def finish(j, i, s):
        rows = slice(i * HALF, (i + 1) * HALF)
        lse = jnp.sum(jnp.where(lane == j, lse_ref[rows, :], 0.0), axis=1, keepdims=True)
        peak = jnp.maximum(lse, jnp.max(s, axis=1, keepdims=True))
        peak = jnp.where(first, lse, peak)
        p = jnp.exp2(s - jnp.where(first, HIDDEN, peak)).astype(BF)
        acc = jnp.dot(p, values_ref[...], preferred_element_type=F32)
        weight = jnp.exp2(lse - peak)
        mixture = acc[:, 0:HEAD] + weight * own_ref[rows, head_columns(j)]
        out_ref[rows, head_columns(j)] = (mixture / (acc[:, HEAD : 2 * HEAD] + weight)).astype(BF)

    def write(j):
        cols = head_columns(j)
        return pltpu.make_async_copy(out_ref.at[:, cols], out_hbm.at[:, cols], out_sems.at[j])

    head_loop(scores, finish, s_ref, [late, own_late], write)
    for j in range(HEADS):
        write(j).wait()


VMEM = pl.BlockSpec(memory_space=pltpu.VMEM)
HBM = pl.BlockSpec(memory_space=pltpu.HBM)
ANY = pl.BlockSpec(memory_space=pl.ANY)
WIDE = HEADS * HEAD


def in_hbm(*arrays):
    return [pltpu.with_memory_space_constraint(a, pltpu.HBM) for a in arrays]


def shape(dims, dtype=BF):
    return jax.ShapeDtypeStruct(dims, dtype)


def buffer(dims, dtype=BF):
    return pltpu.VMEM(dims, dtype)


def run(kernel, name, operands, in_specs, out_shape, out_specs, scratch, flops, nbytes, exps=0):
    return pl.pallas_call(
        kernel,
        in_specs=in_specs,
        out_specs=out_specs,
        out_shape=out_shape,
        scratch_shapes=scratch,
        compiler_params=pltpu.CompilerParams(vmem_limit_bytes=24 * 1024 * 1024),
        cost_estimate=pl.CostEstimate(flops=flops, bytes_accessed=nbytes, transcendentals=exps),
        name=name,
    )(*operands)


def prep_call(query, k, v):
    return run(
        prep_kernel, "prep", in_hbm(query, k, v), [HBM] * 3,
        (shape((HALF, WIDE)), shape((BLOCK, HEAD)), shape((BLOCK, 2 * HEAD))), (VMEM,) * 3,
        [buffer((BLOCK, HEAD)), pltpu.SemaphoreType.DMA((3,))], 1 << 18, 2 << 20,
    )


def query_call(q, k, values, kp, vp):
    return run(
        query_kernel, "query_attention", (q, k, values, kp, vp), [VMEM] * 5,
        shape((16, SEND1, HEAD)), VMEM, [buffer((BLOCK, 2 * HEAD))],
        4 * 2048 * 1536 * 256, 3 << 20, 2048 * 1536,
    )


def own_call(ctx_query, k, v, after):
    return run(
        own_kernel, "context_own", (*in_hbm(ctx_query, k, v), after), [HBM, HBM, HBM, ANY],
        (pltpu.HBM((BLOCK, WIDE), F32), pltpu.HBM((BLOCK, HEAD), F32)), (HBM, HBM),
        [
            buffer((BLOCK, WIDE)), buffer((BLOCK, HEAD)), buffer((BLOCK, 2 * HEAD)), buffer((BLOCK, WIDE), F32),
            buffer((BLOCK, HEAD), F32), buffer((HALF, HALF), F32), buffer((BLOCK, HEAD)),
            pltpu.SemaphoreType.DMA((4,)), pltpu.SemaphoreType.DMA((HEADS,)),
        ],
        4 * 6144 * 512 * 256, 4 << 20, 6144 * 512,
    )


def anchor_call(ctx_query, k, v, own, lse):
    return run(
        anchor_kernel, "context_anchor", in_hbm(ctx_query, k, v, own, lse), [HBM] * 5,
        shape((BLOCK, WIDE)), HBM,
        [
            buffer((BLOCK, WIDE)), buffer((BLOCK, HEAD)), buffer((BLOCK, 2 * HEAD)), buffer((BLOCK, WIDE), F32),
            buffer((BLOCK, HEAD), F32), buffer((BLOCK, WIDE)), buffer((HALF, BLOCK), F32), buffer((BLOCK, HEAD)),
            pltpu.SemaphoreType.DMA((7,)), pltpu.SemaphoreType.DMA((HEADS,)),
        ],
        4 * 6144 * 768 * 256, 6 << 20, 6144 * 768,
    )


def combine_call(received, after):
    return run(
        combine_kernel, "combine", (received, *in_hbm(after)), [VMEM, HBM],
        shape((16, SEND2, HEAD)), VMEM, [], 1 << 20, 3 << 19,
    )


def project_call(mine, other, w):
    return run(
        project_kernel, "project", (mine, other, w), [VMEM] * 3,
        (shape((8, 64, 256)), pltpu.HBM((BLOCK, HEAD), BF), pltpu.HBM((BLOCK, HEAD), BF)), (VMEM, HBM, HBM),
        [buffer((BLOCK, HEAD)), buffer((BLOCK, HEAD)), pltpu.SemaphoreType.DMA((2,))],
        2 * 512 * 1024 * 256, 2 << 20,
    )


def final_call(received):
    return run(final_kernel, "final_sum", (received,), [VMEM], shape((64, 256)), VMEM, [], 1 << 17, 1 << 18)


def swap(value):
    return lax.ppermute(value, "c", [(0, 1), (1, 0)])


def exchange(value, axes):
    return lax.all_to_all(value, axes, 0, 0, tiled=True)


def per_device(ctx_query, context_key, context_value, query, out_weight):
    key_p, value_p = swap(context_key), swap(context_value)
    q, k, values = prep_call(query, context_key, context_value)
    sent = query_call(q, k, values, key_p, value_p)
    received = exchange(sent, ("y", "x"))
    own, lse = own_call(ctx_query, context_key, context_value, sent)
    gathered = exchange(combine_call(received, lse), ("y", "x"))
    shares, key_a, value_a = project_call(gathered, swap(gathered), out_weight)
    ctx_out = anchor_call(ctx_query, key_a, value_a, own, lse)
    answer = final_call(exchange(shares, "z"))
    return ctx_out, answer


def solution(mesh):
    fine = Mesh(mesh.devices.reshape(4, 4, 2, 8), ("y", "x", "c", "z"))
    hst = ("y", "x", "c")
    in_specs = (P(hst, "z"), P(hst, "z"), P(hst, "z"), P(None, "z"), P("z", hst))
    out_specs = (P(hst, "z"), P("z", hst))
    return jax.shard_map(
        per_device, mesh=fine, in_specs=in_specs, out_specs=out_specs, check_vma=False
    )
```

```python
import functools

import jax
import jax.numpy as jnp
from jax import lax
from jax.experimental import pallas as pl
from jax.experimental.pallas import tpu as pltpu
from jax.sharding import Mesh, PartitionSpec as P

HEAD = 128
BLOCK = 768
HEADS = 8
HALF = 256
STATS = HEAD + 16
ANCHOR_ROWS = 48
SEND1 = STATS + ANCHOR_ROWS
SEND2 = HEAD + ANCHOR_ROWS
HIDDEN = 1e30
LOG2_SCALE = 1.4426950408889634 * HEAD ** (-0.5)
BF = jnp.bfloat16
F32 = jnp.float32


def scores_of(q, k):
    return lax.dot_general(q, k, (((1,), (1,)), ((), ())), preferred_element_type=F32) * LOG2_SCALE


def pipelined(count, scores, finish):
    s = scores(0)
    for n in range(count):
        s_next = scores(n + 1) if n + 1 < count else None
        finish(n, s)
        s = s_next


def to_lanes(column):
    r = lax.broadcasted_iota(jnp.int32, (HEAD, HEAD), 0)
    c = lax.broadcasted_iota(jnp.int32, (HEAD, HEAD), 1)
    return jnp.sum(jnp.where(r == c, column, 0.0), axis=0, keepdims=True)


def prep_kernel(q_hbm, k_hbm, v_hbm, q_ref, k_ref, values_ref, v_buf, sems):
    rows = pl.ds(pl.multiple_of(HALF * lax.axis_index("c"), HALF), HALF)
    copies = [
        pltpu.make_async_copy(v_hbm, v_buf, sems.at[0]),
        pltpu.make_async_copy(k_hbm, k_ref, sems.at[1]),
        pltpu.make_async_copy(q_hbm.at[rows, :], q_ref, sems.at[2]),
    ]
    for copy in copies:
        copy.start()
    values_ref[:, HEAD : 2 * HEAD] = jnp.ones((BLOCK, HEAD), BF)
    for copy in copies:
        copy.wait()
    values_ref[:, 0:HEAD] = v_buf[...]


def query_kernel(q_ref, k_ref, values_ref, kp_ref, vp_ref, out_ref, values_p):
    core = lax.axis_index("c")
    values_p[:, 0:HEAD] = vp_ref[...]
    values_p[:, HEAD : 2 * HEAD] = jnp.ones((BLOCK, HEAD), BF)
    row_id = lax.broadcasted_iota(jnp.int32, (16, HEAD), 0)

    def scores(j):
        q = q_ref[:, HEAD * j : HEAD * j + HEAD]
        return scores_of(q, k_ref[...]), scores_of(q, kp_ref[...])

    def finish(j, s):
        peak = jnp.maximum(
            jnp.max(s[0], axis=1, keepdims=True), jnp.max(s[1], axis=1, keepdims=True)
        )
        peak = peak.astype(BF).astype(F32)
        acc = jnp.dot(
            jnp.exp2(s[0] - peak).astype(BF), values_ref[...], preferred_element_type=F32
        ) + jnp.dot(jnp.exp2(s[1] - peak).astype(BF), values_p[...], preferred_element_type=F32)
        total = acc[:, HEAD : HEAD + 1]
        for half in range(2):
            rows = slice(half * HEAD, half * HEAD + HEAD)
            out_ref[2 * j + half, 0:HEAD, :] = acc[rows, 0:HEAD].astype(BF)
            peak_l = to_lanes(peak[rows])
            total_l = to_lanes(total[rows])
            high = total_l.astype(BF).astype(F32)
            stats = jnp.where(row_id == 0, peak_l, 0.0)
            stats = jnp.where(row_id == 1, high, stats)
            stats = jnp.where(row_id == 2, total_l - high, stats)
            out_ref[2 * j + half, HEAD:STATS, :] = stats.astype(BF)
            at = (2 * j + half) * ANCHOR_ROWS
            out_ref[2 * j + half, STATS:SEND1, :] = jnp.where(
                core == 0, k_ref[at : at + ANCHOR_ROWS, :], vp_ref[at : at + ANCHOR_ROWS, :]
            )

    pipelined(HEADS, scores, finish)


def combine_kernel(in_ref, after_ref, out_ref):
    stats = in_ref[:, HEAD:STATS, :].astype(F32)
    peak = stats[:, 0, :]
    total = stats[:, 1, :] + stats[:, 2, :]
    top = jnp.max(peak, axis=0, keepdims=True)
    weight = jnp.exp2(peak - top)
    weight = weight / jnp.sum(weight * total, axis=0, keepdims=True)
    weight_t = jnp.concatenate([weight, jnp.zeros((HEAD - 16, HEAD), F32)], axis=0).T
    out = jnp.zeros((HEAD, HEAD), F32)
    for g in range(16):
        out = out + weight_t[:, g : g + 1] * in_ref[g, 0:HEAD, :].astype(F32)
    out = out.astype(BF)
    anchor = in_ref[0, STATS:SEND1, :]
    for g in range(16):
        out_ref[g, 0:HEAD, :] = out
        out_ref[g, HEAD:SEND2, :] = anchor


def project_kernel(mine_ref, other_ref, w_ref, out_ref, k_hbm, v_hbm, k_ref, v_ref, sems):
    core = lax.axis_index("c")
    for g in range(16):
        rows = slice(g * ANCHOR_ROWS, (g + 1) * ANCHOR_ROWS)
        one, two = mine_ref[g, HEAD:SEND2, :], other_ref[g, HEAD:SEND2, :]
        k_ref[rows, :] = jnp.where(core == 0, one, two)
        v_ref[rows, :] = jnp.where(core == 0, two, one)
    copies = (
        pltpu.make_async_copy(k_ref, k_hbm, sems.at[0]),
        pltpu.make_async_copy(v_ref, v_hbm, sems.at[1]),
    )
    for copy in copies:
        copy.start()
    for ref, owner in ((mine_ref, core), (other_ref, 1 - core)):
        a = jnp.concatenate(
            [
                jnp.concatenate([ref[2 * j + half, 0:HEAD, :] for j in range(HEADS)], axis=1)
                for half in range(2)
            ],
            axis=0,
        )
        y = jnp.dot(a, w_ref[...], preferred_element_type=F32).astype(BF)
        for z in range(4):
            out_ref[4 * owner + z] = y[64 * z : 64 * z + 64, :]
    for copy in copies:
        copy.wait()


def final_kernel(in_ref, out_ref):
    total = in_ref[0].astype(F32)
    for z in range(1, 8):
        total = total + in_ref[z].astype(F32)
    out_ref[...] = total.astype(BF)


STEP = 2
STEP_COLUMNS = STEP * HEAD


def fill_values(v_ref, values_ref):
    @pl.when(pl.program_id(0) == 0)
    def _():
        values_ref[:, 0:HEAD] = v_ref[...]
        values_ref[:, HEAD : 2 * HEAD] = jnp.ones((BLOCK, HEAD), BF)


def own_kernel(q_ref, k_ref, v_ref, after_ref, out_ref, lse_ref, values_ref):
    fill_values(v_ref, values_ref)

    @pl.when(pl.program_id(0) == 0)
    def _():
        lse_ref[...] = jnp.zeros((BLOCK, HEAD), F32)

    lane = lax.broadcasted_iota(jnp.int32, (HALF, HEAD), 1)
    r = lax.broadcasted_iota(jnp.int32, (HALF, HALF), 0)
    c = lax.broadcasted_iota(jnp.int32, (HALF, HALF), 1)

    def scores(h):
        return [
            scores_of(q_ref[i * HALF : (i + 1) * HALF, HEAD * h : HEAD * h + HEAD], k_ref[0 : (i + 1) * HALF, :])
            for i in range(3)
        ]

    def finish(h, s):
        head = pl.program_id(0) * STEP + h
        parts, peaks = [], []
        for i in range(3):
            diagonal = jnp.where(c <= r, s[i][:, i * HALF :], -HIDDEN)
            part = jnp.concatenate([s[i][:, 0 : i * HALF], diagonal], axis=1) if i else diagonal
            parts.append(part)
            peaks.append(jnp.max(part, axis=1, keepdims=True))
        for i in range(3):
            rows = slice(i * HALF, (i + 1) * HALF)
            p = jnp.exp2(parts[i] - peaks[i]).astype(BF)
            acc = jnp.dot(p, values_ref[0 : (i + 1) * HALF, :], preferred_element_type=F32)
            total = acc[:, HEAD : 2 * HEAD]
            out_ref[rows, HEAD * h : HEAD * h + HEAD] = (acc[:, 0:HEAD] / total).astype(BF)
            lse_ref[rows, :] = jnp.where(lane == head, peaks[i] + jnp.log2(total), lse_ref[rows, :])

    pipelined(STEP, scores, finish)


def anchor_kernel(q_ref, k_ref, v_ref, own_ref, lse_ref, out_ref, values_ref):
    fill_values(v_ref, values_ref)
    first = jnp.logical_and(
        lax.axis_index("c") == 0,
        jnp.logical_and(lax.axis_index("x") == 0, lax.axis_index("y") == 0),
    )
    lane = lax.broadcasted_iota(jnp.int32, (BLOCK, HEAD), 1)

    def scores(h):
        return scores_of(q_ref[:, HEAD * h : HEAD * h + HEAD], k_ref[...])

    def finish(h, s):
        head = pl.program_id(0) * STEP + h
        lse = jnp.sum(jnp.where(lane == head, lse_ref[...], 0.0), axis=1, keepdims=True)
        peak = jnp.maximum(lse, jnp.max(s, axis=1, keepdims=True))
        peak = jnp.where(first, lse, peak)
        p = jnp.exp2(s - jnp.where(first, HIDDEN, peak)).astype(BF)
        acc = jnp.dot(p, values_ref[...], preferred_element_type=F32)
        weight = jnp.exp2(lse - peak)
        mixture = acc[:, 0:HEAD] + weight * own_ref[:, HEAD * h : HEAD * h + HEAD].astype(F32)
        out_ref[:, HEAD * h : HEAD * h + HEAD] = (mixture / (acc[:, HEAD : 2 * HEAD] + weight)).astype(BF)

    pipelined(STEP, scores, finish)


VMEM = pl.BlockSpec(memory_space=pltpu.VMEM)
HBM = pl.BlockSpec(memory_space=pltpu.HBM)
ANY = pl.BlockSpec(memory_space=pl.ANY)
WIDE = HEADS * HEAD
STEP_BLOCK = pl.BlockSpec((BLOCK, STEP_COLUMNS), lambda t: (0, t))
HEAD_BLOCK = pl.BlockSpec((BLOCK, HEAD), lambda t: (0, 0))


def in_hbm(*arrays):
    return [pltpu.with_memory_space_constraint(a, pltpu.HBM) for a in arrays]


def shape(dims, dtype=BF):
    return jax.ShapeDtypeStruct(dims, dtype)


def buffer(dims, dtype=BF):
    return pltpu.VMEM(dims, dtype)


def run(kernel, name, operands, in_specs, out_shape, out_specs, scratch, flops, nbytes, exps=0, grid=()):
    return pl.pallas_call(
        kernel,
        grid=grid,
        in_specs=in_specs,
        out_specs=out_specs,
        out_shape=out_shape,
        scratch_shapes=scratch,
        compiler_params=pltpu.CompilerParams(vmem_limit_bytes=24 * 1024 * 1024),
        cost_estimate=pl.CostEstimate(flops=flops, bytes_accessed=nbytes, transcendentals=exps),
        name=name,
    )(*operands)


def prep_call(query, k, v):
    return run(
        prep_kernel, "prep", in_hbm(query, k, v), [HBM] * 3,
        (shape((HALF, WIDE)), shape((BLOCK, HEAD)), shape((BLOCK, 2 * HEAD))), (VMEM,) * 3,
        [buffer((BLOCK, HEAD)), pltpu.SemaphoreType.DMA((3,))], 1 << 18, 2 << 20,
    )


def query_call(q, k, values, kp, vp):
    return run(
        query_kernel, "query_attention", (q, k, values, kp, vp), [VMEM] * 5,
        shape((16, SEND1, HEAD)), VMEM, [buffer((BLOCK, 2 * HEAD))],
        4 * 2048 * 1536 * 256, 3 << 20, 2048 * 1536,
    )


def own_call(ctx_query, k, v, after):
    return run(
        own_kernel, "context_own", (*in_hbm(ctx_query, k, v), after),
        [STEP_BLOCK, HEAD_BLOCK, HEAD_BLOCK, ANY],
        (pltpu.HBM((BLOCK, WIDE), BF), pltpu.HBM((BLOCK, HEAD), F32)), (STEP_BLOCK, HEAD_BLOCK),
        [buffer((BLOCK, 2 * HEAD))], 4 * 6144 * 512 * 256, 4 << 20, 6144 * 512, grid=(HEADS // STEP,),
    )


def anchor_call(ctx_query, k, v, own, lse):
    return run(
        anchor_kernel, "context_anchor", in_hbm(ctx_query, k, v, own, lse),
        [STEP_BLOCK, HEAD_BLOCK, HEAD_BLOCK, STEP_BLOCK, HEAD_BLOCK],
        shape((BLOCK, WIDE)), STEP_BLOCK,
        [buffer((BLOCK, 2 * HEAD))], 4 * 6144 * 768 * 256, 6 << 20, 6144 * 768, grid=(HEADS // STEP,),
    )


def combine_call(received, after):
    return run(
        combine_kernel, "combine", (received, *in_hbm(after)), [VMEM, HBM],
        shape((16, SEND2, HEAD)), VMEM, [], 1 << 20, 3 << 19,
    )


def project_call(mine, other, w):
    return run(
        project_kernel, "project", (mine, other, w), [VMEM] * 3,
        (shape((8, 64, 256)), pltpu.HBM((BLOCK, HEAD), BF), pltpu.HBM((BLOCK, HEAD), BF)), (VMEM, HBM, HBM),
        [buffer((BLOCK, HEAD)), buffer((BLOCK, HEAD)), pltpu.SemaphoreType.DMA((2,))],
        2 * 512 * 1024 * 256, 2 << 20,
    )


def final_call(received):
    return run(final_kernel, "final_sum", (received,), [VMEM], shape((64, 256)), VMEM, [], 1 << 17, 1 << 18)


def swap(value):
    return lax.ppermute(value, "c", [(0, 1), (1, 0)])


def exchange(value, axes):
    return lax.all_to_all(value, axes, 0, 0, tiled=True)


def per_device(ctx_query, context_key, context_value, query, out_weight):
    key_p, value_p = swap(context_key), swap(context_value)
    q, k, values = prep_call(query, context_key, context_value)
    sent = query_call(q, k, values, key_p, value_p)
    received = exchange(sent, ("y", "x"))
    own, lse = own_call(ctx_query, context_key, context_value, sent)
    gathered = exchange(combine_call(received, lse), ("y", "x"))
    shares, key_a, value_a = project_call(gathered, swap(gathered), out_weight)
    ctx_out = anchor_call(ctx_query, key_a, value_a, own, lse)
    answer = final_call(exchange(shares, "z"))
    return ctx_out, answer


def solution(mesh):
    fine = Mesh(mesh.devices.reshape(4, 4, 2, 8), ("y", "x", "c", "z"))
    hst = ("y", "x", "c")
    in_specs = (P(hst, "z"), P(hst, "z"), P(hst, "z"), P(None, "z"), P("z", hst))
    out_specs = (P(hst, "z"), P("z", hst))
    return jax.shard_map(
        per_device, mesh=fine, in_specs=in_specs, out_specs=out_specs, check_vma=False
    )
```

```python
import functools

import jax
import jax.numpy as jnp
from jax import lax
from jax.experimental import pallas as pl
from jax.experimental.pallas import tpu as pltpu
from jax.sharding import Mesh, PartitionSpec as P

HEAD = 128
BLOCK = 768
HEADS = 8
HALF = 256
STATS = HEAD + 16
ANCHOR_ROWS = 48
SEND1 = STATS + ANCHOR_ROWS
SEND2 = HEAD + ANCHOR_ROWS
HIDDEN = 1e30
LOG2_SCALE = 1.4426950408889634 * HEAD ** (-0.5)
BF = jnp.bfloat16
F32 = jnp.float32


def scores_of(q, k):
    return lax.dot_general(q, k, (((1,), (1,)), ((), ())), preferred_element_type=F32) * LOG2_SCALE


def pipelined(count, scores, finish):
    s = scores(0)
    for n in range(count):
        s_next = scores(n + 1) if n + 1 < count else None
        finish(n, s)
        s = s_next


def to_lanes(column):
    r = lax.broadcasted_iota(jnp.int32, (HEAD, HEAD), 0)
    c = lax.broadcasted_iota(jnp.int32, (HEAD, HEAD), 1)
    return jnp.sum(jnp.where(r == c, column, 0.0), axis=0, keepdims=True)


def prep_kernel(q_hbm, k_hbm, v_hbm, q_ref, k_ref, values_ref, v_buf, sems):
    rows = pl.ds(pl.multiple_of(HALF * lax.axis_index("c"), HALF), HALF)
    copies = [
        pltpu.make_async_copy(v_hbm, v_buf, sems.at[0]),
        pltpu.make_async_copy(k_hbm, k_ref, sems.at[1]),
        pltpu.make_async_copy(q_hbm.at[rows, :], q_ref, sems.at[2]),
    ]
    for copy in copies:
        copy.start()
    values_ref[:, HEAD : 2 * HEAD] = jnp.ones((BLOCK, HEAD), BF)
    for copy in copies:
        copy.wait()
    values_ref[:, 0:HEAD] = v_buf[...]


def query_kernel(q_ref, k_ref, values_ref, kp_ref, vp_ref, out_ref, values_p):
    core = lax.axis_index("c")
    values_p[:, 0:HEAD] = vp_ref[...]
    values_p[:, HEAD : 2 * HEAD] = jnp.ones((BLOCK, HEAD), BF)
    row_id = lax.broadcasted_iota(jnp.int32, (16, HEAD), 0)

    def scores(j):
        q = q_ref[:, HEAD * j : HEAD * j + HEAD]
        return scores_of(q, k_ref[...]), scores_of(q, kp_ref[...])

    def finish(j, s):
        peak = jnp.maximum(
            jnp.max(s[0], axis=1, keepdims=True), jnp.max(s[1], axis=1, keepdims=True)
        )
        peak = peak.astype(BF).astype(F32)
        acc = jnp.dot(
            jnp.exp2(s[0] - peak).astype(BF), values_ref[...], preferred_element_type=F32
        ) + jnp.dot(jnp.exp2(s[1] - peak).astype(BF), values_p[...], preferred_element_type=F32)
        total = acc[:, HEAD : HEAD + 1]
        for half in range(2):
            rows = slice(half * HEAD, half * HEAD + HEAD)
            out_ref[2 * j + half, 0:HEAD, :] = acc[rows, 0:HEAD].astype(BF)
            peak_l = to_lanes(peak[rows])
            total_l = to_lanes(total[rows])
            high = total_l.astype(BF).astype(F32)
            stats = jnp.where(row_id == 0, peak_l, 0.0)
            stats = jnp.where(row_id == 1, high, stats)
            stats = jnp.where(row_id == 2, total_l - high, stats)
            out_ref[2 * j + half, HEAD:STATS, :] = stats.astype(BF)
            at = (2 * j + half) * ANCHOR_ROWS
            out_ref[2 * j + half, STATS:SEND1, :] = jnp.where(
                core == 0, k_ref[at : at + ANCHOR_ROWS, :], vp_ref[at : at + ANCHOR_ROWS, :]
            )

    pipelined(HEADS, scores, finish)


def combine_kernel(in_ref, after_ref, out_ref):
    stats = in_ref[:, HEAD:STATS, :].astype(F32)
    peak = stats[:, 0, :]
    total = stats[:, 1, :] + stats[:, 2, :]
    top = jnp.max(peak, axis=0, keepdims=True)
    weight = jnp.exp2(peak - top)
    weight = weight / jnp.sum(weight * total, axis=0, keepdims=True)
    weight_t = jnp.concatenate([weight, jnp.zeros((HEAD - 16, HEAD), F32)], axis=0).T
    out = jnp.zeros((HEAD, HEAD), F32)
    for g in range(16):
        out = out + weight_t[:, g : g + 1] * in_ref[g, 0:HEAD, :].astype(F32)
    out = out.astype(BF)
    anchor = in_ref[0, STATS:SEND1, :]
    for g in range(16):
        out_ref[g, 0:HEAD, :] = out
        out_ref[g, HEAD:SEND2, :] = anchor


def project_kernel(mine_ref, other_ref, w_ref, out_ref, k_hbm, v_hbm, k_ref, v_ref, sems):
    core = lax.axis_index("c")
    for g in range(16):
        rows = slice(g * ANCHOR_ROWS, (g + 1) * ANCHOR_ROWS)
        one, two = mine_ref[g, HEAD:SEND2, :], other_ref[g, HEAD:SEND2, :]
        k_ref[rows, :] = jnp.where(core == 0, one, two)
        v_ref[rows, :] = jnp.where(core == 0, two, one)
    copies = (
        pltpu.make_async_copy(k_ref, k_hbm, sems.at[0]),
        pltpu.make_async_copy(v_ref, v_hbm, sems.at[1]),
    )
    for copy in copies:
        copy.start()
    for ref, owner in ((mine_ref, core), (other_ref, 1 - core)):
        a = jnp.concatenate(
            [
                jnp.concatenate([ref[2 * j + half, 0:HEAD, :] for j in range(HEADS)], axis=1)
                for half in range(2)
            ],
            axis=0,
        )
        y = jnp.dot(a, w_ref[...], preferred_element_type=F32).astype(BF)
        for z in range(4):
            out_ref[4 * owner + z] = y[64 * z : 64 * z + 64, :]
    for copy in copies:
        copy.wait()


def final_kernel(in_ref, out_ref):
    total = in_ref[0].astype(F32)
    for z in range(1, 8):
        total = total + in_ref[z].astype(F32)
    out_ref[...] = total.astype(BF)


STEP = 2
STEP_COLUMNS = STEP * HEAD


def fill_values(v_ref, values_ref):
    @pl.when(pl.program_id(0) == 0)
    def _():
        values_ref[:, 0:HEAD] = v_ref[...]
        values_ref[:, HEAD : 2 * HEAD] = jnp.ones((BLOCK, HEAD), BF)


def own_kernel(q_ref, k_ref, v_ref, after_ref, x_ref, y_ref, z_ref, out_ref, lse_ref, values_ref):
    fill_values(v_ref, values_ref)

    @pl.when(pl.program_id(0) == 0)
    def _():
        lse_ref[...] = jnp.zeros((BLOCK, HEAD), F32)

    lane = lax.broadcasted_iota(jnp.int32, (HALF, HEAD), 1)
    r = lax.broadcasted_iota(jnp.int32, (HALF, HALF), 0)
    c = lax.broadcasted_iota(jnp.int32, (HALF, HALF), 1)

    def scores(h):
        return [
            scores_of(q_ref[i * HALF : (i + 1) * HALF, HEAD * h : HEAD * h + HEAD], k_ref[0 : (i + 1) * HALF, :])
            for i in range(3)
        ]

    def finish(h, s):
        head = pl.program_id(0) * STEP + h
        parts, peaks = [], []
        for i in range(3):
            diagonal = jnp.where(c <= r, s[i][:, i * HALF :], -HIDDEN)
            part = jnp.concatenate([s[i][:, 0 : i * HALF], diagonal], axis=1) if i else diagonal
            parts.append(part)
            peaks.append(jnp.max(part, axis=1, keepdims=True))
        for i in range(3):
            rows = slice(i * HALF, (i + 1) * HALF)
            p = jnp.exp2(parts[i] - peaks[i]).astype(BF)
            acc = jnp.dot(p, values_ref[0 : (i + 1) * HALF, :], preferred_element_type=F32)
            total = acc[:, HEAD : 2 * HEAD]
            out_ref[rows, HEAD * h : HEAD * h + HEAD] = (acc[:, 0:HEAD] / total).astype(BF)
            lse_ref[rows, :] = jnp.where(lane == head, peaks[i] + jnp.log2(total), lse_ref[rows, :])

    pipelined(STEP, scores, finish)


def anchor_kernel(q_ref, k_ref, v_ref, own_ref, lse_ref, out_ref, values_ref):
    fill_values(v_ref, values_ref)
    first = jnp.logical_and(
        lax.axis_index("c") == 0,
        jnp.logical_and(lax.axis_index("x") == 0, lax.axis_index("y") == 0),
    )
    lane = lax.broadcasted_iota(jnp.int32, (BLOCK, HEAD), 1)

    def scores(h):
        return scores_of(q_ref[:, HEAD * h : HEAD * h + HEAD], k_ref[...])

    def finish(h, s):
        head = pl.program_id(0) * STEP + h
        lse = jnp.sum(jnp.where(lane == head, lse_ref[...], 0.0), axis=1, keepdims=True)
        peak = jnp.maximum(lse, jnp.max(s, axis=1, keepdims=True))
        peak = jnp.where(first, lse, peak)
        p = jnp.exp2(s - jnp.where(first, HIDDEN, peak)).astype(BF)
        acc = jnp.dot(p, values_ref[...], preferred_element_type=F32)
        weight = jnp.exp2(lse - peak)
        mixture = acc[:, 0:HEAD] + weight * own_ref[:, HEAD * h : HEAD * h + HEAD].astype(F32)
        out_ref[:, HEAD * h : HEAD * h + HEAD] = (mixture / (acc[:, HEAD : 2 * HEAD] + weight)).astype(BF)

    pipelined(STEP, scores, finish)


VMEM = pl.BlockSpec(memory_space=pltpu.VMEM)
HBM = pl.BlockSpec(memory_space=pltpu.HBM)
ANY = pl.BlockSpec(memory_space=pl.ANY)
WIDE = HEADS * HEAD
STEP_BLOCK = pl.BlockSpec((BLOCK, STEP_COLUMNS), lambda t: (0, t))
HEAD_BLOCK = pl.BlockSpec((BLOCK, HEAD), lambda t: (0, 0))


def in_hbm(*arrays):
    return [pltpu.with_memory_space_constraint(a, pltpu.HBM) for a in arrays]


def shape(dims, dtype=BF):
    return jax.ShapeDtypeStruct(dims, dtype)


def buffer(dims, dtype=BF):
    return pltpu.VMEM(dims, dtype)


def run(kernel, name, operands, in_specs, out_shape, out_specs, scratch, flops, nbytes, exps=0, grid=()):
    return pl.pallas_call(
        kernel,
        grid=grid,
        in_specs=in_specs,
        out_specs=out_specs,
        out_shape=out_shape,
        scratch_shapes=scratch,
        compiler_params=pltpu.CompilerParams(vmem_limit_bytes=24 * 1024 * 1024),
        cost_estimate=pl.CostEstimate(flops=flops, bytes_accessed=nbytes, transcendentals=exps),
        name=name,
    )(*operands)


def prep_call(query, k, v):
    return run(
        prep_kernel, "prep", in_hbm(query, k, v), [HBM] * 3,
        (shape((HALF, WIDE)), shape((BLOCK, HEAD)), shape((BLOCK, 2 * HEAD))), (VMEM,) * 3,
        [buffer((BLOCK, HEAD)), pltpu.SemaphoreType.DMA((3,))], 1 << 18, 2 << 20,
    )


def query_call(q, k, values, kp, vp):
    return run(
        query_kernel, "query_attention", (q, k, values, kp, vp), [VMEM] * 5,
        shape((16, SEND1, HEAD)), VMEM, [buffer((BLOCK, 2 * HEAD))],
        4 * 2048 * 1536 * 256, 3 << 20, 2048 * 1536,
    )


def own_call(ctx_query, k, v, after, greetings):
    return run(
        own_kernel, "context_own", (*in_hbm(ctx_query, k, v), after, *greetings),
        [STEP_BLOCK, HEAD_BLOCK, HEAD_BLOCK] + [ANY] * 4,
        (pltpu.HBM((BLOCK, WIDE), BF), pltpu.HBM((BLOCK, HEAD), F32)), (STEP_BLOCK, HEAD_BLOCK),
        [buffer((BLOCK, 2 * HEAD))], 4 * 6144 * 512 * 256, 4 << 20, 6144 * 512, grid=(HEADS // STEP,),
    )


def anchor_call(ctx_query, k, v, own, lse):
    return run(
        anchor_kernel, "context_anchor", in_hbm(ctx_query, k, v, own, lse),
        [STEP_BLOCK, HEAD_BLOCK, HEAD_BLOCK, STEP_BLOCK, HEAD_BLOCK],
        shape((BLOCK, WIDE)), STEP_BLOCK,
        [buffer((BLOCK, 2 * HEAD))], 4 * 6144 * 768 * 256, 6 << 20, 6144 * 768, grid=(HEADS // STEP,),
    )


def combine_call(received, after):
    return run(
        combine_kernel, "combine", (received, *in_hbm(after)), [VMEM, HBM],
        shape((16, SEND2, HEAD)), VMEM, [], 1 << 20, 3 << 19,
    )


def project_call(mine, other, w):
    return run(
        project_kernel, "project", (mine, other, w), [VMEM] * 3,
        (shape((8, 64, 256)), pltpu.HBM((BLOCK, HEAD), BF), pltpu.HBM((BLOCK, HEAD), BF)), (VMEM, HBM, HBM),
        [buffer((BLOCK, HEAD)), buffer((BLOCK, HEAD)), pltpu.SemaphoreType.DMA((2,))],
        2 * 512 * 1024 * 256, 2 << 20,
    )


def final_call(received):
    return run(final_kernel, "final_sum", (received,), [VMEM], shape((64, 256)), VMEM, [], 1 << 17, 1 << 18)


def swap(value):
    return lax.ppermute(value, "c", [(0, 1), (1, 0)])


def greet(value, axis, size):
    return lax.ppermute(value, axis, [(i, (i + 1) % size) for i in range(size)])


def exchange(value, axes):
    return lax.all_to_all(value, axes, 0, 0, tiled=True)


def per_device(ctx_query, context_key, context_value, query, out_weight):
    key_p, value_p = swap(context_key), swap(context_value)
    few = context_key[0:16]
    greetings = [greet(few, axis, size) for axis, size in (("x", 4), ("y", 4), ("z", 8))]
    q, k, values = prep_call(query, context_key, context_value)
    sent = query_call(q, k, values, key_p, value_p)
    received = exchange(sent, ("y", "x"))
    own, lse = own_call(ctx_query, context_key, context_value, sent, greetings)
    gathered = exchange(combine_call(received, lse), ("y", "x"))
    shares, key_a, value_a = project_call(gathered, swap(gathered), out_weight)
    ctx_out = anchor_call(ctx_query, key_a, value_a, own, lse)
    answer = final_call(exchange(shares, "z"))
    return ctx_out, answer


def solution(mesh):
    fine = Mesh(mesh.devices.reshape(4, 4, 2, 8), ("y", "x", "c", "z"))
    hst = ("y", "x", "c")
    in_specs = (P(hst, "z"), P(hst, "z"), P(hst, "z"), P(None, "z"), P("z", hst))
    out_specs = (P(hst, "z"), P("z", hst))
    return jax.shard_map(
        per_device, mesh=fine, in_specs=in_specs, out_specs=out_specs, check_vma=False
    )
```

```python
import functools

import jax
import jax.numpy as jnp
from jax import lax
from jax.experimental import pallas as pl
from jax.experimental.pallas import tpu as pltpu
from jax.sharding import Mesh, PartitionSpec as P

HEAD = 128
BLOCK = 768
HEADS = 8
HALF = 256
STATS = HEAD + 16
ANCHOR_ROWS = 48
SEND1 = STATS + ANCHOR_ROWS
SEND2 = HEAD + ANCHOR_ROWS
HIDDEN = 1e30
LOG2_SCALE = 1.4426950408889634 * HEAD ** (-0.5)
BF = jnp.bfloat16
F32 = jnp.float32


def scores_of(q, k):
    return lax.dot_general(q, k, (((1,), (1,)), ((), ())), preferred_element_type=F32) * LOG2_SCALE


def pipelined(count, scores, finish):
    s = scores(0)
    for n in range(count):
        s_next = scores(n + 1) if n + 1 < count else None
        finish(n, s)
        s = s_next


def to_lanes(column):
    r = lax.broadcasted_iota(jnp.int32, (HEAD, HEAD), 0)
    c = lax.broadcasted_iota(jnp.int32, (HEAD, HEAD), 1)
    return jnp.sum(jnp.where(r == c, column, 0.0), axis=0, keepdims=True)


def prep_kernel(q_hbm, k_hbm, v_hbm, q_ref, k_ref, values_ref, v_buf, sems):
    rows = pl.ds(pl.multiple_of(HALF * lax.axis_index("c"), HALF), HALF)
    copies = [
        pltpu.make_async_copy(v_hbm, v_buf, sems.at[0]),
        pltpu.make_async_copy(k_hbm, k_ref, sems.at[1]),
        pltpu.make_async_copy(q_hbm.at[rows, :], q_ref, sems.at[2]),
    ]
    for copy in copies:
        copy.start()
    values_ref[:, HEAD : 2 * HEAD] = jnp.ones((BLOCK, HEAD), BF)
    for copy in copies:
        copy.wait()
    values_ref[:, 0:HEAD] = v_buf[...]


def query_kernel(q_ref, k_ref, values_ref, kp_ref, vp_ref, out_hbm, values_p, out_ref, sems):
    core = lax.axis_index("c")
    values_p[:, 0:HEAD] = vp_ref[...]
    values_p[:, HEAD : 2 * HEAD] = jnp.ones((BLOCK, HEAD), BF)
    row_id = lax.broadcasted_iota(jnp.int32, (16, HEAD), 0)

    def scores(j):
        q = q_ref[:, HEAD * j : HEAD * j + HEAD]
        return scores_of(q, k_ref[...]), scores_of(q, kp_ref[...])

    def finish(j, s):
        peak = jnp.maximum(
            jnp.max(s[0], axis=1, keepdims=True), jnp.max(s[1], axis=1, keepdims=True)
        )
        peak = peak.astype(BF).astype(F32)
        acc = jnp.dot(
            jnp.exp2(s[0] - peak).astype(BF), values_ref[...], preferred_element_type=F32
        ) + jnp.dot(jnp.exp2(s[1] - peak).astype(BF), values_p[...], preferred_element_type=F32)
        total = acc[:, HEAD : HEAD + 1]
        for half in range(2):
            rows = slice(half * HEAD, half * HEAD + HEAD)
            out_ref[2 * j + half, 0:HEAD, :] = acc[rows, 0:HEAD].astype(BF)
            peak_l = to_lanes(peak[rows])
            total_l = to_lanes(total[rows])
            high = total_l.astype(BF).astype(F32)
            stats = jnp.where(row_id == 0, peak_l, 0.0)
            stats = jnp.where(row_id == 1, high, stats)
            stats = jnp.where(row_id == 2, total_l - high, stats)
            out_ref[2 * j + half, HEAD:STATS, :] = stats.astype(BF)
            at = (2 * j + half) * ANCHOR_ROWS
            out_ref[2 * j + half, STATS:SEND1, :] = jnp.where(
                core == 0, k_ref[at : at + ANCHOR_ROWS, :], vp_ref[at : at + ANCHOR_ROWS, :]
            )

    def write(j):
        rows = slice(2 * j, 2 * j + 2)
        return pltpu.make_async_copy(out_ref.at[rows], out_hbm.at[rows], sems.at[j])

    def finish_and_write(j, s):
        finish(j, s)
        write(j).start()

    pipelined(HEADS, scores, finish_and_write)
    for j in range(HEADS):
        write(j).wait()


def combine_kernel(in_ref, after_ref, out_ref):
    stats = in_ref[:, HEAD:STATS, :].astype(F32)
    peak = stats[:, 0, :]
    total = stats[:, 1, :] + stats[:, 2, :]
    top = jnp.max(peak, axis=0, keepdims=True)
    weight = jnp.exp2(peak - top)
    weight = weight / jnp.sum(weight * total, axis=0, keepdims=True)
    weight_t = jnp.concatenate([weight, jnp.zeros((HEAD - 16, HEAD), F32)], axis=0).T
    out = jnp.zeros((HEAD, HEAD), F32)
    for g in range(16):
        out = out + weight_t[:, g : g + 1] * in_ref[g, 0:HEAD, :].astype(F32)
    out = out.astype(BF)
    anchor = in_ref[0, STATS:SEND1, :]
    for g in range(16):
        out_ref[g, 0:HEAD, :] = out
        out_ref[g, HEAD:SEND2, :] = anchor


def project_kernel(mine_ref, other_ref, w_ref, out_hbm, k_hbm, v_hbm, out_ref, k_ref, v_ref, sems):
    core = lax.axis_index("c")
    for g in range(16):
        rows = slice(g * ANCHOR_ROWS, (g + 1) * ANCHOR_ROWS)
        one, two = mine_ref[g, HEAD:SEND2, :], other_ref[g, HEAD:SEND2, :]
        k_ref[rows, :] = jnp.where(core == 0, one, two)
        v_ref[rows, :] = jnp.where(core == 0, two, one)
    copies = [
        pltpu.make_async_copy(k_ref, k_hbm, sems.at[0]),
        pltpu.make_async_copy(v_ref, v_hbm, sems.at[1]),
    ]
    for copy in copies:
        copy.start()
    for ref, owner in ((mine_ref, core), (other_ref, 1 - core)):
        a = jnp.concatenate(
            [
                jnp.concatenate([ref[2 * j + half, 0:HEAD, :] for j in range(HEADS)], axis=1)
                for half in range(2)
            ],
            axis=0,
        )
        y = jnp.dot(a, w_ref[...], preferred_element_type=F32).astype(BF)
        for z in range(4):
            out_ref[4 * owner + z] = y[64 * z : 64 * z + 64, :]
        half = pl.ds(4 * owner, 4)
        copies.append(pltpu.make_async_copy(out_ref.at[half], out_hbm.at[half], sems.at[len(copies)]))
        copies[-1].start()
    for copy in copies:
        copy.wait()


def final_kernel(in_ref, out_ref):
    total = in_ref[0].astype(F32)
    for z in range(1, 8):
        total = total + in_ref[z].astype(F32)
    out_ref[...] = total.astype(BF)


STEP = 2
STEP_COLUMNS = STEP * HEAD


def fill_values(v_ref, values_ref):
    @pl.when(pl.program_id(0) == 0)
    def _():
        values_ref[:, 0:HEAD] = v_ref[...]
        values_ref[:, HEAD : 2 * HEAD] = jnp.ones((BLOCK, HEAD), BF)


def own_kernel(q_ref, k_ref, v_ref, after_ref, out_ref, lse_ref, values_ref):
    fill_values(v_ref, values_ref)

    @pl.when(pl.program_id(0) == 0)
    def _():
        lse_ref[...] = jnp.zeros((BLOCK, HEAD), F32)

    lane = lax.broadcasted_iota(jnp.int32, (HALF, HEAD), 1)
    r = lax.broadcasted_iota(jnp.int32, (HALF, HALF), 0)
    c = lax.broadcasted_iota(jnp.int32, (HALF, HALF), 1)

    def scores(h):
        return [
            scores_of(q_ref[i * HALF : (i + 1) * HALF, HEAD * h : HEAD * h + HEAD], k_ref[0 : (i + 1) * HALF, :])
            for i in range(3)
        ]

    def finish(h, s):
        head = pl.program_id(0) * STEP + h
        parts, peaks = [], []
        for i in range(3):
            diagonal = jnp.where(c <= r, s[i][:, i * HALF :], -HIDDEN)
            part = jnp.concatenate([s[i][:, 0 : i * HALF], diagonal], axis=1) if i else diagonal
            parts.append(part)
            peaks.append(jnp.max(part, axis=1, keepdims=True))
        for i in range(3):
            rows = slice(i * HALF, (i + 1) * HALF)
            p = jnp.exp2(parts[i] - peaks[i]).astype(BF)
            acc = jnp.dot(p, values_ref[0 : (i + 1) * HALF, :], preferred_element_type=F32)
            total = acc[:, HEAD : 2 * HEAD]
            out_ref[rows, HEAD * h : HEAD * h + HEAD] = (acc[:, 0:HEAD] / total).astype(BF)
            lse_ref[rows, :] = jnp.where(lane == head, peaks[i] + jnp.log2(total), lse_ref[rows, :])

    pipelined(STEP, scores, finish)


def anchor_kernel(q_ref, k_ref, v_ref, own_ref, lse_ref, out_ref, values_ref, keys_ref):
    fill_values(v_ref, values_ref)

    @pl.when(pl.program_id(0) == 0)
    def _():
        k = k_ref[...].astype(F32) * LOG2_SCALE
        high = k.astype(BF)
        keys_ref[:, 0:HEAD] = high
        keys_ref[:, HEAD : 2 * HEAD] = (k - high.astype(F32)).astype(BF)

    first = jnp.logical_and(
        lax.axis_index("c") == 0,
        jnp.logical_and(lax.axis_index("x") == 0, lax.axis_index("y") == 0),
    )
    lane = lax.broadcasted_iota(jnp.int32, (BLOCK, HEAD), 1)

    def scores(h):
        q = q_ref[:, HEAD * h : HEAD * h + HEAD]
        return lax.dot_general(
            jnp.concatenate([q, q], axis=1), keys_ref[...], (((1,), (1,)), ((), ())), preferred_element_type=F32
        )

    def finish(h, s):
        head = pl.program_id(0) * STEP + h
        lse = jnp.sum(jnp.where(lane == head, lse_ref[...], 0.0), axis=1, keepdims=True)
        peak = jnp.maximum(lse, jnp.max(s, axis=1, keepdims=True))
        p = jnp.exp2(s - peak).astype(BF)
        acc = jnp.dot(p, values_ref[...], preferred_element_type=F32)
        weight = jnp.exp2(lse - peak)
        mixture = acc[:, 0:HEAD] + weight * own_ref[:, HEAD * h : HEAD * h + HEAD].astype(F32)
        out_ref[:, HEAD * h : HEAD * h + HEAD] = (mixture / (acc[:, HEAD : 2 * HEAD] + weight)).astype(BF)

    @pl.when(first)
    def _():
        out_ref[...] = own_ref[...]

    @pl.when(jnp.logical_not(first))
    def _():
        pipelined(STEP, scores, finish)


VMEM = pl.BlockSpec(memory_space=pltpu.VMEM)
HBM = pl.BlockSpec(memory_space=pltpu.HBM)
ANY = pl.BlockSpec(memory_space=pl.ANY)
WIDE = HEADS * HEAD
STEP_BLOCK = pl.BlockSpec((BLOCK, STEP_COLUMNS), lambda t: (0, t))
HEAD_BLOCK = pl.BlockSpec((BLOCK, HEAD), lambda t: (0, 0))


def in_hbm(*arrays):
    return [pltpu.with_memory_space_constraint(a, pltpu.HBM) for a in arrays]


def shape(dims, dtype=BF):
    return jax.ShapeDtypeStruct(dims, dtype)


def buffer(dims, dtype=BF):
    return pltpu.VMEM(dims, dtype)


def run(kernel, name, operands, in_specs, out_shape, out_specs, scratch, flops, nbytes, exps=0, grid=()):
    return pl.pallas_call(
        kernel,
        grid=grid,
        in_specs=in_specs,
        out_specs=out_specs,
        out_shape=out_shape,
        scratch_shapes=scratch,
        compiler_params=pltpu.CompilerParams(vmem_limit_bytes=24 * 1024 * 1024),
        cost_estimate=pl.CostEstimate(flops=flops, bytes_accessed=nbytes, transcendentals=exps),
        name=name,
    )(*operands)


def prep_call(query, k, v):
    return run(
        prep_kernel, "prep", in_hbm(query, k, v), [HBM] * 3,
        (shape((HALF, WIDE)), shape((BLOCK, HEAD)), shape((BLOCK, 2 * HEAD))), (VMEM,) * 3,
        [buffer((BLOCK, HEAD)), pltpu.SemaphoreType.DMA((3,))], 1 << 18, 2 << 20,
    )


def query_call(q, k, values, kp, vp):
    return run(
        query_kernel, "query_attention", (q, k, values, kp, vp), [VMEM] * 5,
        pltpu.HBM((16, SEND1, HEAD), BF), HBM,
        [buffer((BLOCK, 2 * HEAD)), buffer((16, SEND1, HEAD)), pltpu.SemaphoreType.DMA((HEADS,))],
        4 * 2048 * 1536 * 256, 3 << 20, 2048 * 1536,
    )


def own_call(ctx_query, k, v, after):
    return run(
        own_kernel, "context_own", (*in_hbm(ctx_query, k, v), after),
        [STEP_BLOCK, HEAD_BLOCK, HEAD_BLOCK, ANY],
        (pltpu.HBM((BLOCK, WIDE), BF), pltpu.HBM((BLOCK, HEAD), F32)), (STEP_BLOCK, HEAD_BLOCK),
        [buffer((BLOCK, 2 * HEAD))], 4 * 6144 * 512 * 256, 4 << 20, 6144 * 512, grid=(HEADS // STEP,),
    )


def anchor_call(ctx_query, k, v, own, lse):
    return run(
        anchor_kernel, "context_anchor", in_hbm(ctx_query, k, v, own, lse),
        [STEP_BLOCK, HEAD_BLOCK, HEAD_BLOCK, STEP_BLOCK, HEAD_BLOCK],
        shape((BLOCK, WIDE)), STEP_BLOCK,
        [buffer((BLOCK, 2 * HEAD))] * 2, 4 * 6144 * 768 * 256, 6 << 20, 6144 * 768, grid=(HEADS // STEP,),
    )


def combine_call(received, after):
    return run(
        combine_kernel, "combine", (received, *in_hbm(after)), [VMEM, HBM],
        shape((16, SEND2, HEAD)), VMEM, [], 1 << 20, 3 << 19,
    )


def project_call(mine, other, w):
    return run(
        project_kernel, "project", (mine, other, w), [VMEM] * 3,
        (pltpu.HBM((8, 64, 256), BF), pltpu.HBM((BLOCK, HEAD), BF), pltpu.HBM((BLOCK, HEAD), BF)), (HBM,) * 3,
        [buffer((8, 64, 256)), buffer((BLOCK, HEAD)), buffer((BLOCK, HEAD)), pltpu.SemaphoreType.DMA((4,))],
        2 * 512 * 1024 * 256, 2 << 20,
    )


def final_call(received):
    return run(final_kernel, "final_sum", (received,), [VMEM], shape((64, 256)), VMEM, [], 1 << 17, 1 << 18)


def swap(value):
    return lax.ppermute(value, "c", [(0, 1), (1, 0)])


def exchange(value, axes):
    return lax.all_to_all(value, axes, 0, 0, tiled=True)


def per_device(ctx_query, context_key, context_value, query, out_weight):
    key_p, value_p = swap(context_key), swap(context_value)
    q, k, values = prep_call(query, context_key, context_value)
    sent = query_call(q, k, values, key_p, value_p)
    received = exchange(sent, ("y", "x"))
    own, lse = own_call(ctx_query, context_key, context_value, sent)
    gathered = exchange(combine_call(received, lse), ("y", "x"))
    shares, key_a, value_a = project_call(gathered, swap(gathered), out_weight)
    ctx_out = anchor_call(ctx_query, key_a, value_a, own, lse)
    answer = final_call(exchange(shares, "z"))
    return ctx_out, answer


def solution(mesh):
    fine = Mesh(mesh.devices.reshape(4, 4, 2, 8), ("y", "x", "c", "z"))
    hst = ("y", "x", "c")
    in_specs = (P(hst, "z"), P(hst, "z"), P(hst, "z"), P(None, "z"), P("z", hst))
    out_specs = (P(hst, "z"), P("z", hst))
    return jax.shard_map(
        per_device, mesh=fine, in_specs=in_specs, out_specs=out_specs, check_vma=False
    )
```

```python
import functools

import jax
import jax.numpy as jnp
from jax import lax
from jax.experimental import pallas as pl
from jax.experimental.pallas import tpu as pltpu
from jax.sharding import Mesh, PartitionSpec as P

HEAD = 128
BLOCK = 768
HEADS = 8
HALF = 256
STATS = HEAD + 16
ANCHOR_ROWS = 48
SEND1 = STATS + ANCHOR_ROWS
SEND2 = HEAD + ANCHOR_ROWS
HIDDEN = 1e30
LOG2_SCALE = 1.4426950408889634 * HEAD ** (-0.5)
BF = jnp.bfloat16
F32 = jnp.float32


def scores_of(q, k):
    return lax.dot_general(q, k, (((1,), (1,)), ((), ())), preferred_element_type=F32) * LOG2_SCALE


def pipelined(count, scores, finish):
    s = scores(0)
    for n in range(count):
        s_next = scores(n + 1) if n + 1 < count else None
        finish(n, s)
        s = s_next


def to_lanes(column):
    r = lax.broadcasted_iota(jnp.int32, (HEAD, HEAD), 0)
    c = lax.broadcasted_iota(jnp.int32, (HEAD, HEAD), 1)
    return jnp.sum(jnp.where(r == c, column, 0.0), axis=0, keepdims=True)


def prep_kernel(q_hbm, k_hbm, v_hbm, q_ref, k_ref, values_ref, v_buf, sems):
    rows = pl.ds(pl.multiple_of(HALF * lax.axis_index("c"), HALF), HALF)
    copies = [
        pltpu.make_async_copy(v_hbm, v_buf, sems.at[0]),
        pltpu.make_async_copy(k_hbm, k_ref, sems.at[1]),
        pltpu.make_async_copy(q_hbm.at[rows, :], q_ref, sems.at[2]),
    ]
    for copy in copies:
        copy.start()
    values_ref[:, HEAD : 2 * HEAD] = jnp.ones((BLOCK, HEAD), BF)
    for copy in copies:
        copy.wait()
    values_ref[:, 0:HEAD] = v_buf[...]


def query_kernel(q_ref, k_ref, values_ref, kp_ref, vp_ref, out_hbm, values_p, out_ref, sems):
    core = lax.axis_index("c")
    values_p[:, 0:HEAD] = vp_ref[...]
    values_p[:, HEAD : 2 * HEAD] = jnp.ones((BLOCK, HEAD), BF)
    row_id = lax.broadcasted_iota(jnp.int32, (16, HEAD), 0)

    def scores(j):
        q = q_ref[:, HEAD * j : HEAD * j + HEAD]
        return scores_of(q, k_ref[...]), scores_of(q, kp_ref[...])

    def finish(j, s):
        peak = jnp.maximum(
            jnp.max(s[0], axis=1, keepdims=True), jnp.max(s[1], axis=1, keepdims=True)
        )
        peak = peak.astype(BF).astype(F32)
        acc = jnp.dot(
            jnp.exp2(s[0] - peak).astype(BF), values_ref[...], preferred_element_type=F32
        ) + jnp.dot(jnp.exp2(s[1] - peak).astype(BF), values_p[...], preferred_element_type=F32)
        total = acc[:, HEAD : HEAD + 1]
        for half in range(2):
            rows = slice(half * HEAD, half * HEAD + HEAD)
            out_ref[2 * j + half, 0:HEAD, :] = acc[rows, 0:HEAD].astype(BF)
            peak_l = to_lanes(peak[rows])
            total_l = to_lanes(total[rows])
            high = total_l.astype(BF).astype(F32)
            stats = jnp.where(row_id == 0, peak_l, 0.0)
            stats = jnp.where(row_id == 1, high, stats)
            stats = jnp.where(row_id == 2, total_l - high, stats)
            out_ref[2 * j + half, HEAD:STATS, :] = stats.astype(BF)
            at = (2 * j + half) * ANCHOR_ROWS
            out_ref[2 * j + half, STATS:SEND1, :] = jnp.where(
                core == 0, k_ref[at : at + ANCHOR_ROWS, :], vp_ref[at : at + ANCHOR_ROWS, :]
            )

    def write(j):
        rows = slice(2 * j, 2 * j + 2)
        return pltpu.make_async_copy(out_ref.at[rows], out_hbm.at[rows], sems.at[j])

    def finish_and_write(j, s):
        finish(j, s)
        write(j).start()

    pipelined(HEADS, scores, finish_and_write)
    for j in range(HEADS):
        write(j).wait()


def combine_kernel(in_ref, after_ref, out_ref):
    stats = in_ref[:, HEAD:STATS, :].astype(F32)
    peak = stats[:, 0, :]
    total = stats[:, 1, :] + stats[:, 2, :]
    top = jnp.max(peak, axis=0, keepdims=True)
    weight = jnp.exp2(peak - top)
    weight = weight / jnp.sum(weight * total, axis=0, keepdims=True)
    weight_t = jnp.concatenate([weight, jnp.zeros((HEAD - 16, HEAD), F32)], axis=0).T
    out = jnp.zeros((HEAD, HEAD), F32)
    for g in range(16):
        out = out + weight_t[:, g : g + 1] * in_ref[g, 0:HEAD, :].astype(F32)
    out = out.astype(BF)
    anchor = in_ref[0, STATS:SEND1, :]
    for g in range(16):
        out_ref[g, 0:HEAD, :] = out
        out_ref[g, HEAD:SEND2, :] = anchor


def project_kernel(mine_ref, other_ref, w_ref, out_hbm, k_hbm, v_hbm, out_ref, k_ref, v_ref, sems):
    core = lax.axis_index("c")
    for g in range(16):
        rows = slice(g * ANCHOR_ROWS, (g + 1) * ANCHOR_ROWS)
        one, two = mine_ref[g, HEAD:SEND2, :], other_ref[g, HEAD:SEND2, :]
        k_ref[rows, :] = jnp.where(core == 0, one, two)
        v_ref[rows, :] = jnp.where(core == 0, two, one)
    copies = [
        pltpu.make_async_copy(k_ref, k_hbm, sems.at[0]),
        pltpu.make_async_copy(v_ref, v_hbm, sems.at[1]),
    ]
    for copy in copies:
        copy.start()
    for ref, owner in ((mine_ref, core), (other_ref, 1 - core)):
        a = jnp.concatenate(
            [
                jnp.concatenate([ref[2 * j + half, 0:HEAD, :] for j in range(HEADS)], axis=1)
                for half in range(2)
            ],
            axis=0,
        )
        y = jnp.dot(a, w_ref[...], preferred_element_type=F32).astype(BF)
        for z in range(4):
            out_ref[4 * owner + z] = y[64 * z : 64 * z + 64, :]
        half = pl.ds(4 * owner, 4)
        copies.append(pltpu.make_async_copy(out_ref.at[half], out_hbm.at[half], sems.at[len(copies)]))
        copies[-1].start()
    for copy in copies:
        copy.wait()


def final_kernel(in_ref, out_ref):
    total = in_ref[0].astype(F32)
    for z in range(1, 8):
        total = total + in_ref[z].astype(F32)
    out_ref[...] = total.astype(BF)


STEP = 2
STEP_COLUMNS = STEP * HEAD


def fill_values(v_ref, values_ref):
    @pl.when(pl.program_id(0) == 0)
    def _():
        values_ref[:, 0:HEAD] = v_ref[...]
        values_ref[:, HEAD : 2 * HEAD] = jnp.ones((BLOCK, HEAD), BF)


def own_kernel(q_ref, k_ref, v_ref, after_ref, out_ref, lse_ref, values_ref):
    fill_values(v_ref, values_ref)

    @pl.when(pl.program_id(0) == 0)
    def _():
        lse_ref[...] = jnp.zeros((BLOCK, HEAD), F32)

    lane = lax.broadcasted_iota(jnp.int32, (HALF, HEAD), 1)
    r = lax.broadcasted_iota(jnp.int32, (HALF, HALF), 0)
    c = lax.broadcasted_iota(jnp.int32, (HALF, HALF), 1)

    def scores(h):
        return [
            scores_of(q_ref[i * HALF : (i + 1) * HALF, HEAD * h : HEAD * h + HEAD], k_ref[0 : (i + 1) * HALF, :])
            for i in range(3)
        ]

    def finish(h, s):
        head = pl.program_id(0) * STEP + h
        parts, peaks = [], []
        for i in range(3):
            diagonal = jnp.where(c <= r, s[i][:, i * HALF :], -HIDDEN)
            part = jnp.concatenate([s[i][:, 0 : i * HALF], diagonal], axis=1) if i else diagonal
            parts.append(part)
            peaks.append(jnp.max(part, axis=1, keepdims=True))
        for i in range(3):
            rows = slice(i * HALF, (i + 1) * HALF)
            p = jnp.exp2(parts[i] - peaks[i]).astype(BF)
            acc = jnp.dot(p, values_ref[0 : (i + 1) * HALF, :], preferred_element_type=F32)
            total = acc[:, HEAD : 2 * HEAD]
            out_ref[rows, HEAD * h : HEAD * h + HEAD] = (acc[:, 0:HEAD] / total).astype(BF)
            lse_ref[rows, :] = jnp.where(lane == head, peaks[i] + jnp.log2(total), lse_ref[rows, :])

    pipelined(STEP, scores, finish)


def anchor_kernel(q_ref, k_ref, v_ref, own_ref, lse_ref, out_ref, values_ref, keys_ref):
    fill_values(v_ref, values_ref)

    @pl.when(pl.program_id(0) == 0)
    def _():
        k = k_ref[...].astype(F32) * LOG2_SCALE
        high = k.astype(BF)
        keys_ref[:, 0:HEAD] = high
        keys_ref[:, HEAD : 2 * HEAD] = (k - high.astype(F32)).astype(BF)

    first = jnp.logical_and(
        lax.axis_index("c") == 0,
        jnp.logical_and(lax.axis_index("x") == 0, lax.axis_index("y") == 0),
    )
    lane = lax.broadcasted_iota(jnp.int32, (BLOCK, HEAD), 1)

    def scores(h):
        q = q_ref[:, HEAD * h : HEAD * h + HEAD]
        return lax.dot_general(
            jnp.concatenate([q, q], axis=1), keys_ref[...], (((1,), (1,)), ((), ())), preferred_element_type=F32
        )

    def finish(h, s):
        head = pl.program_id(0) * STEP + h
        lse = jnp.sum(jnp.where(lane == head, lse_ref[...], 0.0), axis=1, keepdims=True)
        peak = jnp.maximum(lse, jnp.max(s, axis=1, keepdims=True))
        p = jnp.exp2(s - peak).astype(BF)
        acc = jnp.dot(p, values_ref[...], preferred_element_type=F32)
        weight = jnp.exp2(lse - peak)
        mixture = acc[:, 0:HEAD] + weight * own_ref[:, HEAD * h : HEAD * h + HEAD].astype(F32)
        out_ref[:, HEAD * h : HEAD * h + HEAD] = (mixture / (acc[:, HEAD : 2 * HEAD] + weight)).astype(BF)

    @pl.when(first)
    def _():
        out_ref[...] = own_ref[...]

    @pl.when(jnp.logical_not(first))
    def _():
        pipelined(STEP, scores, finish)


VMEM = pl.BlockSpec(memory_space=pltpu.VMEM)
HBM = pl.BlockSpec(memory_space=pltpu.HBM)
WIDE = HEADS * HEAD
STEP_BLOCK = pl.BlockSpec((BLOCK, STEP_COLUMNS), lambda t: (0, t))
HEAD_BLOCK = pl.BlockSpec((BLOCK, HEAD), lambda t: (0, 0))


def in_hbm(*arrays):
    return [pltpu.with_memory_space_constraint(a, pltpu.HBM) for a in arrays]


def shape(dims, dtype=BF):
    return jax.ShapeDtypeStruct(dims, dtype)


def buffer(dims, dtype=BF):
    return pltpu.VMEM(dims, dtype)


def run(kernel, name, operands, in_specs, out_shape, out_specs, scratch, flops, nbytes, exps=0, grid=()):
    return pl.pallas_call(
        kernel,
        grid=grid,
        in_specs=in_specs,
        out_specs=out_specs,
        out_shape=out_shape,
        scratch_shapes=scratch,
        compiler_params=pltpu.CompilerParams(vmem_limit_bytes=24 * 1024 * 1024),
        cost_estimate=pl.CostEstimate(flops=flops, bytes_accessed=nbytes, transcendentals=exps),
        name=name,
    )(*operands)


def prep_call(query, k, v):
    return run(
        prep_kernel, "prep", in_hbm(query, k, v), [HBM] * 3,
        (shape((HALF, WIDE)), shape((BLOCK, HEAD)), shape((BLOCK, 2 * HEAD))), (VMEM,) * 3,
        [buffer((BLOCK, HEAD)), pltpu.SemaphoreType.DMA((3,))], 1 << 18, 2 << 20,
    )


def query_call(q, k, values, kp, vp):
    return run(
        query_kernel, "query_attention", (q, k, values, kp, vp), [VMEM] * 5,
        pltpu.HBM((16, SEND1, HEAD), BF), HBM,
        [buffer((BLOCK, 2 * HEAD)), buffer((16, SEND1, HEAD)), pltpu.SemaphoreType.DMA((HEADS,))],
        4 * 2048 * 1536 * 256, 3 << 20, 2048 * 1536,
    )


def own_call(ctx_query, k, v, after):
    return run(
        own_kernel, "context_own", in_hbm(ctx_query, k, v, after),
        [STEP_BLOCK, HEAD_BLOCK, HEAD_BLOCK, HBM],
        (pltpu.HBM((BLOCK, WIDE), BF), pltpu.HBM((BLOCK, HEAD), F32)), (STEP_BLOCK, HEAD_BLOCK),
        [buffer((BLOCK, 2 * HEAD))], 4 * 6144 * 512 * 256, 4 << 20, 6144 * 512, grid=(HEADS // STEP,),
    )


def anchor_call(ctx_query, k, v, own, lse):
    return run(
        anchor_kernel, "context_anchor", in_hbm(ctx_query, k, v, own, lse),
        [STEP_BLOCK, HEAD_BLOCK, HEAD_BLOCK, STEP_BLOCK, HEAD_BLOCK],
        shape((BLOCK, WIDE)), STEP_BLOCK,
        [buffer((BLOCK, 2 * HEAD))] * 2, 4 * 6144 * 768 * 256, 6 << 20, 6144 * 768, grid=(HEADS // STEP,),
    )


def combine_call(received, after):
    return run(
        combine_kernel, "combine", (received, *in_hbm(after)), [VMEM, HBM],
        shape((16, SEND2, HEAD)), VMEM, [], 1 << 20, 3 << 19,
    )


def project_call(mine, other, w):
    return run(
        project_kernel, "project", (mine, other, w), [VMEM] * 3,
        (pltpu.HBM((8, 64, 256), BF), pltpu.HBM((BLOCK, HEAD), BF), pltpu.HBM((BLOCK, HEAD), BF)), (HBM,) * 3,
        [buffer((8, 64, 256)), buffer((BLOCK, HEAD)), buffer((BLOCK, HEAD)), pltpu.SemaphoreType.DMA((4,))],
        2 * 512 * 1024 * 256, 2 << 20,
    )


def final_call(received):
    return run(final_kernel, "final_sum", (received,), [VMEM], shape((64, 256)), VMEM, [], 1 << 17, 1 << 18)


def swap(value):
    return lax.ppermute(value, "c", [(0, 1), (1, 0)])


def exchange(value, axes):
    return lax.all_to_all(value, axes, 0, 0, tiled=True)


def per_device(ctx_query, context_key, context_value, query, out_weight):
    key_p, value_p = swap(context_key), swap(context_value)
    q, k, values = prep_call(query, context_key, context_value)
    sent = query_call(q, k, values, key_p, value_p)
    received = exchange(sent, ("x", "y"))
    own, lse = own_call(ctx_query, context_key, context_value, sent)
    gathered = exchange(combine_call(received, lse), ("x", "y"))
    shares, key_a, value_a = project_call(gathered, swap(gathered), out_weight)
    ctx_out = anchor_call(ctx_query, key_a, value_a, own, lse)
    answer = final_call(exchange(shares, "z"))
    return ctx_out, answer


def solution(mesh):
    fine = Mesh(mesh.devices.reshape(4, 4, 2, 8), ("y", "x", "c", "z"))
    hst = ("y", "x", "c")
    in_specs = (P(hst, "z"), P(hst, "z"), P(hst, "z"), P(None, "z"), P("z", hst))
    out_specs = (P(hst, "z"), P("z", hst))
    return jax.shard_map(
        per_device, mesh=fine, in_specs=in_specs, out_specs=out_specs, check_vma=False
    )
```

```python
import functools

import jax
import jax.numpy as jnp
from jax import lax
from jax.experimental import pallas as pl
from jax.experimental.pallas import tpu as pltpu
from jax.sharding import Mesh, PartitionSpec as P

HEAD = 128
BLOCK = 768
HEADS = 8
HALF = 256
STATS = HEAD + 16
ANCHOR_ROWS = 48
SEND1 = STATS + ANCHOR_ROWS
SEND2 = HEAD + ANCHOR_ROWS
HIDDEN = 1e30
LOG2_SCALE = 1.4426950408889634 * HEAD ** (-0.5)
BF = jnp.bfloat16
F32 = jnp.float32


def scores_of(q, k):
    return lax.dot_general(q, k, (((1,), (1,)), ((), ())), preferred_element_type=F32) * LOG2_SCALE


def pipelined(count, scores, finish):
    s = scores(0)
    for n in range(count):
        s_next = scores(n + 1) if n + 1 < count else None
        finish(n, s)
        s = s_next


def to_lanes(column):
    r = lax.broadcasted_iota(jnp.int32, (HEAD, HEAD), 0)
    c = lax.broadcasted_iota(jnp.int32, (HEAD, HEAD), 1)
    return jnp.sum(jnp.where(r == c, column, 0.0), axis=0, keepdims=True)


def prep_kernel(q_hbm, k_hbm, v_hbm, q_ref, k_ref, values_ref, v_buf, sems):
    rows = pl.ds(pl.multiple_of(HALF * lax.axis_index("c"), HALF), HALF)
    copies = [
        pltpu.make_async_copy(v_hbm, v_buf, sems.at[0]),
        pltpu.make_async_copy(k_hbm, k_ref, sems.at[1]),
        pltpu.make_async_copy(q_hbm.at[rows, :], q_ref, sems.at[2]),
    ]
    for copy in copies:
        copy.start()
    values_ref[:, HEAD : 2 * HEAD] = jnp.ones((BLOCK, HEAD), BF)
    for copy in copies:
        copy.wait()
    values_ref[:, 0:HEAD] = v_buf[...]


def query_kernel(q_ref, k_ref, values_ref, kp_ref, vp_ref, out_hbm, values_p, out_ref, sems):
    core = lax.axis_index("c")
    values_p[:, 0:HEAD] = vp_ref[...]
    values_p[:, HEAD : 2 * HEAD] = jnp.ones((BLOCK, HEAD), BF)
    row_id = lax.broadcasted_iota(jnp.int32, (16, HEAD), 0)

    def scores(j):
        q = q_ref[:, HEAD * j : HEAD * j + HEAD]
        return scores_of(q, k_ref[...]), scores_of(q, kp_ref[...])

    def finish(j, s):
        peak = jnp.maximum(
            jnp.max(s[0], axis=1, keepdims=True), jnp.max(s[1], axis=1, keepdims=True)
        )
        peak = peak.astype(BF).astype(F32)
        acc = jnp.dot(
            jnp.exp2(s[0] - peak).astype(BF), values_ref[...], preferred_element_type=F32
        ) + jnp.dot(jnp.exp2(s[1] - peak).astype(BF), values_p[...], preferred_element_type=F32)
        total = acc[:, HEAD : HEAD + 1]
        for half in range(2):
            rows = slice(half * HEAD, half * HEAD + HEAD)
            out_ref[2 * j + half, 0:HEAD, :] = acc[rows, 0:HEAD].astype(BF)
            peak_l = to_lanes(peak[rows])
            total_l = to_lanes(total[rows])
            high = total_l.astype(BF).astype(F32)
            stats = jnp.where(row_id == 0, peak_l, 0.0)
            stats = jnp.where(row_id == 1, high, stats)
            stats = jnp.where(row_id == 2, total_l - high, stats)
            out_ref[2 * j + half, HEAD:STATS, :] = stats.astype(BF)
            at = (2 * j + half) * ANCHOR_ROWS
            out_ref[2 * j + half, STATS:SEND1, :] = jnp.where(
                core == 0, k_ref[at : at + ANCHOR_ROWS, :], vp_ref[at : at + ANCHOR_ROWS, :]
            )

    def write(j):
        rows = slice(2 * j, 2 * j + 2)
        return pltpu.make_async_copy(out_ref.at[rows], out_hbm.at[rows], sems.at[j])

    def finish_and_write(j, s):
        finish(j, s)
        write(j).start()

    pipelined(HEADS, scores, finish_and_write)
    for j in range(HEADS):
        write(j).wait()


def combine_kernel(in_ref, after_ref, out_ref):
    stats = in_ref[:, HEAD:STATS, :].astype(F32)
    peak = stats[:, 0, :]
    total = stats[:, 1, :] + stats[:, 2, :]
    top = jnp.max(peak, axis=0, keepdims=True)
    weight = jnp.exp2(peak - top)
    weight = weight / jnp.sum(weight * total, axis=0, keepdims=True)
    weight_t = jnp.concatenate([weight, jnp.zeros((HEAD - 16, HEAD), F32)], axis=0).T
    out = jnp.zeros((HEAD, HEAD), F32)
    for g in range(16):
        out = out + weight_t[:, g : g + 1] * in_ref[g, 0:HEAD, :].astype(F32)
    out = out.astype(BF)
    anchor = in_ref[0, STATS:SEND1, :]
    for g in range(16):
        out_ref[g, 0:HEAD, :] = out
        out_ref[g, HEAD:SEND2, :] = anchor


def project_rows(ref, w_ref, owner, out_hbm, out_ref, sem):
    a = jnp.concatenate(
        [
            jnp.concatenate([ref[2 * j + half, 0:HEAD, :] for j in range(HEADS)], axis=1)
            for half in range(2)
        ],
        axis=0,
    )
    y = jnp.dot(a, w_ref[...], preferred_element_type=F32).astype(BF)
    for z in range(4):
        out_ref[z] = y[64 * z : 64 * z + 64, :]
    copy = pltpu.make_async_copy(out_ref, out_hbm.at[pl.ds(4 * owner, 4)], sem)
    copy.start()
    return copy


def project_mine_kernel(mine_ref, w_ref, out_hbm, out_ref, sem):
    project_rows(mine_ref, w_ref, lax.axis_index("c"), out_hbm, out_ref, sem).wait()


def project_other_kernel(
    half_done_hbm, mine_ref, other_ref, w_ref, out_hbm, k_hbm, v_hbm, out_ref, k_ref, v_ref, sem, sems
):
    core = lax.axis_index("c")
    for g in range(16):
        rows = slice(g * ANCHOR_ROWS, (g + 1) * ANCHOR_ROWS)
        one, two = mine_ref[g, HEAD:SEND2, :], other_ref[g, HEAD:SEND2, :]
        k_ref[rows, :] = jnp.where(core == 0, one, two)
        v_ref[rows, :] = jnp.where(core == 0, two, one)
    copies = [
        pltpu.make_async_copy(k_ref, k_hbm, sems.at[0]),
        pltpu.make_async_copy(v_ref, v_hbm, sems.at[1]),
    ]
    for copy in copies:
        copy.start()
    copies.append(project_rows(other_ref, w_ref, 1 - core, out_hbm, out_ref, sem))
    for copy in copies:
        copy.wait()


STEP = 2
STEP_COLUMNS = STEP * HEAD


def fill_values(v_ref, values_ref):
    @pl.when(pl.program_id(0) == 0)
    def _():
        values_ref[:, 0:HEAD] = v_ref[...]
        values_ref[:, HEAD : 2 * HEAD] = jnp.ones((BLOCK, HEAD), BF)


def own_kernel(q_ref, k_ref, v_ref, after_ref, out_ref, lse_ref, values_ref):
    fill_values(v_ref, values_ref)

    @pl.when(pl.program_id(0) == 0)
    def _():
        lse_ref[...] = jnp.zeros((BLOCK, HEAD), F32)

    lane = lax.broadcasted_iota(jnp.int32, (HALF, HEAD), 1)
    r = lax.broadcasted_iota(jnp.int32, (HALF, HALF), 0)
    c = lax.broadcasted_iota(jnp.int32, (HALF, HALF), 1)

    def scores(h):
        return [
            scores_of(q_ref[i * HALF : (i + 1) * HALF, HEAD * h : HEAD * h + HEAD], k_ref[0 : (i + 1) * HALF, :])
            for i in range(3)
        ]

    def finish(h, s):
        head = pl.program_id(0) * STEP + h
        parts, peaks = [], []
        for i in range(3):
            diagonal = jnp.where(c <= r, s[i][:, i * HALF :], -HIDDEN)
            part = jnp.concatenate([s[i][:, 0 : i * HALF], diagonal], axis=1) if i else diagonal
            parts.append(part)
            peaks.append(jnp.max(part, axis=1, keepdims=True))
        for i in range(3):
            rows = slice(i * HALF, (i + 1) * HALF)
            p = jnp.exp2(parts[i] - peaks[i]).astype(BF)
            acc = jnp.dot(p, values_ref[0 : (i + 1) * HALF, :], preferred_element_type=F32)
            total = acc[:, HEAD : 2 * HEAD]
            out_ref[rows, HEAD * h : HEAD * h + HEAD] = (acc[:, 0:HEAD] / total).astype(BF)
            lse_ref[rows, :] = jnp.where(lane == head, peaks[i] + jnp.log2(total), lse_ref[rows, :])

    pipelined(STEP, scores, finish)


def anchor_kernel(q_ref, k_ref, v_ref, own_ref, lse_ref, out_ref, values_ref, keys_ref):
    fill_values(v_ref, values_ref)

    @pl.when(pl.program_id(0) == 0)
    def _():
        k = k_ref[...].astype(F32) * LOG2_SCALE
        high = k.astype(BF)
        keys_ref[:, 0:HEAD] = high
        keys_ref[:, HEAD : 2 * HEAD] = (k - high.astype(F32)).astype(BF)

    first = jnp.logical_and(
        lax.axis_index("c") == 0,
        jnp.logical_and(lax.axis_index("x") == 0, lax.axis_index("y") == 0),
    )
    lane = lax.broadcasted_iota(jnp.int32, (BLOCK, HEAD), 1)

    def scores(h):
        q = q_ref[:, HEAD * h : HEAD * h + HEAD]
        return lax.dot_general(
            jnp.concatenate([q, q], axis=1), keys_ref[...], (((1,), (1,)), ((), ())), preferred_element_type=F32
        )

    def finish(h, s):
        head = pl.program_id(0) * STEP + h
        lse = jnp.sum(jnp.where(lane == head, lse_ref[...], 0.0), axis=1, keepdims=True)
        peak = jnp.maximum(lse, jnp.max(s, axis=1, keepdims=True))
        p = jnp.exp2(s - peak).astype(BF)
        acc = jnp.dot(p, values_ref[...], preferred_element_type=F32)
        weight = jnp.exp2(lse - peak)
        mixture = acc[:, 0:HEAD] + weight * own_ref[:, HEAD * h : HEAD * h + HEAD].astype(F32)
        out_ref[:, HEAD * h : HEAD * h + HEAD] = (mixture / (acc[:, HEAD : 2 * HEAD] + weight)).astype(BF)

    @pl.when(first)
    def _():
        out_ref[...] = own_ref[...]

    @pl.when(jnp.logical_not(first))
    def _():
        pipelined(STEP, scores, finish)


VMEM = pl.BlockSpec(memory_space=pltpu.VMEM)
HBM = pl.BlockSpec(memory_space=pltpu.HBM)
WIDE = HEADS * HEAD
STEP_BLOCK = pl.BlockSpec((BLOCK, STEP_COLUMNS), lambda t: (0, t))
HEAD_BLOCK = pl.BlockSpec((BLOCK, HEAD), lambda t: (0, 0))


def in_hbm(*arrays):
    return [pltpu.with_memory_space_constraint(a, pltpu.HBM) for a in arrays]


def shape(dims, dtype=BF):
    return jax.ShapeDtypeStruct(dims, dtype)


def buffer(dims, dtype=BF):
    return pltpu.VMEM(dims, dtype)


def run(kernel, name, operands, in_specs, out_shape, out_specs, scratch, flops, nbytes, exps=0, grid=(), aliases=None):
    return pl.pallas_call(
        kernel,
        grid=grid,
        in_specs=in_specs,
        out_specs=out_specs,
        out_shape=out_shape,
        scratch_shapes=scratch,
        input_output_aliases=aliases or {},
        compiler_params=pltpu.CompilerParams(vmem_limit_bytes=24 * 1024 * 1024),
        cost_estimate=pl.CostEstimate(flops=flops, bytes_accessed=nbytes, transcendentals=exps),
        name=name,
    )(*operands)


def prep_call(query, k, v):
    return run(
        prep_kernel, "prep", in_hbm(query, k, v), [HBM] * 3,
        (shape((HALF, WIDE)), shape((BLOCK, HEAD)), shape((BLOCK, 2 * HEAD))), (VMEM,) * 3,
        [buffer((BLOCK, HEAD)), pltpu.SemaphoreType.DMA((3,))], 1 << 18, 2 << 20,
    )


def query_call(q, k, values, kp, vp):
    return run(
        query_kernel, "query_attention", (q, k, values, kp, vp), [VMEM] * 5,
        pltpu.HBM((16, SEND1, HEAD), BF), HBM,
        [buffer((BLOCK, 2 * HEAD)), buffer((16, SEND1, HEAD)), pltpu.SemaphoreType.DMA((HEADS,))],
        4 * 2048 * 1536 * 256, 3 << 20, 2048 * 1536,
    )


def own_call(ctx_query, k, v, after):
    return run(
        own_kernel, "context_own", in_hbm(ctx_query, k, v, after),
        [STEP_BLOCK, HEAD_BLOCK, HEAD_BLOCK, HBM],
        (pltpu.HBM((BLOCK, WIDE), BF), pltpu.HBM((BLOCK, HEAD), F32)), (STEP_BLOCK, HEAD_BLOCK),
        [buffer((BLOCK, 2 * HEAD))], 4 * 6144 * 512 * 256, 4 << 20, 6144 * 512, grid=(HEADS // STEP,),
    )


def anchor_call(ctx_query, k, v, own, lse):
    return run(
        anchor_kernel, "context_anchor", in_hbm(ctx_query, k, v, own, lse),
        [STEP_BLOCK, HEAD_BLOCK, HEAD_BLOCK, STEP_BLOCK, HEAD_BLOCK],
        shape((BLOCK, WIDE)), STEP_BLOCK,
        [buffer((BLOCK, 2 * HEAD))] * 2, 4 * 6144 * 768 * 256, 6 << 20, 6144 * 768, grid=(HEADS // STEP,),
    )


def combine_call(received, after):
    return run(
        combine_kernel, "combine", (received, *in_hbm(after)), [VMEM, HBM],
        shape((16, SEND2, HEAD)), VMEM, [], 1 << 20, 3 << 19,
    )


def project_mine_call(mine, w):
    return run(
        project_mine_kernel, "project_mine", (mine, w), [VMEM] * 2,
        pltpu.HBM((8, 64, 256), BF), HBM,
        [buffer((4, 64, 256)), pltpu.SemaphoreType.DMA], 2 * 256 * 1024 * 256, 1 << 20,
    )


def project_other_call(half_done, mine, other, w):
    return run(
        project_other_kernel, "project_other", (*in_hbm(half_done), mine, other, w), [HBM] + [VMEM] * 3,
        (pltpu.HBM((8, 64, 256), BF), pltpu.HBM((BLOCK, HEAD), BF), pltpu.HBM((BLOCK, HEAD), BF)), (HBM,) * 3,
        [
            buffer((4, 64, 256)), buffer((BLOCK, HEAD)), buffer((BLOCK, HEAD)),
            pltpu.SemaphoreType.DMA, pltpu.SemaphoreType.DMA((2,)),
        ],
        2 * 256 * 1024 * 256, 1 << 20, aliases={0: 0},
    )


def final_sum(received):
    return jnp.sum(received.astype(F32), axis=0).astype(BF)


def swap(value):
    return lax.ppermute(value, "c", [(0, 1), (1, 0)])


def exchange(value, axes):
    return lax.all_to_all(value, axes, 0, 0, tiled=True)


def per_device(ctx_query, context_key, context_value, query, out_weight):
    key_p, value_p = swap(context_key), swap(context_value)
    q, k, values = prep_call(query, context_key, context_value)
    sent = query_call(q, k, values, key_p, value_p)
    received = exchange(sent, ("x", "y"))
    own, lse = own_call(ctx_query, context_key, context_value, sent)
    gathered = exchange(combine_call(received, lse), ("x", "y"))
    other = swap(gathered)
    half_done = project_mine_call(gathered, out_weight)
    shares, key_a, value_a = project_other_call(half_done, gathered, other, out_weight)
    ctx_out = anchor_call(ctx_query, key_a, value_a, own, lse)
    answer = final_sum(exchange(shares, "z"))
    return ctx_out, answer


def solution(mesh):
    fine = Mesh(mesh.devices.reshape(4, 4, 2, 8), ("y", "x", "c", "z"))
    hst = ("y", "x", "c")
    in_specs = (P(hst, "z"), P(hst, "z"), P(hst, "z"), P(None, "z"), P("z", hst))
    out_specs = (P(hst, "z"), P("z", hst))
    return jax.shard_map(
        per_device, mesh=fine, in_specs=in_specs, out_specs=out_specs, check_vma=False
    )
```

```python
import functools

import jax
import jax.numpy as jnp
from jax import lax
from jax.experimental import pallas as pl
from jax.experimental.pallas import tpu as pltpu
from jax.sharding import Mesh, PartitionSpec as P

HEAD = 128
BLOCK = 768
HEADS = 8
HALF = 256
STATS = HEAD + 16
ANCHOR_ROWS = 48
SEND1 = STATS + ANCHOR_ROWS
SEND2 = HEAD + ANCHOR_ROWS
HIDDEN = 1e30
LOG2_SCALE = 1.4426950408889634 * HEAD ** (-0.5)
BF = jnp.bfloat16
F32 = jnp.float32


def scores_of(q, k):
    return lax.dot_general(q, k, (((1,), (1,)), ((), ())), preferred_element_type=F32) * LOG2_SCALE


def pipelined(count, scores, finish):
    s = scores(0)
    for n in range(count):
        s_next = scores(n + 1) if n + 1 < count else None
        finish(n, s)
        s = s_next


def to_lanes(column):
    r = lax.broadcasted_iota(jnp.int32, (HEAD, HEAD), 0)
    c = lax.broadcasted_iota(jnp.int32, (HEAD, HEAD), 1)
    return jnp.sum(jnp.where(r == c, column, 0.0), axis=0, keepdims=True)


def prep_kernel(q_hbm, k_hbm, v_hbm, q_ref, k_ref, values_ref, v_buf, sems):
    rows = pl.ds(pl.multiple_of(HALF * lax.axis_index("c"), HALF), HALF)
    copies = [
        pltpu.make_async_copy(v_hbm, v_buf, sems.at[0]),
        pltpu.make_async_copy(k_hbm, k_ref, sems.at[1]),
        pltpu.make_async_copy(q_hbm.at[rows, :], q_ref, sems.at[2]),
    ]
    for copy in copies:
        copy.start()
    values_ref[:, HEAD : 2 * HEAD] = jnp.ones((BLOCK, HEAD), BF)
    for copy in copies:
        copy.wait()
    values_ref[:, 0:HEAD] = v_buf[...]


def query_kernel(first_head, q_ref, k_ref, values_ref, kp_ref, vp_ref, *refs):
    out_hbm, values_p, out_ref, sems = refs[-4:]
    core = lax.axis_index("c")
    values_p[:, 0:HEAD] = vp_ref[...]
    values_p[:, HEAD : 2 * HEAD] = jnp.ones((BLOCK, HEAD), BF)
    row_id = lax.broadcasted_iota(jnp.int32, (16, HEAD), 0)

    def scores(j):
        at = HEAD * (first_head + j)
        q = q_ref[:, at : at + HEAD]
        return scores_of(q, k_ref[...]), scores_of(q, kp_ref[...])

    def finish(j, s):
        peak = jnp.maximum(
            jnp.max(s[0], axis=1, keepdims=True), jnp.max(s[1], axis=1, keepdims=True)
        )
        peak = peak.astype(BF).astype(F32)
        acc = jnp.dot(
            jnp.exp2(s[0] - peak).astype(BF), values_ref[...], preferred_element_type=F32
        ) + jnp.dot(jnp.exp2(s[1] - peak).astype(BF), values_p[...], preferred_element_type=F32)
        total = acc[:, HEAD : HEAD + 1]
        for half in range(2):
            rows = slice(half * HEAD, half * HEAD + HEAD)
            out_ref[2 * j + half, 0:HEAD, :] = acc[rows, 0:HEAD].astype(BF)
            peak_l = to_lanes(peak[rows])
            total_l = to_lanes(total[rows])
            high = total_l.astype(BF).astype(F32)
            stats = jnp.where(row_id == 0, peak_l, 0.0)
            stats = jnp.where(row_id == 1, high, stats)
            stats = jnp.where(row_id == 2, total_l - high, stats)
            out_ref[2 * j + half, HEAD:STATS, :] = stats.astype(BF)
            at = (2 * (first_head + j) + half) * ANCHOR_ROWS
            out_ref[2 * j + half, STATS:SEND1, :] = jnp.where(
                core == 0, k_ref[at : at + ANCHOR_ROWS, :], vp_ref[at : at + ANCHOR_ROWS, :]
            )

    def write(j):
        rows = slice(2 * (first_head + j), 2 * (first_head + j) + 2)
        return pltpu.make_async_copy(out_ref.at[2 * j : 2 * j + 2], out_hbm.at[rows], sems.at[j])

    def finish_and_write(j, s):
        finish(j, s)
        write(j).start()

    pipelined(HEADS // 2, scores, finish_and_write)
    for j in range(HEADS // 2):
        write(j).wait()


def combine_kernel(in_ref, after_ref, out_ref):
    stats = in_ref[:, HEAD:STATS, :].astype(F32)
    peak = stats[:, 0, :]
    total = stats[:, 1, :] + stats[:, 2, :]
    top = jnp.max(peak, axis=0, keepdims=True)
    weight = jnp.exp2(peak - top)
    weight = weight / jnp.sum(weight * total, axis=0, keepdims=True)
    weight_t = jnp.concatenate([weight, jnp.zeros((HEAD - 16, HEAD), F32)], axis=0).T
    out = jnp.zeros((HEAD, HEAD), F32)
    for g in range(16):
        out = out + weight_t[:, g : g + 1] * in_ref[g, 0:HEAD, :].astype(F32)
    out = out.astype(BF)
    anchor = in_ref[0, STATS:SEND1, :]
    for g in range(16):
        out_ref[g, 0:HEAD, :] = out
        out_ref[g, HEAD:SEND2, :] = anchor


def project_kernel(mine_ref, other_ref, w_ref, out_hbm, k_hbm, v_hbm, out_ref, k_ref, v_ref, sems):
    core = lax.axis_index("c")
    for g in range(16):
        rows = slice(g * ANCHOR_ROWS, (g + 1) * ANCHOR_ROWS)
        one, two = mine_ref[g, HEAD:SEND2, :], other_ref[g, HEAD:SEND2, :]
        k_ref[rows, :] = jnp.where(core == 0, one, two)
        v_ref[rows, :] = jnp.where(core == 0, two, one)
    copies = [
        pltpu.make_async_copy(k_ref, k_hbm, sems.at[0]),
        pltpu.make_async_copy(v_ref, v_hbm, sems.at[1]),
    ]
    for copy in copies:
        copy.start()
    for ref, owner in ((mine_ref, core), (other_ref, 1 - core)):
        a = jnp.concatenate(
            [
                jnp.concatenate([ref[2 * j + half, 0:HEAD, :] for j in range(HEADS)], axis=1)
                for half in range(2)
            ],
            axis=0,
        )
        y = jnp.dot(a, w_ref[...], preferred_element_type=F32).astype(BF)
        for z in range(4):
            out_ref[4 * owner + z] = y[64 * z : 64 * z + 64, :]
        half = pl.ds(4 * owner, 4)
        copies.append(pltpu.make_async_copy(out_ref.at[half], out_hbm.at[half], sems.at[len(copies)]))
        copies[-1].start()
    for copy in copies:
        copy.wait()


def final_kernel(in_ref, out_ref):
    total = in_ref[0].astype(F32)
    for z in range(1, 8):
        total = total + in_ref[z].astype(F32)
    out_ref[...] = total.astype(BF)


STEP = 2
STEP_COLUMNS = STEP * HEAD


def fill_values(v_ref, values_ref):
    @pl.when(pl.program_id(0) == 0)
    def _():
        values_ref[:, 0:HEAD] = v_ref[...]
        values_ref[:, HEAD : 2 * HEAD] = jnp.ones((BLOCK, HEAD), BF)


def own_kernel(q_ref, k_ref, v_ref, after_ref, out_ref, lse_ref, values_ref):
    fill_values(v_ref, values_ref)

    @pl.when(pl.program_id(0) == 0)
    def _():
        lse_ref[...] = jnp.zeros((BLOCK, HEAD), F32)

    lane = lax.broadcasted_iota(jnp.int32, (HALF, HEAD), 1)
    r = lax.broadcasted_iota(jnp.int32, (HALF, HALF), 0)
    c = lax.broadcasted_iota(jnp.int32, (HALF, HALF), 1)

    def scores(h):
        return [
            scores_of(q_ref[i * HALF : (i + 1) * HALF, HEAD * h : HEAD * h + HEAD], k_ref[0 : (i + 1) * HALF, :])
            for i in range(3)
        ]

    def finish(h, s):
        head = pl.program_id(0) * STEP + h
        parts, peaks = [], []
        for i in range(3):
            diagonal = jnp.where(c <= r, s[i][:, i * HALF :], -HIDDEN)
            part = jnp.concatenate([s[i][:, 0 : i * HALF], diagonal], axis=1) if i else diagonal
            parts.append(part)
            peaks.append(jnp.max(part, axis=1, keepdims=True))
        for i in range(3):
            rows = slice(i * HALF, (i + 1) * HALF)
            p = jnp.exp2(parts[i] - peaks[i]).astype(BF)
            acc = jnp.dot(p, values_ref[0 : (i + 1) * HALF, :], preferred_element_type=F32)
            total = acc[:, HEAD : 2 * HEAD]
            out_ref[rows, HEAD * h : HEAD * h + HEAD] = (acc[:, 0:HEAD] / total).astype(BF)
            lse_ref[rows, :] = jnp.where(lane == head, peaks[i] + jnp.log2(total), lse_ref[rows, :])

    pipelined(STEP, scores, finish)


def anchor_kernel(q_ref, k_ref, v_ref, own_ref, lse_ref, out_ref, values_ref, keys_ref):
    fill_values(v_ref, values_ref)

    @pl.when(pl.program_id(0) == 0)
    def _():
        k = k_ref[...].astype(F32) * LOG2_SCALE
        high = k.astype(BF)
        keys_ref[:, 0:HEAD] = high
        keys_ref[:, HEAD : 2 * HEAD] = (k - high.astype(F32)).astype(BF)

    first = jnp.logical_and(
        lax.axis_index("c") == 0,
        jnp.logical_and(lax.axis_index("x") == 0, lax.axis_index("y") == 0),
    )
    lane = lax.broadcasted_iota(jnp.int32, (BLOCK, HEAD), 1)

    def scores(h):
        q = q_ref[:, HEAD * h : HEAD * h + HEAD]
        return lax.dot_general(
            jnp.concatenate([q, q], axis=1), keys_ref[...], (((1,), (1,)), ((), ())), preferred_element_type=F32
        )

    def finish(h, s):
        head = pl.program_id(0) * STEP + h
        lse = jnp.sum(jnp.where(lane == head, lse_ref[...], 0.0), axis=1, keepdims=True)
        peak = jnp.maximum(lse, jnp.max(s, axis=1, keepdims=True))
        p = jnp.exp2(s - peak).astype(BF)
        acc = jnp.dot(p, values_ref[...], preferred_element_type=F32)
        weight = jnp.exp2(lse - peak)
        mixture = acc[:, 0:HEAD] + weight * own_ref[:, HEAD * h : HEAD * h + HEAD].astype(F32)
        out_ref[:, HEAD * h : HEAD * h + HEAD] = (mixture / (acc[:, HEAD : 2 * HEAD] + weight)).astype(BF)

    @pl.when(first)
    def _():
        out_ref[...] = own_ref[...]

    @pl.when(jnp.logical_not(first))
    def _():
        pipelined(STEP, scores, finish)


VMEM = pl.BlockSpec(memory_space=pltpu.VMEM)
HBM = pl.BlockSpec(memory_space=pltpu.HBM)
ANY = pl.BlockSpec(memory_space=pl.ANY)
WIDE = HEADS * HEAD
STEP_BLOCK = pl.BlockSpec((BLOCK, STEP_COLUMNS), lambda t: (0, t))
HEAD_BLOCK = pl.BlockSpec((BLOCK, HEAD), lambda t: (0, 0))


def in_hbm(*arrays):
    return [pltpu.with_memory_space_constraint(a, pltpu.HBM) for a in arrays]


def shape(dims, dtype=BF):
    return jax.ShapeDtypeStruct(dims, dtype)


def buffer(dims, dtype=BF):
    return pltpu.VMEM(dims, dtype)


def run(kernel, name, operands, in_specs, out_shape, out_specs, scratch, flops, nbytes, exps=0, grid=(), aliases=None):
    return pl.pallas_call(
        kernel,
        grid=grid,
        in_specs=in_specs,
        out_specs=out_specs,
        out_shape=out_shape,
        scratch_shapes=scratch,
        input_output_aliases=aliases or {},
        compiler_params=pltpu.CompilerParams(vmem_limit_bytes=24 * 1024 * 1024),
        cost_estimate=pl.CostEstimate(flops=flops, bytes_accessed=nbytes, transcendentals=exps),
        name=name,
    )(*operands)


def prep_call(query, k, v):
    return run(
        prep_kernel, "prep", in_hbm(query, k, v), [HBM] * 3,
        (shape((HALF, WIDE)), shape((BLOCK, HEAD)), shape((BLOCK, 2 * HEAD))), (VMEM,) * 3,
        [buffer((BLOCK, HEAD)), pltpu.SemaphoreType.DMA((3,))], 1 << 18, 2 << 20,
    )


def query_call(first_head, q, k, values, kp, vp, *more, anywhere=()):
    return run(
        functools.partial(query_kernel, first_head), f"query_attention_{first_head}",
        (q, k, values, kp, vp, *in_hbm(*more), *anywhere),
        [VMEM] * 5 + [HBM] * len(more) + [ANY] * len(anywhere),
        pltpu.HBM((16, SEND1, HEAD), BF), HBM,
        [buffer((BLOCK, 2 * HEAD)), buffer((HEADS, SEND1, HEAD)), pltpu.SemaphoreType.DMA((HEADS // 2,))],
        2 * 2048 * 1536 * 256, 3 << 20, 1024 * 1536, aliases={5: 0} if more else None,
    )


def own_call(ctx_query, k, v, after):
    return run(
        own_kernel, "context_own", in_hbm(ctx_query, k, v, after),
        [STEP_BLOCK, HEAD_BLOCK, HEAD_BLOCK, HBM],
        (pltpu.HBM((BLOCK, WIDE), BF), pltpu.HBM((BLOCK, HEAD), F32)), (STEP_BLOCK, HEAD_BLOCK),
        [buffer((BLOCK, 2 * HEAD))], 4 * 6144 * 512 * 256, 4 << 20, 6144 * 512, grid=(HEADS // STEP,),
    )


def anchor_call(ctx_query, k, v, own, lse):
    return run(
        anchor_kernel, "context_anchor", in_hbm(ctx_query, k, v, own, lse),
        [STEP_BLOCK, HEAD_BLOCK, HEAD_BLOCK, STEP_BLOCK, HEAD_BLOCK],
        shape((BLOCK, WIDE)), STEP_BLOCK,
        [buffer((BLOCK, 2 * HEAD))] * 2, 4 * 6144 * 768 * 256, 6 << 20, 6144 * 768, grid=(HEADS // STEP,),
    )


def combine_call(received, after):
    return run(
        combine_kernel, "combine", (received, *in_hbm(after)), [VMEM, HBM],
        shape((16, SEND2, HEAD)), VMEM, [], 1 << 20, 3 << 19,
    )


def project_call(mine, other, w):
    return run(
        project_kernel, "project", (mine, other, w), [VMEM] * 3,
        (pltpu.HBM((8, 64, 256), BF), pltpu.HBM((BLOCK, HEAD), BF), pltpu.HBM((BLOCK, HEAD), BF)), (HBM,) * 3,
        [buffer((8, 64, 256)), buffer((BLOCK, HEAD)), buffer((BLOCK, HEAD)), pltpu.SemaphoreType.DMA((4,))],
        2 * 512 * 1024 * 256, 2 << 20,
    )


def final_call(received):
    return run(final_kernel, "final_sum", (received,), [VMEM], shape((64, 256)), VMEM, [], 1 << 17, 1 << 18)


def swap(value):
    return lax.ppermute(value, "c", [(0, 1), (1, 0)])


def greet(axis, size):
    few = jnp.ones((16, HEAD), BF)
    return lax.ppermute(few, axis, [(i, (i + 1) % size) for i in range(size)])


def exchange(value, axes):
    return lax.all_to_all(value, axes, 0, 0, tiled=True)


def per_device(ctx_query, context_key, context_value, query, out_weight):
    key_p, value_p = swap(context_key), swap(context_value)
    q, k, values = prep_call(query, context_key, context_value)
    greetings = (greet("x", 4), greet("y", 4))
    half_sent = query_call(0, q, k, values, key_p, value_p)
    sent = query_call(HEADS // 2, q, k, values, key_p, value_p, half_sent, anywhere=greetings)
    received = exchange(sent, ("x", "y"))
    own, lse = own_call(ctx_query, context_key, context_value, sent)
    gathered = exchange(combine_call(received, lse), ("x", "y"))
    shares, key_a, value_a = project_call(gathered, swap(gathered), out_weight)
    ctx_out = anchor_call(ctx_query, key_a, value_a, own, lse)
    answer = final_call(exchange(shares, "z"))
    return ctx_out, answer


def solution(mesh):
    fine = Mesh(mesh.devices.reshape(4, 4, 2, 8), ("y", "x", "c", "z"))
    hst = ("y", "x", "c")
    in_specs = (P(hst, "z"), P(hst, "z"), P(hst, "z"), P(None, "z"), P("z", hst))
    out_specs = (P(hst, "z"), P("z", hst))
    return jax.shard_map(
        per_device, mesh=fine, in_specs=in_specs, out_specs=out_specs, check_vma=False
    )
```

```python
import functools

import jax
import jax.numpy as jnp
from jax import lax
from jax.experimental import pallas as pl
from jax.experimental.pallas import tpu as pltpu
from jax.sharding import Mesh, PartitionSpec as P

HEAD = 128
BLOCK = 768
HEADS = 8
HALF = 256
STATS = HEAD + 16
ANCHOR_ROWS = 48
SEND1 = STATS + ANCHOR_ROWS
SEND2 = HEAD + ANCHOR_ROWS
HIDDEN = 1e30
Z_ORDER = [[4, 5, 6, 7, 0, 1, 2, 3]]
LOG2_SCALE = 1.4426950408889634 * HEAD ** (-0.5)
BF = jnp.bfloat16
F32 = jnp.float32


def scores_of(q, k):
    return lax.dot_general(q, k, (((1,), (1,)), ((), ())), preferred_element_type=F32) * LOG2_SCALE


def pipelined(count, scores, finish):
    s = scores(0)
    for n in range(count):
        s_next = scores(n + 1) if n + 1 < count else None
        finish(n, s)
        s = s_next


def to_lanes(column):
    r = lax.broadcasted_iota(jnp.int32, (HEAD, HEAD), 0)
    c = lax.broadcasted_iota(jnp.int32, (HEAD, HEAD), 1)
    return jnp.sum(jnp.where(r == c, column, 0.0), axis=0, keepdims=True)


def prep_kernel(q_hbm, k_hbm, v_hbm, q_ref, k_ref, values_ref, v_buf, sems):
    rows = pl.ds(pl.multiple_of(HALF * lax.axis_index("c"), HALF), HALF)
    copies = [
        pltpu.make_async_copy(v_hbm, v_buf, sems.at[0]),
        pltpu.make_async_copy(k_hbm, k_ref, sems.at[1]),
        pltpu.make_async_copy(q_hbm.at[rows, :], q_ref, sems.at[2]),
    ]
    for copy in copies:
        copy.start()
    values_ref[:, HEAD : 2 * HEAD] = jnp.ones((BLOCK, HEAD), BF)
    for copy in copies:
        copy.wait()
    values_ref[:, 0:HEAD] = v_buf[...]


def query_kernel(q_ref, k_ref, values_ref, kp_ref, vp_ref, out_hbm, values_p, out_ref, sems):
    core = lax.axis_index("c")
    values_p[:, 0:HEAD] = vp_ref[...]
    values_p[:, HEAD : 2 * HEAD] = jnp.ones((BLOCK, HEAD), BF)
    row_id = lax.broadcasted_iota(jnp.int32, (16, HEAD), 0)

    def scores(j):
        q = q_ref[:, HEAD * j : HEAD * j + HEAD]
        return scores_of(q, k_ref[...]), scores_of(q, kp_ref[...])

    def finish(j, s):
        peak = jnp.maximum(
            jnp.max(s[0], axis=1, keepdims=True), jnp.max(s[1], axis=1, keepdims=True)
        )
        peak = peak.astype(BF).astype(F32)
        acc = jnp.dot(
            jnp.exp2(s[0] - peak).astype(BF), values_ref[...], preferred_element_type=F32
        ) + jnp.dot(jnp.exp2(s[1] - peak).astype(BF), values_p[...], preferred_element_type=F32)
        total = acc[:, HEAD : HEAD + 1]
        for half in range(2):
            rows = slice(half * HEAD, half * HEAD + HEAD)
            out_ref[2 * j + half, 0:HEAD, :] = acc[rows, 0:HEAD].astype(BF)
            peak_l = to_lanes(peak[rows])
            total_l = to_lanes(total[rows])
            high = total_l.astype(BF).astype(F32)
            stats = jnp.where(row_id == 0, peak_l, 0.0)
            stats = jnp.where(row_id == 1, high, stats)
            stats = jnp.where(row_id == 2, total_l - high, stats)
            out_ref[2 * j + half, HEAD:STATS, :] = stats.astype(BF)
            at = (2 * j + half) * ANCHOR_ROWS
            out_ref[2 * j + half, STATS:SEND1, :] = jnp.where(
                core == 0, k_ref[at : at + ANCHOR_ROWS, :], vp_ref[at : at + ANCHOR_ROWS, :]
            )

    def write(j):
        rows = slice(2 * j, 2 * j + 2)
        return pltpu.make_async_copy(out_ref.at[rows], out_hbm.at[rows], sems.at[j])

    def finish_and_write(j, s):
        finish(j, s)
        write(j).start()

    pipelined(HEADS, scores, finish_and_write)
    for j in range(HEADS):
        write(j).wait()


def combine_kernel(in_ref, after_ref, out_ref):
    stats = in_ref[:, HEAD:STATS, :].astype(F32)
    peak = stats[:, 0, :]
    total = stats[:, 1, :] + stats[:, 2, :]
    top = jnp.max(peak, axis=0, keepdims=True)
    weight = jnp.exp2(peak - top)
    weight = weight / jnp.sum(weight * total, axis=0, keepdims=True)
    weight_t = jnp.concatenate([weight, jnp.zeros((HEAD - 16, HEAD), F32)], axis=0).T
    out = jnp.zeros((HEAD, HEAD), F32)
    for g in range(16):
        out = out + weight_t[:, g : g + 1] * in_ref[g, 0:HEAD, :].astype(F32)
    out = out.astype(BF)
    anchor = in_ref[0, STATS:SEND1, :]
    for g in range(16):
        out_ref[g, 0:HEAD, :] = out
        out_ref[g, HEAD:SEND2, :] = anchor


def project_kernel(mine_ref, other_ref, w_ref, out_hbm, k_hbm, v_hbm, out_ref, k_ref, v_ref, sems):
    core = lax.axis_index("c")
    for g in range(16):
        rows = slice(g * ANCHOR_ROWS, (g + 1) * ANCHOR_ROWS)
        one, two = mine_ref[g, HEAD:SEND2, :], other_ref[g, HEAD:SEND2, :]
        k_ref[rows, :] = jnp.where(core == 0, one, two)
        v_ref[rows, :] = jnp.where(core == 0, two, one)
    copies = [
        pltpu.make_async_copy(k_ref, k_hbm, sems.at[0]),
        pltpu.make_async_copy(v_ref, v_hbm, sems.at[1]),
    ]
    for copy in copies:
        copy.start()
    for ref, place in ((mine_ref, 1 - core), (other_ref, core)):
        a = jnp.concatenate(
            [
                jnp.concatenate([ref[2 * j + half, 0:HEAD, :] for j in range(HEADS)], axis=1)
                for half in range(2)
            ],
            axis=0,
        )
        y = jnp.dot(a, w_ref[...], preferred_element_type=F32).astype(BF)
        for z in range(4):
            out_ref[4 * place + z] = y[64 * z : 64 * z + 64, :]
        half = pl.ds(4 * place, 4)
        copies.append(pltpu.make_async_copy(out_ref.at[half], out_hbm.at[half], sems.at[len(copies)]))
        copies[-1].start()
    for copy in copies:
        copy.wait()


def final_kernel(in_ref, out_ref):
    total = in_ref[0].astype(F32)
    for z in range(1, 8):
        total = total + in_ref[z].astype(F32)
    out_ref[...] = total.astype(BF)


STEP = 2
STEP_COLUMNS = STEP * HEAD


def fill_values(v_ref, values_ref):
    @pl.when(pl.program_id(0) == 0)
    def _():
        values_ref[:, 0:HEAD] = v_ref[...]
        values_ref[:, HEAD : 2 * HEAD] = jnp.ones((BLOCK, HEAD), BF)


def own_kernel(q_ref, k_ref, v_ref, after_ref, out_ref, lse_ref, values_ref):
    fill_values(v_ref, values_ref)

    @pl.when(pl.program_id(0) == 0)
    def _():
        lse_ref[...] = jnp.zeros((BLOCK, HEAD), F32)

    lane = lax.broadcasted_iota(jnp.int32, (HALF, HEAD), 1)
    r = lax.broadcasted_iota(jnp.int32, (HALF, HALF), 0)
    c = lax.broadcasted_iota(jnp.int32, (HALF, HALF), 1)

    def scores(h):
        return [
            scores_of(q_ref[i * HALF : (i + 1) * HALF, HEAD * h : HEAD * h + HEAD], k_ref[0 : (i + 1) * HALF, :])
            for i in range(3)
        ]

    def finish(h, s):
        head = pl.program_id(0) * STEP + h
        parts, peaks = [], []
        for i in range(3):
            diagonal = jnp.where(c <= r, s[i][:, i * HALF :], -HIDDEN)
            part = jnp.concatenate([s[i][:, 0 : i * HALF], diagonal], axis=1) if i else diagonal
            parts.append(part)
            peaks.append(jnp.max(part, axis=1, keepdims=True))
        for i in range(3):
            rows = slice(i * HALF, (i + 1) * HALF)
            p = jnp.exp2(parts[i] - peaks[i]).astype(BF)
            acc = jnp.dot(p, values_ref[0 : (i + 1) * HALF, :], preferred_element_type=F32)
            total = acc[:, HEAD : 2 * HEAD]
            out_ref[rows, HEAD * h : HEAD * h + HEAD] = (acc[:, 0:HEAD] / total).astype(BF)
            lse_ref[rows, :] = jnp.where(lane == head, peaks[i] + jnp.log2(total), lse_ref[rows, :])

    pipelined(STEP, scores, finish)


def anchor_kernel(q_ref, k_ref, v_ref, own_ref, lse_ref, out_ref, values_ref, keys_ref):
    fill_values(v_ref, values_ref)

    @pl.when(pl.program_id(0) == 0)
    def _():
        k = k_ref[...].astype(F32) * LOG2_SCALE
        high = k.astype(BF)
        keys_ref[:, 0:HEAD] = high
        keys_ref[:, HEAD : 2 * HEAD] = (k - high.astype(F32)).astype(BF)

    first = jnp.logical_and(
        lax.axis_index("c") == 0,
        jnp.logical_and(lax.axis_index("x") == 0, lax.axis_index("y") == 0),
    )
    lane = lax.broadcasted_iota(jnp.int32, (BLOCK, HEAD), 1)

    def scores(h):
        q = q_ref[:, HEAD * h : HEAD * h + HEAD]
        return lax.dot_general(
            jnp.concatenate([q, q], axis=1), keys_ref[...], (((1,), (1,)), ((), ())), preferred_element_type=F32
        )

    def finish(h, s):
        head = pl.program_id(0) * STEP + h
        lse = jnp.sum(jnp.where(lane == head, lse_ref[...], 0.0), axis=1, keepdims=True)
        peak = jnp.maximum(lse, jnp.max(s, axis=1, keepdims=True))
        p = jnp.exp2(s - peak).astype(BF)
        acc = jnp.dot(p, values_ref[...], preferred_element_type=F32)
        weight = jnp.exp2(lse - peak)
        mixture = acc[:, 0:HEAD] + weight * own_ref[:, HEAD * h : HEAD * h + HEAD].astype(F32)
        out_ref[:, HEAD * h : HEAD * h + HEAD] = (mixture / (acc[:, HEAD : 2 * HEAD] + weight)).astype(BF)

    @pl.when(first)
    def _():
        out_ref[...] = own_ref[...]

    @pl.when(jnp.logical_not(first))
    def _():
        pipelined(STEP, scores, finish)


VMEM = pl.BlockSpec(memory_space=pltpu.VMEM)
HBM = pl.BlockSpec(memory_space=pltpu.HBM)
WIDE = HEADS * HEAD
STEP_BLOCK = pl.BlockSpec((BLOCK, STEP_COLUMNS), lambda t: (0, t))
HEAD_BLOCK = pl.BlockSpec((BLOCK, HEAD), lambda t: (0, 0))


def in_hbm(*arrays):
    return [pltpu.with_memory_space_constraint(a, pltpu.HBM) for a in arrays]


def shape(dims, dtype=BF):
    return jax.ShapeDtypeStruct(dims, dtype)


def buffer(dims, dtype=BF):
    return pltpu.VMEM(dims, dtype)


def run(kernel, name, operands, in_specs, out_shape, out_specs, scratch, flops, nbytes, exps=0, grid=()):
    return pl.pallas_call(
        kernel,
        grid=grid,
        in_specs=in_specs,
        out_specs=out_specs,
        out_shape=out_shape,
        scratch_shapes=scratch,
        compiler_params=pltpu.CompilerParams(vmem_limit_bytes=24 * 1024 * 1024),
        cost_estimate=pl.CostEstimate(flops=flops, bytes_accessed=nbytes, transcendentals=exps),
        name=name,
    )(*operands)


def prep_call(query, k, v):
    return run(
        prep_kernel, "prep", in_hbm(query, k, v), [HBM] * 3,
        (shape((HALF, WIDE)), shape((BLOCK, HEAD)), shape((BLOCK, 2 * HEAD))), (VMEM,) * 3,
        [buffer((BLOCK, HEAD)), pltpu.SemaphoreType.DMA((3,))], 1 << 18, 2 << 20,
    )


def query_call(q, k, values, kp, vp):
    return run(
        query_kernel, "query_attention", (q, k, values, kp, vp), [VMEM] * 5,
        pltpu.HBM((16, SEND1, HEAD), BF), HBM,
        [buffer((BLOCK, 2 * HEAD)), buffer((16, SEND1, HEAD)), pltpu.SemaphoreType.DMA((HEADS,))],
        4 * 2048 * 1536 * 256, 3 << 20, 2048 * 1536,
    )


def own_call(ctx_query, k, v, after):
    return run(
        own_kernel, "context_own", in_hbm(ctx_query, k, v, after),
        [STEP_BLOCK, HEAD_BLOCK, HEAD_BLOCK, HBM],
        (pltpu.HBM((BLOCK, WIDE), BF), pltpu.HBM((BLOCK, HEAD), F32)), (STEP_BLOCK, HEAD_BLOCK),
        [buffer((BLOCK, 2 * HEAD))], 4 * 6144 * 512 * 256, 4 << 20, 6144 * 512, grid=(HEADS // STEP,),
    )


def anchor_call(ctx_query, k, v, own, lse):
    return run(
        anchor_kernel, "context_anchor", in_hbm(ctx_query, k, v, own, lse),
        [STEP_BLOCK, HEAD_BLOCK, HEAD_BLOCK, STEP_BLOCK, HEAD_BLOCK],
        shape((BLOCK, WIDE)), STEP_BLOCK,
        [buffer((BLOCK, 2 * HEAD))] * 2, 4 * 6144 * 768 * 256, 6 << 20, 6144 * 768, grid=(HEADS // STEP,),
    )


def combine_call(received, after):
    return run(
        combine_kernel, "combine", (received, *in_hbm(after)), [VMEM, HBM],
        shape((16, SEND2, HEAD)), VMEM, [], 1 << 20, 3 << 19,
    )


def project_call(mine, other, w):
    return run(
        project_kernel, "project", (mine, other, w), [VMEM] * 3,
        (pltpu.HBM((8, 64, 256), BF), pltpu.HBM((BLOCK, HEAD), BF), pltpu.HBM((BLOCK, HEAD), BF)), (HBM,) * 3,
        [buffer((8, 64, 256)), buffer((BLOCK, HEAD)), buffer((BLOCK, HEAD)), pltpu.SemaphoreType.DMA((4,))],
        2 * 512 * 1024 * 256, 2 << 20,
    )


def final_call(received):
    return run(final_kernel, "final_sum", (received,), [VMEM], shape((64, 256)), VMEM, [], 1 << 17, 1 << 18)


def swap(value):
    return lax.ppermute(value, "c", [(0, 1), (1, 0)])


def exchange(value, axes, order=None):
    return lax.all_to_all(value, axes, 0, 0, axis_index_groups=order, tiled=True)


def per_device(ctx_query, context_key, context_value, query, out_weight):
    key_p, value_p = swap(context_key), swap(context_value)
    q, k, values = prep_call(query, context_key, context_value)
    sent = query_call(q, k, values, key_p, value_p)
    received = exchange(sent, ("x", "y"))
    own, lse = own_call(ctx_query, context_key, context_value, sent)
    gathered = exchange(combine_call(received, lse), ("x", "y"))
    shares, key_a, value_a = project_call(gathered, swap(gathered), out_weight)
    ctx_out = anchor_call(ctx_query, key_a, value_a, own, lse)
    answer = final_call(exchange(shares, "z", Z_ORDER))
    return ctx_out, answer


def solution(mesh):
    fine = Mesh(mesh.devices.reshape(4, 4, 2, 8), ("y", "x", "c", "z"))
    hst = ("y", "x", "c")
    in_specs = (P(hst, "z"), P(hst, "z"), P(hst, "z"), P(None, "z"), P("z", hst))
    out_specs = (P(hst, "z"), P("z", hst))
    return jax.shard_map(
        per_device, mesh=fine, in_specs=in_specs, out_specs=out_specs, check_vma=False
    )
```

```python
import functools

import jax
import jax.numpy as jnp
from jax import lax
from jax.experimental import pallas as pl
from jax.experimental.pallas import tpu as pltpu
from jax.sharding import Mesh, PartitionSpec as P

HEAD = 128
BLOCK = 768
HEADS = 8
HALF = 256
STATS = HEAD + 16
ANCHOR_ROWS = 48
SEND1 = STATS + ANCHOR_ROWS
SEND2 = HEAD + ANCHOR_ROWS
HIDDEN = 1e30
Z_ORDER = [[6, 7, 0, 1, 2, 3, 4, 5]]
PLANE_ORDER = [[8, 9, 10, 11, 12, 13, 14, 15, 0, 1, 2, 3, 4, 5, 6, 7]]
ROOT = 8
LOG2_SCALE = 1.4426950408889634 * HEAD ** (-0.5)
BF = jnp.bfloat16
F32 = jnp.float32


def scores_of(q, k):
    return lax.dot_general(q, k, (((1,), (1,)), ((), ())), preferred_element_type=F32) * LOG2_SCALE


def pipelined(count, scores, finish):
    s = scores(0)
    for n in range(count):
        s_next = scores(n + 1) if n + 1 < count else None
        finish(n, s)
        s = s_next


def to_lanes(column):
    r = lax.broadcasted_iota(jnp.int32, (HEAD, HEAD), 0)
    c = lax.broadcasted_iota(jnp.int32, (HEAD, HEAD), 1)
    return jnp.sum(jnp.where(r == c, column, 0.0), axis=0, keepdims=True)


def prep_kernel(q_hbm, k_hbm, v_hbm, q_ref, k_ref, values_ref, v_buf, sems):
    rows = pl.ds(pl.multiple_of(HALF * lax.axis_index("c"), HALF), HALF)
    copies = [
        pltpu.make_async_copy(v_hbm, v_buf, sems.at[0]),
        pltpu.make_async_copy(k_hbm, k_ref, sems.at[1]),
        pltpu.make_async_copy(q_hbm.at[rows, :], q_ref, sems.at[2]),
    ]
    for copy in copies:
        copy.start()
    values_ref[:, HEAD : 2 * HEAD] = jnp.ones((BLOCK, HEAD), BF)
    for copy in copies:
        copy.wait()
    values_ref[:, 0:HEAD] = v_buf[...]


def query_kernel(q_ref, k_ref, values_ref, kp_ref, vp_ref, out_hbm, values_p, out_ref, sems):
    core = lax.axis_index("c")
    values_p[:, 0:HEAD] = vp_ref[...]
    values_p[:, HEAD : 2 * HEAD] = jnp.ones((BLOCK, HEAD), BF)
    row_id = lax.broadcasted_iota(jnp.int32, (16, HEAD), 0)

    def scores(j):
        q = q_ref[:, HEAD * j : HEAD * j + HEAD]
        return scores_of(q, k_ref[...]), scores_of(q, kp_ref[...])

    def finish(j, s):
        peak = jnp.maximum(
            jnp.max(s[0], axis=1, keepdims=True), jnp.max(s[1], axis=1, keepdims=True)
        )
        peak = peak.astype(BF).astype(F32)
        acc = jnp.dot(
            jnp.exp2(s[0] - peak).astype(BF), values_ref[...], preferred_element_type=F32
        ) + jnp.dot(jnp.exp2(s[1] - peak).astype(BF), values_p[...], preferred_element_type=F32)
        total = acc[:, HEAD : HEAD + 1]
        for half in range(2):
            rows = slice(half * HEAD, half * HEAD + HEAD)
            out_ref[2 * j + half, 0:HEAD, :] = acc[rows, 0:HEAD].astype(BF)
            peak_l = to_lanes(peak[rows])
            total_l = to_lanes(total[rows])
            high = total_l.astype(BF).astype(F32)
            stats = jnp.where(row_id == 0, peak_l, 0.0)
            stats = jnp.where(row_id == 1, high, stats)
            stats = jnp.where(row_id == 2, total_l - high, stats)
            out_ref[2 * j + half, HEAD:STATS, :] = stats.astype(BF)
            at = (2 * j + half) * ANCHOR_ROWS
            out_ref[2 * j + half, STATS:SEND1, :] = jnp.where(
                core == 0, k_ref[at : at + ANCHOR_ROWS, :], vp_ref[at : at + ANCHOR_ROWS, :]
            )

    def write(j):
        rows = slice(2 * j, 2 * j + 2)
        return pltpu.make_async_copy(out_ref.at[rows], out_hbm.at[rows], sems.at[j])

    def finish_and_write(j, s):
        finish(j, s)
        write(j).start()

    pipelined(HEADS, scores, finish_and_write)
    for j in range(HEADS):
        write(j).wait()


def combine_kernel(in_ref, after_ref, out_ref):
    stats = in_ref[:, HEAD:STATS, :].astype(F32)
    peak = stats[:, 0, :]
    total = stats[:, 1, :] + stats[:, 2, :]
    top = jnp.max(peak, axis=0, keepdims=True)
    weight = jnp.exp2(peak - top)
    weight = weight / jnp.sum(weight * total, axis=0, keepdims=True)
    weight_t = jnp.concatenate([weight, jnp.zeros((HEAD - 16, HEAD), F32)], axis=0).T
    out = jnp.zeros((HEAD, HEAD), F32)
    for g in range(16):
        out = out + weight_t[:, g : g + 1] * in_ref[g, 0:HEAD, :].astype(F32)
    out = out.astype(BF)
    anchor = in_ref[ROOT, STATS:SEND1, :]
    for g in range(16):
        out_ref[g, 0:HEAD, :] = out
        out_ref[g, HEAD:SEND2, :] = anchor


def project_kernel(mine_ref, other_ref, w_ref, out_hbm, k_hbm, v_hbm, out_ref, k_ref, v_ref, sems):
    core = lax.axis_index("c")
    for g in range(16):
        rows = slice(g * ANCHOR_ROWS, (g + 1) * ANCHOR_ROWS)
        one, two = mine_ref[g, HEAD:SEND2, :], other_ref[g, HEAD:SEND2, :]
        k_ref[rows, :] = jnp.where(core == 0, one, two)
        v_ref[rows, :] = jnp.where(core == 0, two, one)
    copies = [
        pltpu.make_async_copy(k_ref, k_hbm, sems.at[0]),
        pltpu.make_async_copy(v_ref, v_hbm, sems.at[1]),
    ]
    for copy in copies:
        copy.start()
    for ref, owner in ((mine_ref, core), (other_ref, 1 - core)):
        a = jnp.concatenate(
            [
                jnp.concatenate([ref[2 * j + half, 0:HEAD, :] for j in range(HEADS)], axis=1)
                for half in range(2)
            ],
            axis=0,
        )
        y = jnp.dot(a, w_ref[...], preferred_element_type=F32).astype(BF)
        for t in range(2):
            place = lax.rem(2 * owner + t + 1, 4)
            for z in range(2):
                at = 64 * (2 * t + z)
                out_ref[2 * place + z] = y[at : at + 64, :]
            pair = pl.ds(2 * place, 2)
            copies.append(pltpu.make_async_copy(out_ref.at[pair], out_hbm.at[pair], sems.at[len(copies)]))
            copies[-1].start()
    for copy in copies:
        copy.wait()


def final_kernel(in_ref, out_ref):
    total = in_ref[0].astype(F32)
    for z in range(1, 8):
        total = total + in_ref[z].astype(F32)
    out_ref[...] = total.astype(BF)


STEP = 2
STEP_COLUMNS = STEP * HEAD


def fill_values(v_ref, values_ref):
    @pl.when(pl.program_id(0) == 0)
    def _():
        values_ref[:, 0:HEAD] = v_ref[...]
        values_ref[:, HEAD : 2 * HEAD] = jnp.ones((BLOCK, HEAD), BF)


def own_kernel(q_ref, k_ref, v_ref, after_ref, out_ref, lse_ref, values_ref):
    fill_values(v_ref, values_ref)

    @pl.when(pl.program_id(0) == 0)
    def _():
        lse_ref[...] = jnp.zeros((BLOCK, HEAD), F32)

    lane = lax.broadcasted_iota(jnp.int32, (HALF, HEAD), 1)
    r = lax.broadcasted_iota(jnp.int32, (HALF, HALF), 0)
    c = lax.broadcasted_iota(jnp.int32, (HALF, HALF), 1)

    def scores(h):
        return [
            scores_of(q_ref[i * HALF : (i + 1) * HALF, HEAD * h : HEAD * h + HEAD], k_ref[0 : (i + 1) * HALF, :])
            for i in range(3)
        ]

    def finish(h, s):
        head = pl.program_id(0) * STEP + h
        parts, peaks = [], []
        for i in range(3):
            diagonal = jnp.where(c <= r, s[i][:, i * HALF :], -HIDDEN)
            part = jnp.concatenate([s[i][:, 0 : i * HALF], diagonal], axis=1) if i else diagonal
            parts.append(part)
            peaks.append(jnp.max(part, axis=1, keepdims=True))
        for i in range(3):
            rows = slice(i * HALF, (i + 1) * HALF)
            p = jnp.exp2(parts[i] - peaks[i]).astype(BF)
            acc = jnp.dot(p, values_ref[0 : (i + 1) * HALF, :], preferred_element_type=F32)
            total = acc[:, HEAD : 2 * HEAD]
            out_ref[rows, HEAD * h : HEAD * h + HEAD] = (acc[:, 0:HEAD] / total).astype(BF)
            lse_ref[rows, :] = jnp.where(lane == head, peaks[i] + jnp.log2(total), lse_ref[rows, :])

    pipelined(STEP, scores, finish)


def anchor_kernel(q_ref, k_ref, v_ref, own_ref, lse_ref, out_ref, values_ref, keys_ref):
    fill_values(v_ref, values_ref)

    @pl.when(pl.program_id(0) == 0)
    def _():
        k = k_ref[...].astype(F32) * LOG2_SCALE
        high = k.astype(BF)
        keys_ref[:, 0:HEAD] = high
        keys_ref[:, HEAD : 2 * HEAD] = (k - high.astype(F32)).astype(BF)

    first = jnp.logical_and(
        lax.axis_index("c") == 0,
        jnp.logical_and(lax.axis_index("x") == 0, lax.axis_index("y") == 0),
    )
    lane = lax.broadcasted_iota(jnp.int32, (BLOCK, HEAD), 1)

    def scores(h):
        q = q_ref[:, HEAD * h : HEAD * h + HEAD]
        return lax.dot_general(
            jnp.concatenate([q, q], axis=1), keys_ref[...], (((1,), (1,)), ((), ())), preferred_element_type=F32
        )

    def finish(h, s):
        head = pl.program_id(0) * STEP + h
        lse = jnp.sum(jnp.where(lane == head, lse_ref[...], 0.0), axis=1, keepdims=True)
        peak = jnp.maximum(lse, jnp.max(s, axis=1, keepdims=True))
        p = jnp.exp2(s - peak).astype(BF)
        acc = jnp.dot(p, values_ref[...], preferred_element_type=F32)
        weight = jnp.exp2(lse - peak)
        mixture = acc[:, 0:HEAD] + weight * own_ref[:, HEAD * h : HEAD * h + HEAD].astype(F32)
        out_ref[:, HEAD * h : HEAD * h + HEAD] = (mixture / (acc[:, HEAD : 2 * HEAD] + weight)).astype(BF)

    @pl.when(first)
    def _():
        out_ref[...] = own_ref[...]

    @pl.when(jnp.logical_not(first))
    def _():
        pipelined(STEP, scores, finish)


VMEM = pl.BlockSpec(memory_space=pltpu.VMEM)
HBM = pl.BlockSpec(memory_space=pltpu.HBM)
WIDE = HEADS * HEAD
STEP_BLOCK = pl.BlockSpec((BLOCK, STEP_COLUMNS), lambda t: (0, t))
HEAD_BLOCK = pl.BlockSpec((BLOCK, HEAD), lambda t: (0, 0))


def in_hbm(*arrays):
    return [pltpu.with_memory_space_constraint(a, pltpu.HBM) for a in arrays]


def shape(dims, dtype=BF):
    return jax.ShapeDtypeStruct(dims, dtype)


def buffer(dims, dtype=BF):
    return pltpu.VMEM(dims, dtype)


def run(kernel, name, operands, in_specs, out_shape, out_specs, scratch, flops, nbytes, exps=0, grid=()):
    return pl.pallas_call(
        kernel,
        grid=grid,
        in_specs=in_specs,
        out_specs=out_specs,
        out_shape=out_shape,
        scratch_shapes=scratch,
        compiler_params=pltpu.CompilerParams(vmem_limit_bytes=24 * 1024 * 1024),
        cost_estimate=pl.CostEstimate(flops=flops, bytes_accessed=nbytes, transcendentals=exps),
        name=name,
    )(*operands)


def prep_call(query, k, v):
    return run(
        prep_kernel, "prep", in_hbm(query, k, v), [HBM] * 3,
        (shape((HALF, WIDE)), shape((BLOCK, HEAD)), shape((BLOCK, 2 * HEAD))), (VMEM,) * 3,
        [buffer((BLOCK, HEAD)), pltpu.SemaphoreType.DMA((3,))], 1 << 18, 2 << 20,
    )


def query_call(q, k, values, kp, vp):
    return run(
        query_kernel, "query_attention", (q, k, values, kp, vp), [VMEM] * 5,
        pltpu.HBM((16, SEND1, HEAD), BF), HBM,
        [buffer((BLOCK, 2 * HEAD)), buffer((16, SEND1, HEAD)), pltpu.SemaphoreType.DMA((HEADS,))],
        4 * 2048 * 1536 * 256, 3 << 20, 2048 * 1536,
    )


def own_call(ctx_query, k, v, after):
    return run(
        own_kernel, "context_own", in_hbm(ctx_query, k, v, after),
        [STEP_BLOCK, HEAD_BLOCK, HEAD_BLOCK, HBM],
        (pltpu.HBM((BLOCK, WIDE), BF), pltpu.HBM((BLOCK, HEAD), F32)), (STEP_BLOCK, HEAD_BLOCK),
        [buffer((BLOCK, 2 * HEAD))], 4 * 6144 * 512 * 256, 4 << 20, 6144 * 512, grid=(HEADS // STEP,),
    )


def anchor_call(ctx_query, k, v, own, lse):
    return run(
        anchor_kernel, "context_anchor", in_hbm(ctx_query, k, v, own, lse),
        [STEP_BLOCK, HEAD_BLOCK, HEAD_BLOCK, STEP_BLOCK, HEAD_BLOCK],
        shape((BLOCK, WIDE)), STEP_BLOCK,
        [buffer((BLOCK, 2 * HEAD))] * 2, 4 * 6144 * 768 * 256, 6 << 20, 6144 * 768, grid=(HEADS // STEP,),
    )


def combine_call(received, after):
    return run(
        combine_kernel, "combine", (received, *in_hbm(after)), [VMEM, HBM],
        shape((16, SEND2, HEAD)), VMEM, [], 1 << 20, 3 << 19,
    )


def project_call(mine, other, w):
    return run(
        project_kernel, "project", (mine, other, w), [VMEM] * 3,
        (pltpu.HBM((8, 64, 256), BF), pltpu.HBM((BLOCK, HEAD), BF), pltpu.HBM((BLOCK, HEAD), BF)), (HBM,) * 3,
        [buffer((8, 64, 256)), buffer((BLOCK, HEAD)), buffer((BLOCK, HEAD)), pltpu.SemaphoreType.DMA((6,))],
        2 * 512 * 1024 * 256, 2 << 20,
    )


def final_call(received):
    return run(final_kernel, "final_sum", (received,), [VMEM], shape((64, 256)), VMEM, [], 1 << 17, 1 << 18)


def swap(value):
    return lax.ppermute(value, "c", [(0, 1), (1, 0)])


def exchange(value, axes, order=None):
    return lax.all_to_all(value, axes, 0, 0, axis_index_groups=order, tiled=True)


def per_device(ctx_query, context_key, context_value, query, out_weight):
    key_p, value_p = swap(context_key), swap(context_value)
    q, k, values = prep_call(query, context_key, context_value)
    sent = query_call(q, k, values, key_p, value_p)
    received = exchange(sent, ("x", "y"), PLANE_ORDER)
    own, lse = own_call(ctx_query, context_key, context_value, sent)
    gathered = exchange(combine_call(received, lse), ("x", "y"), PLANE_ORDER)
    shares, key_a, value_a = project_call(gathered, swap(gathered), out_weight)
    ctx_out = anchor_call(ctx_query, key_a, value_a, own, lse)
    answer = final_call(exchange(shares, "z", Z_ORDER))
    return ctx_out, answer


def solution(mesh):
    fine = Mesh(mesh.devices.reshape(4, 4, 2, 8), ("y", "x", "c", "z"))
    hst = ("y", "x", "c")
    in_specs = (P(hst, "z"), P(hst, "z"), P(hst, "z"), P(None, "z"), P("z", hst))
    out_specs = (P(hst, "z"), P("z", hst))
    return jax.shard_map(
        per_device, mesh=fine, in_specs=in_specs, out_specs=out_specs, check_vma=False
    )
```

```python
import functools

import jax
import jax.numpy as jnp
from jax import lax
from jax.experimental import pallas as pl
from jax.experimental.pallas import tpu as pltpu
from jax.sharding import Mesh, PartitionSpec as P

HEAD = 128
BLOCK = 768
HEADS = 8
HALF = 256
STATS = HEAD + 16
ANCHOR_ROWS = 48
SEND1 = STATS + ANCHOR_ROWS
SEND2 = HEAD + ANCHOR_ROWS
HIDDEN = 1e30
Z_ORDER = [[7, 0, 1, 2, 3, 4, 5, 6]]
PLANE_ORDER = [[8, 9, 10, 11, 12, 13, 14, 15, 0, 1, 2, 3, 4, 5, 6, 7]]
ROOT = 8
LOG2_SCALE = 1.4426950408889634 * HEAD ** (-0.5)
BF = jnp.bfloat16
F32 = jnp.float32


def scores_of(q, k):
    return lax.dot_general(q, k, (((1,), (1,)), ((), ())), preferred_element_type=F32) * LOG2_SCALE


def pipelined(count, scores, finish):
    s = scores(0)
    for n in range(count):
        s_next = scores(n + 1) if n + 1 < count else None
        finish(n, s)
        s = s_next


def to_lanes(column):
    r = lax.broadcasted_iota(jnp.int32, (HEAD, HEAD), 0)
    c = lax.broadcasted_iota(jnp.int32, (HEAD, HEAD), 1)
    return jnp.sum(jnp.where(r == c, column, 0.0), axis=0, keepdims=True)


def prep_kernel(q_hbm, k_hbm, v_hbm, q_ref, k_ref, values_ref, v_buf, sems):
    rows = pl.ds(pl.multiple_of(HALF * lax.axis_index("c"), HALF), HALF)
    copies = [
        pltpu.make_async_copy(v_hbm, v_buf, sems.at[0]),
        pltpu.make_async_copy(k_hbm, k_ref, sems.at[1]),
        pltpu.make_async_copy(q_hbm.at[rows, :], q_ref, sems.at[2]),
    ]
    for copy in copies:
        copy.start()
    values_ref[:, HEAD : 2 * HEAD] = jnp.ones((BLOCK, HEAD), BF)
    for copy in copies:
        copy.wait()
    values_ref[:, 0:HEAD] = v_buf[...]


def query_kernel(q_ref, k_ref, values_ref, kp_ref, vp_ref, out_hbm, values_p, out_ref, sems):
    core = lax.axis_index("c")
    values_p[:, 0:HEAD] = vp_ref[...]
    values_p[:, HEAD : 2 * HEAD] = jnp.ones((BLOCK, HEAD), BF)
    row_id = lax.broadcasted_iota(jnp.int32, (16, HEAD), 0)

    def scores(j):
        q = q_ref[:, HEAD * j : HEAD * j + HEAD]
        return scores_of(q, k_ref[...]), scores_of(q, kp_ref[...])

    def finish(j, s):
        peak = jnp.maximum(
            jnp.max(s[0], axis=1, keepdims=True), jnp.max(s[1], axis=1, keepdims=True)
        )
        peak = peak.astype(BF).astype(F32)
        acc = jnp.dot(
            jnp.exp2(s[0] - peak).astype(BF), values_ref[...], preferred_element_type=F32
        ) + jnp.dot(jnp.exp2(s[1] - peak).astype(BF), values_p[...], preferred_element_type=F32)
        total = acc[:, HEAD : HEAD + 1]
        for half in range(2):
            rows = slice(half * HEAD, half * HEAD + HEAD)
            out_ref[2 * j + half, 0:HEAD, :] = acc[rows, 0:HEAD].astype(BF)
            peak_l = to_lanes(peak[rows])
            total_l = to_lanes(total[rows])
            high = total_l.astype(BF).astype(F32)
            stats = jnp.where(row_id == 0, peak_l, 0.0)
            stats = jnp.where(row_id == 1, high, stats)
            stats = jnp.where(row_id == 2, total_l - high, stats)
            out_ref[2 * j + half, HEAD:STATS, :] = stats.astype(BF)
            at = (2 * j + half) * ANCHOR_ROWS
            out_ref[2 * j + half, STATS:SEND1, :] = jnp.where(
                core == 0, k_ref[at : at + ANCHOR_ROWS, :], vp_ref[at : at + ANCHOR_ROWS, :]
            )

    def write(j):
        rows = slice(2 * j, 2 * j + 2)
        return pltpu.make_async_copy(out_ref.at[rows], out_hbm.at[rows], sems.at[j])

    def finish_and_write(j, s):
        finish(j, s)
        write(j).start()

    pipelined(HEADS, scores, finish_and_write)
    for j in range(HEADS):
        write(j).wait()


def combine_kernel(in_ref, after_ref, out_ref):
    stats = in_ref[:, HEAD:STATS, :].astype(F32)
    peak = stats[:, 0, :]
    total = stats[:, 1, :] + stats[:, 2, :]
    top = jnp.max(peak, axis=0, keepdims=True)
    weight = jnp.exp2(peak - top)
    weight = weight / jnp.sum(weight * total, axis=0, keepdims=True)
    weight_t = jnp.concatenate([weight, jnp.zeros((HEAD - 16, HEAD), F32)], axis=0).T
    out = jnp.zeros((HEAD, HEAD), F32)
    for g in range(16):
        out = out + weight_t[:, g : g + 1] * in_ref[g, 0:HEAD, :].astype(F32)
    out = out.astype(BF)
    anchor = in_ref[ROOT, STATS:SEND1, :]
    for g in range(16):
        out_ref[g, 0:HEAD, :] = out
        out_ref[g, HEAD:SEND2, :] = anchor


def project_kernel(mine_ref, other_ref, w_ref, out_hbm, k_hbm, v_hbm, out_ref, k_ref, v_ref, sems):
    core = lax.axis_index("c")
    for g in range(16):
        rows = slice(g * ANCHOR_ROWS, (g + 1) * ANCHOR_ROWS)
        one, two = mine_ref[g, HEAD:SEND2, :], other_ref[g, HEAD:SEND2, :]
        k_ref[rows, :] = jnp.where(core == 0, one, two)
        v_ref[rows, :] = jnp.where(core == 0, two, one)
    copies = [
        pltpu.make_async_copy(k_ref, k_hbm, sems.at[0]),
        pltpu.make_async_copy(v_ref, v_hbm, sems.at[1]),
    ]
    for copy in copies:
        copy.start()
    for ref, owner in ((mine_ref, core), (other_ref, 1 - core)):
        a = jnp.concatenate(
            [
                jnp.concatenate([ref[2 * j + half, 0:HEAD, :] for j in range(HEADS)], axis=1)
                for half in range(2)
            ],
            axis=0,
        )
        y = jnp.dot(a, w_ref[...], preferred_element_type=F32).astype(BF)
        for z in range(4):
            place = lax.rem(4 * owner + z + 1, 8)
            out_ref[place] = y[64 * z : 64 * z + 64, :]
            copies.append(pltpu.make_async_copy(out_ref.at[place], out_hbm.at[place], sems.at[len(copies)]))
            copies[-1].start()
    for copy in copies:
        copy.wait()


def final_kernel(in_ref, out_ref):
    total = in_ref[0].astype(F32)
    for z in range(1, 8):
        total = total + in_ref[z].astype(F32)
    out_ref[...] = total.astype(BF)


STEP = 2
STEP_COLUMNS = STEP * HEAD


def fill_values(v_ref, values_ref):
    @pl.when(pl.program_id(0) == 0)
    def _():
        values_ref[:, 0:HEAD] = v_ref[...]
        values_ref[:, HEAD : 2 * HEAD] = jnp.ones((BLOCK, HEAD), BF)


def own_kernel(q_ref, k_ref, v_ref, after_ref, out_ref, lse_ref, values_ref):
    fill_values(v_ref, values_ref)

    @pl.when(pl.program_id(0) == 0)
    def _():
        lse_ref[...] = jnp.zeros((BLOCK, HEAD), F32)

    lane = lax.broadcasted_iota(jnp.int32, (HALF, HEAD), 1)
    r = lax.broadcasted_iota(jnp.int32, (HALF, HALF), 0)
    c = lax.broadcasted_iota(jnp.int32, (HALF, HALF), 1)

    def scores(h):
        return [
            scores_of(q_ref[i * HALF : (i + 1) * HALF, HEAD * h : HEAD * h + HEAD], k_ref[0 : (i + 1) * HALF, :])
            for i in range(3)
        ]

    def finish(h, s):
        head = pl.program_id(0) * STEP + h
        parts, peaks = [], []
        for i in range(3):
            diagonal = jnp.where(c <= r, s[i][:, i * HALF :], -HIDDEN)
            part = jnp.concatenate([s[i][:, 0 : i * HALF], diagonal], axis=1) if i else diagonal
            parts.append(part)
            peaks.append(jnp.max(part, axis=1, keepdims=True))
        for i in range(3):
            rows = slice(i * HALF, (i + 1) * HALF)
            p = jnp.exp2(parts[i] - peaks[i]).astype(BF)
            acc = jnp.dot(p, values_ref[0 : (i + 1) * HALF, :], preferred_element_type=F32)
            total = acc[:, HEAD : 2 * HEAD]
            out_ref[rows, HEAD * h : HEAD * h + HEAD] = (acc[:, 0:HEAD] / total).astype(BF)
            lse_ref[rows, :] = jnp.where(lane == head, peaks[i] + jnp.log2(total), lse_ref[rows, :])

    pipelined(STEP, scores, finish)


def anchor_kernel(q_ref, k_ref, v_ref, own_ref, lse_ref, out_ref, values_ref, keys_ref):
    fill_values(v_ref, values_ref)

    @pl.when(pl.program_id(0) == 0)
    def _():
        k = k_ref[...].astype(F32) * LOG2_SCALE
        high = k.astype(BF)
        keys_ref[:, 0:HEAD] = high
        keys_ref[:, HEAD : 2 * HEAD] = (k - high.astype(F32)).astype(BF)

    first = jnp.logical_and(
        lax.axis_index("c") == 0,
        jnp.logical_and(lax.axis_index("x") == 0, lax.axis_index("y") == 0),
    )
    lane = lax.broadcasted_iota(jnp.int32, (BLOCK, HEAD), 1)

    def scores(h):
        q = q_ref[:, HEAD * h : HEAD * h + HEAD]
        return lax.dot_general(
            jnp.concatenate([q, q], axis=1), keys_ref[...], (((1,), (1,)), ((), ())), preferred_element_type=F32
        )

    def finish(h, s):
        head = pl.program_id(0) * STEP + h
        lse = jnp.sum(jnp.where(lane == head, lse_ref[...], 0.0), axis=1, keepdims=True)
        peak = jnp.maximum(lse, jnp.max(s, axis=1, keepdims=True))
        p = jnp.exp2(s - peak).astype(BF)
        acc = jnp.dot(p, values_ref[...], preferred_element_type=F32)
        weight = jnp.exp2(lse - peak)
        mixture = acc[:, 0:HEAD] + weight * own_ref[:, HEAD * h : HEAD * h + HEAD].astype(F32)
        out_ref[:, HEAD * h : HEAD * h + HEAD] = (mixture / (acc[:, HEAD : 2 * HEAD] + weight)).astype(BF)

    @pl.when(first)
    def _():
        out_ref[...] = own_ref[...]

    @pl.when(jnp.logical_not(first))
    def _():
        pipelined(STEP, scores, finish)


VMEM = pl.BlockSpec(memory_space=pltpu.VMEM)
HBM = pl.BlockSpec(memory_space=pltpu.HBM)
WIDE = HEADS * HEAD
STEP_BLOCK = pl.BlockSpec((BLOCK, STEP_COLUMNS), lambda t: (0, t))
HEAD_BLOCK = pl.BlockSpec((BLOCK, HEAD), lambda t: (0, 0))


def in_hbm(*arrays):
    return [pltpu.with_memory_space_constraint(a, pltpu.HBM) for a in arrays]


def shape(dims, dtype=BF):
    return jax.ShapeDtypeStruct(dims, dtype)


def buffer(dims, dtype=BF):
    return pltpu.VMEM(dims, dtype)


def run(kernel, name, operands, in_specs, out_shape, out_specs, scratch, flops, nbytes, exps=0, grid=()):
    return pl.pallas_call(
        kernel,
        grid=grid,
        in_specs=in_specs,
        out_specs=out_specs,
        out_shape=out_shape,
        scratch_shapes=scratch,
        compiler_params=pltpu.CompilerParams(vmem_limit_bytes=24 * 1024 * 1024),
        cost_estimate=pl.CostEstimate(flops=flops, bytes_accessed=nbytes, transcendentals=exps),
        name=name,
    )(*operands)


def prep_call(query, k, v):
    return run(
        prep_kernel, "prep", in_hbm(query, k, v), [HBM] * 3,
        (shape((HALF, WIDE)), shape((BLOCK, HEAD)), shape((BLOCK, 2 * HEAD))), (VMEM,) * 3,
        [buffer((BLOCK, HEAD)), pltpu.SemaphoreType.DMA((3,))], 1 << 18, 2 << 20,
    )


def query_call(q, k, values, kp, vp):
    return run(
        query_kernel, "query_attention", (q, k, values, kp, vp), [VMEM] * 5,
        pltpu.HBM((16, SEND1, HEAD), BF), HBM,
        [buffer((BLOCK, 2 * HEAD)), buffer((16, SEND1, HEAD)), pltpu.SemaphoreType.DMA((HEADS,))],
        4 * 2048 * 1536 * 256, 3 << 20, 2048 * 1536,
    )


def own_call(ctx_query, k, v, after):
    return run(
        own_kernel, "context_own", in_hbm(ctx_query, k, v, after),
        [STEP_BLOCK, HEAD_BLOCK, HEAD_BLOCK, HBM],
        (pltpu.HBM((BLOCK, WIDE), BF), pltpu.HBM((BLOCK, HEAD), F32)), (STEP_BLOCK, HEAD_BLOCK),
        [buffer((BLOCK, 2 * HEAD))], 4 * 6144 * 512 * 256, 4 << 20, 6144 * 512, grid=(HEADS // STEP,),
    )


def anchor_call(ctx_query, k, v, own, lse):
    return run(
        anchor_kernel, "context_anchor", in_hbm(ctx_query, k, v, own, lse),
        [STEP_BLOCK, HEAD_BLOCK, HEAD_BLOCK, STEP_BLOCK, HEAD_BLOCK],
        shape((BLOCK, WIDE)), STEP_BLOCK,
        [buffer((BLOCK, 2 * HEAD))] * 2, 4 * 6144 * 768 * 256, 6 << 20, 6144 * 768, grid=(HEADS // STEP,),
    )


def combine_call(received, after):
    return run(
        combine_kernel, "combine", (received, *in_hbm(after)), [VMEM, HBM],
        shape((16, SEND2, HEAD)), VMEM, [], 1 << 20, 3 << 19,
    )


def project_call(mine, other, w):
    return run(
        project_kernel, "project", (mine, other, w), [VMEM] * 3,
        (pltpu.HBM((8, 64, 256), BF), pltpu.HBM((BLOCK, HEAD), BF), pltpu.HBM((BLOCK, HEAD), BF)), (HBM,) * 3,
        [buffer((8, 64, 256)), buffer((BLOCK, HEAD)), buffer((BLOCK, HEAD)), pltpu.SemaphoreType.DMA((10,))],
        2 * 512 * 1024 * 256, 2 << 20,
    )


def final_call(received):
    return run(final_kernel, "final_sum", (received,), [VMEM], shape((64, 256)), VMEM, [], 1 << 17, 1 << 18)


def swap(value):
    return lax.ppermute(value, "c", [(0, 1), (1, 0)])


def exchange(value, axes, order=None):
    return lax.all_to_all(value, axes, 0, 0, axis_index_groups=order, tiled=True)


def per_device(ctx_query, context_key, context_value, query, out_weight):
    key_p, value_p = swap(context_key), swap(context_value)
    q, k, values = prep_call(query, context_key, context_value)
    sent = query_call(q, k, values, key_p, value_p)
    received = exchange(sent, ("x", "y"), PLANE_ORDER)
    own, lse = own_call(ctx_query, context_key, context_value, sent)
    gathered = exchange(combine_call(received, lse), ("x", "y"), PLANE_ORDER)
    shares, key_a, value_a = project_call(gathered, swap(gathered), out_weight)
    ctx_out = anchor_call(ctx_query, key_a, value_a, own, lse)
    answer = final_call(exchange(shares, "z", Z_ORDER))
    return ctx_out, answer


def solution(mesh):
    fine = Mesh(mesh.devices.reshape(4, 4, 2, 8), ("y", "x", "c", "z"))
    hst = ("y", "x", "c")
    in_specs = (P(hst, "z"), P(hst, "z"), P(hst, "z"), P(None, "z"), P("z", hst))
    out_specs = (P(hst, "z"), P("z", hst))
    return jax.shard_map(
        per_device, mesh=fine, in_specs=in_specs, out_specs=out_specs, check_vma=False
    )
```

```python
import functools

import jax
import jax.numpy as jnp
from jax import lax
from jax.experimental import pallas as pl
from jax.experimental.pallas import tpu as pltpu
from jax.sharding import Mesh, PartitionSpec as P

HEAD = 128
BLOCK = 768
HEADS = 8
HALF = 256
STATS = HEAD + 16
ANCHOR_ROWS = 48
SEND1 = STATS + ANCHOR_ROWS
SEND2 = HEAD + ANCHOR_ROWS
HIDDEN = 1e30
Z_ORDER = [[7, 0, 1, 2, 3, 4, 5, 6]]
PLANE_ORDER = [[10, 11, 12, 13, 14, 15, 0, 1, 2, 3, 4, 5, 6, 7, 8, 9]]
ROOT = 6
LOG2_SCALE = 1.4426950408889634 * HEAD ** (-0.5)
BF = jnp.bfloat16
F32 = jnp.float32


def scores_of(q, k):
    return lax.dot_general(q, k, (((1,), (1,)), ((), ())), preferred_element_type=F32) * LOG2_SCALE


def pipelined(count, scores, finish):
    s = scores(0)
    for n in range(count):
        s_next = scores(n + 1) if n + 1 < count else None
        finish(n, s)
        s = s_next


def to_lanes(column):
    r = lax.broadcasted_iota(jnp.int32, (HEAD, HEAD), 0)
    c = lax.broadcasted_iota(jnp.int32, (HEAD, HEAD), 1)
    return jnp.sum(jnp.where(r == c, column, 0.0), axis=0, keepdims=True)


def prep_kernel(q_hbm, k_hbm, v_hbm, q_ref, k_ref, values_ref, v_buf, sems):
    rows = pl.ds(pl.multiple_of(HALF * lax.axis_index("c"), HALF), HALF)
    copies = [
        pltpu.make_async_copy(v_hbm, v_buf, sems.at[0]),
        pltpu.make_async_copy(k_hbm, k_ref, sems.at[1]),
        pltpu.make_async_copy(q_hbm.at[rows, :], q_ref, sems.at[2]),
    ]
    for copy in copies:
        copy.start()
    values_ref[:, HEAD : 2 * HEAD] = jnp.ones((BLOCK, HEAD), BF)
    for copy in copies:
        copy.wait()
    values_ref[:, 0:HEAD] = v_buf[...]


def query_kernel(q_ref, k_ref, values_ref, kp_ref, vp_ref, out_hbm, values_p, out_ref, sems):
    core = lax.axis_index("c")
    values_p[:, 0:HEAD] = vp_ref[...]
    values_p[:, HEAD : 2 * HEAD] = jnp.ones((BLOCK, HEAD), BF)
    row_id = lax.broadcasted_iota(jnp.int32, (16, HEAD), 0)

    def scores(j):
        q = q_ref[:, HEAD * j : HEAD * j + HEAD]
        return scores_of(q, k_ref[...]), scores_of(q, kp_ref[...])

    def finish(j, s):
        peak = jnp.maximum(
            jnp.max(s[0], axis=1, keepdims=True), jnp.max(s[1], axis=1, keepdims=True)
        )
        peak = peak.astype(BF).astype(F32)
        acc = jnp.dot(
            jnp.exp2(s[0] - peak).astype(BF), values_ref[...], preferred_element_type=F32
        ) + jnp.dot(jnp.exp2(s[1] - peak).astype(BF), values_p[...], preferred_element_type=F32)
        total = acc[:, HEAD : HEAD + 1]
        for half in range(2):
            rows = slice(half * HEAD, half * HEAD + HEAD)
            out_ref[2 * j + half, 0:HEAD, :] = acc[rows, 0:HEAD].astype(BF)
            peak_l = to_lanes(peak[rows])
            total_l = to_lanes(total[rows])
            high = total_l.astype(BF).astype(F32)
            stats = jnp.where(row_id == 0, peak_l, 0.0)
            stats = jnp.where(row_id == 1, high, stats)
            stats = jnp.where(row_id == 2, total_l - high, stats)
            out_ref[2 * j + half, HEAD:STATS, :] = stats.astype(BF)
            at = (2 * j + half) * ANCHOR_ROWS
            out_ref[2 * j + half, STATS:SEND1, :] = jnp.where(
                core == 0, k_ref[at : at + ANCHOR_ROWS, :], vp_ref[at : at + ANCHOR_ROWS, :]
            )

    def write(j):
        rows = slice(2 * j, 2 * j + 2)
        return pltpu.make_async_copy(out_ref.at[rows], out_hbm.at[rows], sems.at[j])

    def finish_and_write(j, s):
        finish(j, s)
        write(j).start()

    pipelined(HEADS, scores, finish_and_write)
    for j in range(HEADS):
        write(j).wait()


def combine_kernel(in_ref, after_ref, out_ref):
    stats = in_ref[:, HEAD:STATS, :].astype(F32)
    peak = stats[:, 0, :]
    total = stats[:, 1, :] + stats[:, 2, :]
    top = jnp.max(peak, axis=0, keepdims=True)
    weight = jnp.exp2(peak - top)
    weight = weight / jnp.sum(weight * total, axis=0, keepdims=True)
    weight_t = jnp.concatenate([weight, jnp.zeros((HEAD - 16, HEAD), F32)], axis=0).T
    out = jnp.zeros((HEAD, HEAD), F32)
    for g in range(16):
        out = out + weight_t[:, g : g + 1] * in_ref[g, 0:HEAD, :].astype(F32)
    out = out.astype(BF)
    anchor = in_ref[ROOT, STATS:SEND1, :]
    for g in range(16):
        out_ref[g, 0:HEAD, :] = out
        out_ref[g, HEAD:SEND2, :] = anchor


def project_kernel(mine_ref, other_ref, w_ref, out_hbm, k_hbm, v_hbm, out_ref, k_ref, v_ref, sems):
    core = lax.axis_index("c")
    for g in range(16):
        rows = slice(g * ANCHOR_ROWS, (g + 1) * ANCHOR_ROWS)
        one, two = mine_ref[g, HEAD:SEND2, :], other_ref[g, HEAD:SEND2, :]
        k_ref[rows, :] = jnp.where(core == 0, one, two)
        v_ref[rows, :] = jnp.where(core == 0, two, one)
    copies = [
        pltpu.make_async_copy(k_ref, k_hbm, sems.at[0]),
        pltpu.make_async_copy(v_ref, v_hbm, sems.at[1]),
    ]
    for copy in copies:
        copy.start()
    for ref, owner in ((mine_ref, core), (other_ref, 1 - core)):
        a = jnp.concatenate(
            [
                jnp.concatenate([ref[2 * j + half, 0:HEAD, :] for j in range(HEADS)], axis=1)
                for half in range(2)
            ],
            axis=0,
        )
        y = jnp.dot(a, w_ref[...], preferred_element_type=F32).astype(BF)
        for z in range(4):
            place = lax.rem(4 * owner + z + 1, 8)
            out_ref[place] = y[64 * z : 64 * z + 64, :]
            copies.append(pltpu.make_async_copy(out_ref.at[place], out_hbm.at[place], sems.at[len(copies)]))
            copies[-1].start()
    for copy in copies:
        copy.wait()


def final_kernel(in_ref, out_ref):
    total = in_ref[0].astype(F32)
    for z in range(1, 8):
        total = total + in_ref[z].astype(F32)
    out_ref[...] = total.astype(BF)


STEP = 2
STEP_COLUMNS = STEP * HEAD


def fill_values(v_ref, values_ref):
    @pl.when(pl.program_id(0) == 0)
    def _():
        values_ref[:, 0:HEAD] = v_ref[...]
        values_ref[:, HEAD : 2 * HEAD] = jnp.ones((BLOCK, HEAD), BF)


def own_kernel(q_ref, k_ref, v_ref, after_ref, out_ref, lse_ref, values_ref):
    fill_values(v_ref, values_ref)

    @pl.when(pl.program_id(0) == 0)
    def _():
        lse_ref[...] = jnp.zeros((BLOCK, HEAD), F32)

    lane = lax.broadcasted_iota(jnp.int32, (HALF, HEAD), 1)
    r = lax.broadcasted_iota(jnp.int32, (HALF, HALF), 0)
    c = lax.broadcasted_iota(jnp.int32, (HALF, HALF), 1)

    def scores(h):
        return [
            scores_of(q_ref[i * HALF : (i + 1) * HALF, HEAD * h : HEAD * h + HEAD], k_ref[0 : (i + 1) * HALF, :])
            for i in range(3)
        ]

    def finish(h, s):
        head = pl.program_id(0) * STEP + h
        parts, peaks = [], []
        for i in range(3):
            diagonal = jnp.where(c <= r, s[i][:, i * HALF :], -HIDDEN)
            part = jnp.concatenate([s[i][:, 0 : i * HALF], diagonal], axis=1) if i else diagonal
            parts.append(part)
            peaks.append(jnp.max(part, axis=1, keepdims=True))
        for i in range(3):
            rows = slice(i * HALF, (i + 1) * HALF)
            p = jnp.exp2(parts[i] - peaks[i]).astype(BF)
            acc = jnp.dot(p, values_ref[0 : (i + 1) * HALF, :], preferred_element_type=F32)
            total = acc[:, HEAD : 2 * HEAD]
            out_ref[rows, HEAD * h : HEAD * h + HEAD] = (acc[:, 0:HEAD] / total).astype(BF)
            lse_ref[rows, :] = jnp.where(lane == head, peaks[i] + jnp.log2(total), lse_ref[rows, :])

    pipelined(STEP, scores, finish)


def anchor_kernel(q_ref, k_ref, v_ref, own_ref, lse_ref, out_ref, values_ref, keys_ref):
    fill_values(v_ref, values_ref)

    @pl.when(pl.program_id(0) == 0)
    def _():
        k = k_ref[...].astype(F32) * LOG2_SCALE
        high = k.astype(BF)
        keys_ref[:, 0:HEAD] = high
        keys_ref[:, HEAD : 2 * HEAD] = (k - high.astype(F32)).astype(BF)

    first = jnp.logical_and(
        lax.axis_index("c") == 0,
        jnp.logical_and(lax.axis_index("x") == 0, lax.axis_index("y") == 0),
    )
    lane = lax.broadcasted_iota(jnp.int32, (BLOCK, HEAD), 1)

    def scores(h):
        q = q_ref[:, HEAD * h : HEAD * h + HEAD]
        return lax.dot_general(
            jnp.concatenate([q, q], axis=1), keys_ref[...], (((1,), (1,)), ((), ())), preferred_element_type=F32
        )

    def finish(h, s):
        head = pl.program_id(0) * STEP + h
        lse = jnp.sum(jnp.where(lane == head, lse_ref[...], 0.0), axis=1, keepdims=True)
        peak = jnp.maximum(lse, jnp.max(s, axis=1, keepdims=True))
        p = jnp.exp2(s - peak).astype(BF)
        acc = jnp.dot(p, values_ref[...], preferred_element_type=F32)
        weight = jnp.exp2(lse - peak)
        mixture = acc[:, 0:HEAD] + weight * own_ref[:, HEAD * h : HEAD * h + HEAD].astype(F32)
        out_ref[:, HEAD * h : HEAD * h + HEAD] = (mixture / (acc[:, HEAD : 2 * HEAD] + weight)).astype(BF)

    @pl.when(first)
    def _():
        out_ref[...] = own_ref[...]

    @pl.when(jnp.logical_not(first))
    def _():
        pipelined(STEP, scores, finish)


VMEM = pl.BlockSpec(memory_space=pltpu.VMEM)
HBM = pl.BlockSpec(memory_space=pltpu.HBM)
WIDE = HEADS * HEAD
STEP_BLOCK = pl.BlockSpec((BLOCK, STEP_COLUMNS), lambda t: (0, t))
HEAD_BLOCK = pl.BlockSpec((BLOCK, HEAD), lambda t: (0, 0))


def in_hbm(*arrays):
    return [pltpu.with_memory_space_constraint(a, pltpu.HBM) for a in arrays]


def shape(dims, dtype=BF):
    return jax.ShapeDtypeStruct(dims, dtype)


def buffer(dims, dtype=BF):
    return pltpu.VMEM(dims, dtype)


def run(kernel, name, operands, in_specs, out_shape, out_specs, scratch, flops, nbytes, exps=0, grid=()):
    return pl.pallas_call(
        kernel,
        grid=grid,
        in_specs=in_specs,
        out_specs=out_specs,
        out_shape=out_shape,
        scratch_shapes=scratch,
        compiler_params=pltpu.CompilerParams(vmem_limit_bytes=24 * 1024 * 1024),
        cost_estimate=pl.CostEstimate(flops=flops, bytes_accessed=nbytes, transcendentals=exps),
        name=name,
    )(*operands)


def prep_call(query, k, v):
    return run(
        prep_kernel, "prep", in_hbm(query, k, v), [HBM] * 3,
        (shape((HALF, WIDE)), shape((BLOCK, HEAD)), shape((BLOCK, 2 * HEAD))), (VMEM,) * 3,
        [buffer((BLOCK, HEAD)), pltpu.SemaphoreType.DMA((3,))], 1 << 18, 2 << 20,
    )


def query_call(q, k, values, kp, vp):
    return run(
        query_kernel, "query_attention", (q, k, values, kp, vp), [VMEM] * 5,
        pltpu.HBM((16, SEND1, HEAD), BF), HBM,
        [buffer((BLOCK, 2 * HEAD)), buffer((16, SEND1, HEAD)), pltpu.SemaphoreType.DMA((HEADS,))],
        4 * 2048 * 1536 * 256, 3 << 20, 2048 * 1536,
    )


def own_call(ctx_query, k, v, after):
    return run(
        own_kernel, "context_own", in_hbm(ctx_query, k, v, after),
        [STEP_BLOCK, HEAD_BLOCK, HEAD_BLOCK, HBM],
        (pltpu.HBM((BLOCK, WIDE), BF), pltpu.HBM((BLOCK, HEAD), F32)), (STEP_BLOCK, HEAD_BLOCK),
        [buffer((BLOCK, 2 * HEAD))], 4 * 6144 * 512 * 256, 4 << 20, 6144 * 512, grid=(HEADS // STEP,),
    )


def anchor_call(ctx_query, k, v, own, lse):
    return run(
        anchor_kernel, "context_anchor", in_hbm(ctx_query, k, v, own, lse),
        [STEP_BLOCK, HEAD_BLOCK, HEAD_BLOCK, STEP_BLOCK, HEAD_BLOCK],
        shape((BLOCK, WIDE)), STEP_BLOCK,
        [buffer((BLOCK, 2 * HEAD))] * 2, 4 * 6144 * 768 * 256, 6 << 20, 6144 * 768, grid=(HEADS // STEP,),
    )


def combine_call(received, after):
    return run(
        combine_kernel, "combine", (received, *in_hbm(after)), [VMEM, HBM],
        shape((16, SEND2, HEAD)), VMEM, [], 1 << 20, 3 << 19,
    )


def project_call(mine, other, w):
    return run(
        project_kernel, "project", (mine, other, w), [VMEM] * 3,
        (pltpu.HBM((8, 64, 256), BF), pltpu.HBM((BLOCK, HEAD), BF), pltpu.HBM((BLOCK, HEAD), BF)), (HBM,) * 3,
        [buffer((8, 64, 256)), buffer((BLOCK, HEAD)), buffer((BLOCK, HEAD)), pltpu.SemaphoreType.DMA((10,))],
        2 * 512 * 1024 * 256, 2 << 20,
    )


def final_call(received):
    return run(final_kernel, "final_sum", (received,), [VMEM], shape((64, 256)), VMEM, [], 1 << 17, 1 << 18)


def swap(value):
    return lax.ppermute(value, "c", [(0, 1), (1, 0)])


def exchange(value, axes, order=None):
    return lax.all_to_all(value, axes, 0, 0, axis_index_groups=order, tiled=True)


def per_device(ctx_query, context_key, context_value, query, out_weight):
    key_p, value_p = swap(context_key), swap(context_value)
    q, k, values = prep_call(query, context_key, context_value)
    sent = query_call(q, k, values, key_p, value_p)
    received = exchange(sent, ("x", "y"), PLANE_ORDER)
    own, lse = own_call(ctx_query, context_key, context_value, sent)
    gathered = exchange(combine_call(received, lse), ("x", "y"), PLANE_ORDER)
    shares, key_a, value_a = project_call(gathered, swap(gathered), out_weight)
    ctx_out = anchor_call(ctx_query, key_a, value_a, own, lse)
    answer = final_call(exchange(shares, "z", Z_ORDER))
    return ctx_out, answer


def solution(mesh):
    fine = Mesh(mesh.devices.reshape(4, 4, 2, 8), ("y", "x", "c", "z"))
    hst = ("y", "x", "c")
    in_specs = (P(hst, "z"), P(hst, "z"), P(hst, "z"), P(None, "z"), P("z", hst))
    out_specs = (P(hst, "z"), P("z", hst))
    return jax.shard_map(
        per_device, mesh=fine, in_specs=in_specs, out_specs=out_specs, check_vma=False
    )
```
